512 devices in a mesh: lat: 64 (over z_hi, y, x, core), lon: 8 (over z_lo).
Axes of the slice: x: 4, y: 4, z: 16 (z_hi: 2, z_lo: 8; z = z_hi * 8 + z_lo), core: 2. Of those that a mesh axis runs over, the one named last changes fastest.
Arguments:
- tokens: bfloat16 [384, 384, 512], P('lat', 'lon')
- cotangent: bfloat16 [384, 384, 512], P('lat', 'lon'), may hold values from -6 to 6
- qkv_weight: bfloat16 [512, 1536], P('lat', 'lon')
- band_rows: int32 [64], replicated, may hold values from 4 to 6, as said below
Outputs:
- token_grad: bfloat16 [384, 384, 512], P('lat', 'lon')
- weight_gradient: float32 [512, 1536], P('lat', 'lon')
The draws below stay inside these ranges and needn't reach their ends.
Inputs may be any that keep to these rules, and one draw needn't show every extreme that they name: `band_rows`: some band is full.
All inputs are finite; a program needn't handle non-finite values.
Results may differ from the reference program's by a relative error of at most 0.017.
Values may be sent and summed in bfloat16 or wider, within the bound.
A program may use at most 64 MiB of HBM per device.

```python
import math
import jax
import jax.numpy as jnp
from jax import lax

D = 512
HEADS = 16
HEAD_DIM = 32
WIN_ROWS = 6
WIN_COLS = 12
ROWS_DEV = 6
NLAT = 384
NLON = 384
N_LAT = 64


def draw_tokens(key, part):
    key = jax.random.fold_in(key, 11)
    return jax.random.normal(key, (NLAT, NLON, D), jnp.float32).astype(jnp.bfloat16)


def draw_qkv_weight(key, part):
    key = jax.random.fold_in(key, 5)
    subkeys = jax.random.split(key, 1)
    values_drawn = jax.random.normal(subkeys[0], (D, 3 * D), jnp.float32) / math.sqrt(D)
    return values_drawn.astype(jnp.bfloat16)


def draw_band_rows(key, part):
    key = jax.random.fold_in(key, 3)
    counts = jax.random.randint(key, (N_LAT,), ROWS_DEV - WIN_ROWS // 2 + 1, ROWS_DEV + 1)
    second = jax.random.fold_in(key, 7)
    picked = jax.random.randint(second, (), 0, N_LAT)
    return counts.at[picked].set(ROWS_DEV).astype(jnp.int32)


def steps_of(stream_key, extent, cuts, smallest, top_value):
    def one(dim, shards_of):
        steps = jax.random.uniform(jax.random.fold_in(jax.random.fold_in(stream_key, 6), dim), (shards_of,), jnp.float32, smallest / len(cuts), top_value / len(cuts))
        return jnp.repeat(jnp.exp(steps), extent[dim] // shards_of).reshape((-1,) + (1,) * (len(extent) - dim - 1))

    level = one(*cuts[0])
    for cut in cuts[1:]:
        level = level * one(*cut)
    return level


def scatter_about(key, dims, scale, reach, pieces=(), kind=jnp.bfloat16):
    factor_of = steps_of(key, dims, pieces, -0.22, 0.18) if pieces else 1.0
    values = jax.random.normal(key, dims, jnp.float32) * scale * factor_of
    return jnp.minimum(jnp.maximum(values, -reach), reach).astype(kind)


def setup_inputs(seed: int = 0) -> dict:
    splits = jax.random.split(jax.random.key(seed), 5)
    tokens = draw_tokens(jax.random.fold_in(splits[4], 71), 0)
    cotangent = scatter_about(splits[1], (NLAT, NLON, D), 1.0, 6.0, ((0, 64), (1, 8)))
    qkv_weight = draw_qkv_weight(jax.random.fold_in(splits[4], 71), 0)
    band_rows = draw_band_rows(jax.random.fold_in(splits[4], 71), 0)
    return {"tokens": tokens, "cotangent": cotangent, "qkv_weight": qkv_weight, "band_rows": band_rows}


epsilon = 1e-05

def to_windows(tensor):
    row_count, col_count, feature_count = tensor.shape
    head_width = feature_count // HEADS
    tensor = tensor.reshape(row_count // WIN_ROWS, WIN_ROWS, col_count // WIN_COLS, WIN_COLS, HEADS, head_width)
    tensor = tensor.transpose(0, 2, 4, 1, 3, 5)
    return tensor.reshape(-1, HEADS, WIN_ROWS * WIN_COLS, head_width)

def from_windows(tensor, row_count, col_count):
    head_width = tensor.shape[-1]
    tensor = tensor.reshape(row_count // WIN_ROWS, col_count // WIN_COLS, HEADS, WIN_ROWS, WIN_COLS, head_width)
    tensor = tensor.transpose(0, 3, 1, 4, 2, 5)
    return tensor.reshape(row_count, col_count, HEADS * head_width)

def key_mask(valid_rows, col_count):
    row_count = valid_rows.shape[0]
    spread = jnp.broadcast_to(valid_rows.reshape(row_count // WIN_ROWS, 1, WIN_ROWS, 1), (row_count // WIN_ROWS, col_count // WIN_COLS, WIN_ROWS, WIN_COLS))
    return spread.reshape(-1, WIN_ROWS * WIN_COLS)

def product(form, left, right):
    return jnp.einsum(form, left.astype(jnp.float32), right.astype(jnp.float32))

def normalize(block):
    values = block.astype(jnp.float32)
    center = values - lax.optimization_barrier(jnp.mean(values, axis=-1, keepdims=True))
    inverse = lax.rsqrt(lax.optimization_barrier(jnp.mean(center * center, axis=-1, keepdims=True)) + epsilon)
    return (center * inverse, inverse)

def norm_backward(grad_in, normed, inverse):
    mean_grad = lax.optimization_barrier(jnp.mean(grad_in, axis=-1, keepdims=True))
    mean_mixed = lax.optimization_barrier(jnp.mean(grad_in * normed, axis=-1, keepdims=True))
    return inverse * (grad_in - mean_grad - normed * mean_mixed)

def window_backward(qkv_block, grad_block, valid_rows):
    row_count, col_count, triple = qkv_block.shape
    width = triple // 3
    query = to_windows(qkv_block[..., :width])
    keyed = to_windows(qkv_block[..., width:2 * width])
    valued = to_windows(qkv_block[..., 2 * width:])
    masked_grad = jnp.where(valid_rows[:, None, None], grad_block, jnp.zeros_like(grad_block))
    out_grad = to_windows(masked_grad)
    factor = HEAD_DIM ** (-0.5)
    allowed = key_mask(valid_rows, col_count)
    scores = product('whqd,whkd->whqk', query, keyed) * factor
    scores = jnp.where(allowed[:, None, None, :], scores, -1000000000.0)
    scores = scores - lax.optimization_barrier(jnp.max(scores, axis=-1, keepdims=True))
    exponent = jnp.exp(scores)
    probs = exponent / lax.optimization_barrier(jnp.sum(exponent, axis=-1, keepdims=True))
    probs_low = probs.astype(jnp.bfloat16)
    weight_grad = product('whqd,whkd->whqk', out_grad, valued)
    value_grad = product('whqk,whqd->whkd', probs_low, out_grad)
    score_grad = (probs * (weight_grad - lax.optimization_barrier(jnp.sum(probs * weight_grad, axis=-1, keepdims=True))) * factor).astype(jnp.bfloat16)
    query_grad = product('whqk,whkd->whqd', score_grad, keyed)
    key_grad = product('whqk,whqd->whkd', score_grad, query)
    joined = jnp.concatenate([from_windows(query_grad, row_count, col_count), from_windows(key_grad, row_count, col_count), from_windows(value_grad, row_count, col_count)], axis=-1)
    return joined.astype(jnp.bfloat16)

def reference(tokens, cotangent, qkv_weight, band_rows):
    shift_rows = WIN_ROWS // 2
    shift_cols = WIN_COLS // 2
    grid_rows = jnp.arange(NLAT, dtype=jnp.int32)
    valid_row = grid_rows % ROWS_DEV < band_rows[grid_rows // ROWS_DEV]
    framed_valid = jnp.concatenate([jnp.zeros((shift_rows,), bool), valid_row[:NLAT - shift_rows]])
    padding = jnp.zeros((shift_rows, NLON, D), jnp.bfloat16)
    framed_tokens = jnp.roll(jnp.concatenate([padding, tokens[:NLAT - shift_rows]], axis=0), shift_cols, axis=1)
    framed_cotangent = jnp.roll(jnp.concatenate([padding, cotangent[:NLAT - shift_rows]], axis=0), shift_cols, axis=1)

    def band_step(running, band_index):
        offset = band_index * WIN_ROWS
        token_block = lax.dynamic_slice_in_dim(framed_tokens, offset, WIN_ROWS, 0)
        grad_block = lax.dynamic_slice_in_dim(framed_cotangent, offset, WIN_ROWS, 0)
        valid_block = lax.dynamic_slice_in_dim(framed_valid, offset, WIN_ROWS, 0)
        normed, inverse = normalize(token_block)
        hidden = normed.astype(jnp.bfloat16).reshape(-1, D)
        qkv = jnp.dot(hidden, qkv_weight, preferred_element_type=jnp.float32).astype(jnp.bfloat16)
        qkv_grad = window_backward(qkv.reshape(WIN_ROWS, NLON, 3 * D), grad_block, valid_block).reshape(-1, 3 * D)
        running = running + jnp.dot(hidden.T, qkv_grad, preferred_element_type=jnp.float32)
        hidden_grad = jnp.dot(qkv_grad, qkv_weight.T, preferred_element_type=jnp.float32).reshape(WIN_ROWS, NLON, D)
        frame_grad = norm_backward(hidden_grad, normed, inverse).astype(jnp.bfloat16)
        return (running, frame_grad)
    weight_gradient, frame_grad = lax.scan(band_step, jnp.zeros((D, 3 * D), jnp.float32), jnp.arange(NLAT // WIN_ROWS, dtype=jnp.int32))
    frame_grad = frame_grad.reshape(NLAT, NLON, D)
    returned = jnp.roll(frame_grad, -shift_cols, axis=1)
    returned = jnp.concatenate([returned[shift_rows:], padding], axis=0)
    token_grad = (cotangent.astype(jnp.float32) + returned.astype(jnp.float32)).astype(jnp.bfloat16)
    return (token_grad, weight_gradient)
```

```python
import functools

import jax
import jax.numpy as jnp
import numpy as np
from jax import lax
from jax.experimental import pallas as pl
from jax.experimental.pallas import tpu as pltpu
from jax.sharding import PartitionSpec as P

MESH = pl.DeviceIdType.MESH
VMEM = pltpu.VMEM
BF16 = jnp.bfloat16
F32 = jnp.float32

WIN_ROWS = 6
WIN_COLS = 12
SHIFT_ROWS = 3
SHIFT_COLS = 6
HEAD_DIM = 32
EPSILON = 1e-05

Z_HI, Y, X, CORES = 2, 4, 4, 2


class Place:
    def __init__(self, lats, lons):
        self.lats, self.lons = lats, lons
        self.planes = Y * X
        self.rings = Z_HI * lons
        self.lat = lax.axis_index("lat")
        self.lon = lax.axis_index("lon")
        self.z_hi = self.lat // (self.planes * CORES)
        self.p = (self.lat % (self.planes * CORES)) // CORES
        self.core = self.lat % CORES
        self.z = self.z_hi * lons + self.lon

    def ring_at(self, z):
        return ((z // self.lons) * self.planes * CORES + self.p * CORES + self.core, z % self.lons)

    def plane_at(self, p):
        return (self.z_hi * self.planes * CORES + p * CORES + self.core, self.lon)

    def ring_index(self, k):
        return (self.z + k) % self.rings

    def plane_index(self, k):
        x = (self.p % X + k % X) % X
        y = (self.p // X + k // X) % Y
        return y * X + x

    def partner(self):
        return (self.lat + 1 - 2 * self.core, self.lon)

    def east(self):
        return (self.lon + 1) % self.lons

    def west(self):
        return (self.lon + self.lons - 1) % self.lons


def remote(src, dst, send, recv, device):
    return pltpu.make_async_remote_copy(
        src_ref=src, dst_ref=dst, send_sem=send, recv_sem=recv, device_id=device, device_id_type=MESH
    )


def enter(place):
    barrier = pltpu.get_barrier_semaphore()

    def signal(device):
        pl.semaphore_signal(barrier, inc=1, device_id=device, device_id_type=MESH)

    @pl.loop(1, place.rings)
    def _(k):
        signal(place.ring_at(place.ring_index(k)))

    @pl.loop(1, place.planes)
    def _(k):
        signal(place.plane_at(place.plane_index(k)))

    signal(place.partner())
    signal((place.lat, place.east()))
    signal((place.lat, place.west()))
    not_first = place.lat > 0
    not_last = place.lat < place.lats - 1

    @pl.when(not_first)
    def _():
        signal((place.lat - 1, place.lon))
        signal((place.lat - 1, place.west()))

    @pl.when(not_last)
    def _():
        signal((place.lat + 1, place.lon))
        signal((place.lat + 1, place.east()))

    count = place.rings + place.planes + 1
    count = count + jnp.where(not_first, 2, 0) + jnp.where(not_last, 2, 0)
    pl.semaphore_wait(barrier, count)


def gather_kernel(
    lats, lons, tok, cot, w, sel, w_out, row_tok, row_cot, side,
    wide, unit, units, blocks, packed, ring_send, ring_recv, plane_send, plane_recv,
    core_send, core_recv, halo_send, halo_recv,
):
    place = Place(lats, lons)
    half = tok.shape[0] // 2
    features = tok.shape[1]
    columns = w_out.shape[1]
    lane = lax.broadcasted_iota(jnp.int32, (8, 128), 1)

    for part in range(2):
        rows = pl.ds(part * half, half)
        packed[part] = (
            jnp.dot(sel[0], tok[rows], preferred_element_type=F32)
            + jnp.dot(sel[1], cot[rows], preferred_element_type=F32)
        ).astype(BF16)
    wide[...] = jnp.zeros_like(wide)
    wide[:, 0 : w.shape[1]] = w[...].astype(F32)
    unit[...] = jnp.concatenate([wide[:, 0:128], wide[:, 128:256]], axis=0).astype(BF16)

    enter(place)

    def ring_copy(k):
        return remote(
            unit, units.at[place.z], ring_send.at[k], ring_recv.at[place.z],
            place.ring_at(place.ring_index(k)),
        )

    def ring_arrival(k):
        z = place.ring_index(k)
        return remote(unit, units.at[z], ring_send.at[k], ring_recv.at[z], place.ring_at(z))

    @pl.loop(1, place.rings)
    def _(k):
        ring_copy(k).start()

    not_first = place.lat > 0
    not_last = place.lat < lats - 1
    south = (place.lat + 1, place.lon)
    side_copy = remote(packed.at[0], side.at[0], halo_send.at[0], halo_recv.at[0], (place.lat, place.east()))
    diag_copy = remote(
        packed.at[1], side.at[1], halo_send.at[1], halo_recv.at[1], (place.lat + 1, place.east())
    )
    tok_copy = remote(tok.at[pl.ds(half, half)], row_tok, halo_send.at[2], halo_recv.at[2], south)
    cot_copy = remote(cot.at[pl.ds(half, half)], row_cot, halo_send.at[3], halo_recv.at[3], south)
    side_copy.start()

    @pl.when(not_last)
    def _():
        diag_copy.start()
        tok_copy.start()
        cot_copy.start()

    @pl.when(jnp.logical_not(not_first))
    def _():
        side[1] = jnp.zeros(side.shape[1:], BF16)
        row_tok[...] = jnp.zeros_like(row_tok)
        row_cot[...] = jnp.zeros_like(row_cot)

    units[place.z] = unit[...]

    @pl.loop(1, place.rings)
    def _(k):
        ring_arrival(k).wait_recv()

    own = blocks.at[place.core, place.p]
    for pair in range(lons // 2):
        tiles = [[], [], []]
        for z_hi in range(Z_HI):
            even = units[z_hi * lons + 2 * pair].astype(F32)
            odd = units[z_hi * lons + 2 * pair + 1].astype(F32)
            turned_top = pltpu.roll(odd[0:8], 64, 1)
            turned_low = pltpu.roll(odd[8:16], 64, 1)
            tiles[0].append(even[0:8])
            tiles[1].append(jnp.where(lane < 64, even[8:16], turned_top))
            tiles[2].append(jnp.where(lane < 64, turned_top, turned_low))
        for j in range(3):
            own[:, pl.ds(pair * 384 + j * 128, 128)] = jnp.concatenate(tiles[j], axis=0).astype(BF16)

    def plane_copy(k):
        return remote(
            own, own, plane_send.at[k], plane_recv.at[place.p], place.plane_at(place.plane_index(k))
        )

    def plane_arrival(k):
        p = place.plane_index(k)
        block = blocks.at[place.core, p]
        return remote(block, block, plane_send.at[k], plane_recv.at[p], place.plane_at(p))

    def core_copy(p):
        block = blocks.at[place.core, p]
        return remote(block, block, core_send.at[p], core_recv.at[p], place.partner())

    def core_arrival(p):
        block = blocks.at[1 - place.core, p]
        return remote(block, block, core_send.at[p], core_recv.at[p], place.partner())

    @pl.loop(1, place.planes)
    def _(k):
        plane_copy(k).start()

    core_copy(place.p).start()

    @pl.loop(1, place.planes)
    def _(k):
        plane_arrival(k).wait_recv()
        core_copy(place.plane_index(k)).start()

    rows = place.planes * 16

    @pl.loop(0, place.planes)
    def _(k):
        p = place.plane_index(k)
        core_arrival(p).wait_recv()
        first = blocks[0, p].astype(F32)
        second = blocks[1, p].astype(F32)
        for z_hi in range(Z_HI):
            take = slice(z_hi * 8, z_hi * 8 + 8)
            at = pl.multiple_of(z_hi * rows + p * 16, 16)
            w_out[pl.ds(at, 16), :] = jnp.concatenate([first[take], second[take]], axis=0).astype(BF16)

    @pl.when(not_first)
    def _():
        diag_copy.wait_recv()
        tok_copy.wait_recv()
        cot_copy.wait_recv()

    side_copy.wait_recv()
    side_copy.wait_send()

    @pl.when(not_last)
    def _():
        diag_copy.wait_send()
        tok_copy.wait_send()
        cot_copy.wait_send()

    @pl.loop(1, place.rings)
    def _(k):
        ring_copy(k).wait_send()

    @pl.loop(1, place.planes)
    def _(k):
        plane_copy(k).wait_send()

    @pl.loop(0, place.planes)
    def _(k):
        core_copy(k).wait_send()


def gather(tok, cot, w, lats, lons):
    tokens, features = tok.shape
    half = tokens // 2
    cols = half // SHIFT_ROWS
    planes, rings = Y * X, Z_HI * lons
    columns = w.shape[1] * lons
    sel = np.zeros((2, 48, half), np.float32)
    for r in range(SHIFT_ROWS):
        for c in range(SHIFT_COLS):
            sel[0, r * SHIFT_COLS + c, r * cols + cols - SHIFT_COLS + c] = 1
            sel[1, 18 + r * SHIFT_COLS + c, r * cols + cols - SHIFT_COLS + c] = 1
    return pl.pallas_call(
        functools.partial(gather_kernel, lats, lons),
        out_shape=(
            jax.ShapeDtypeStruct((8 * lats, columns), BF16),
            jax.ShapeDtypeStruct((half, features), BF16),
            jax.ShapeDtypeStruct((half, features), BF16),
            jax.ShapeDtypeStruct((2, 48, features), BF16),
        ),
        in_specs=[pl.BlockSpec(memory_space=VMEM)] * 4,
        out_specs=[pl.BlockSpec(memory_space=VMEM)] * 4,
        scratch_shapes=[
            VMEM((8, 256), F32),
            VMEM((16, 128), BF16),
            VMEM((rings, 16, 128), BF16),
            VMEM((CORES, planes, 16, columns), BF16),
            VMEM((2, 48, features), BF16),
            pltpu.SemaphoreType.DMA((rings,)),
            pltpu.SemaphoreType.DMA((rings,)),
            pltpu.SemaphoreType.DMA((planes,)),
            pltpu.SemaphoreType.DMA((planes,)),
            pltpu.SemaphoreType.DMA((planes,)),
            pltpu.SemaphoreType.DMA((planes,)),
            pltpu.SemaphoreType.DMA((4,)),
            pltpu.SemaphoreType.DMA((4,)),
        ],
        compiler_params=pltpu.CompilerParams(
            collective_id=0, has_side_effects=True, vmem_limit_bytes=32 * 2**20
        ),
        name="gather",
    )(tok, cot, w, jnp.asarray(sel, BF16))


def sum_kernel(
    lats, lons, part, back, cot, place_sel, token_grad, weight_grad,
    from_core, sums, from_plane, total, units, from_ring, row_back, side_back,
    core_send, core_recv, plane_send, plane_recv, ring_send, ring_recv, halo_send, halo_recv,
):
    place = Place(lats, lons)
    half = cot.shape[0] // 2
    lane = lax.broadcasted_iota(jnp.int32, (8, 128), 1)
    enter(place)

    def core_copy(p):
        return remote(
            part.at[1 - place.core, p], from_core.at[p], core_send.at[p], core_recv.at[p], place.partner()
        )

    def plane_copy(k):
        p = place.plane_index(k)
        return remote(
            sums.at[p], from_plane.at[place.p], plane_send.at[p], plane_recv.at[place.p], place.plane_at(p)
        )

    def plane_arrival(k):
        p = place.plane_index(k)
        return remote(sums.at[p], from_plane.at[p], plane_send.at[p], plane_recv.at[p], place.plane_at(p))

    def ring_copy(k):
        z = place.ring_index(k)
        return remote(
            units.at[z], from_ring.at[place.z], ring_send.at[z], ring_recv.at[place.z], place.ring_at(z)
        )

    def ring_arrival(k):
        z = place.ring_index(k)
        return remote(units.at[z], from_ring.at[z], ring_send.at[z], ring_recv.at[z], place.ring_at(z))

    @pl.loop(0, place.planes)
    def _(k):
        core_copy(place.plane_index(k + 1)).start()

    not_first = place.lat > 0
    not_last = place.lat < lats - 1
    side_copy = remote(
        back.at[pl.ds(2 * half, 32)], side_back.at[0], halo_send.at[0], halo_recv.at[0],
        (place.lat, place.west()),
    )
    diag_copy = remote(
        back.at[pl.ds(2 * half + 32, 32)], side_back.at[1], halo_send.at[1], halo_recv.at[1],
        (place.lat - 1, place.west()),
    )
    row_copy = remote(
        back.at[pl.ds(half, half)], row_back, halo_send.at[2], halo_recv.at[2], (place.lat - 1, place.lon)
    )

    @pl.when(not_first)
    def _():
        row_copy.start()
        diag_copy.start()

    side_copy.start()

    @pl.when(jnp.logical_not(not_last))
    def _():
        row_back[...] = jnp.zeros_like(row_back)
        side_back[1] = jnp.zeros(side_back.shape[1:], BF16)

    @pl.loop(0, place.planes)
    def _(k):
        p = place.plane_index(k + 1)
        core_copy(p).wait_recv()
        sums[p] = (part[place.core, p].astype(F32) + from_core[p].astype(F32)).astype(BF16)

        @pl.when(k < place.planes - 1)
        def _():
            plane_copy(k + 1).start()

    total[...] = sums[place.p].astype(F32)

    @pl.loop(1, place.planes)
    def _(k):
        plane_arrival(k).wait_recv()
        total[...] += from_plane[place.plane_index(k)].astype(F32)

    for pair in range(lons // 2):
        for z_hi in range(Z_HI):
            tiles = [
                total[pl.ds(z_hi * 8, 8), pl.ds(pair * 384 + j * 128, 128)] for j in range(3)
            ]
            turned = [pltpu.roll(tile, 64, 1) for tile in tiles]
            units[z_hi * lons + 2 * pair] = jnp.concatenate([tiles[0], tiles[1]], axis=0).astype(BF16)
            units[z_hi * lons + 2 * pair + 1] = jnp.concatenate(
                [jnp.where(lane < 64, turned[1], turned[2]), turned[2]], axis=0
            ).astype(BF16)

    @pl.loop(1, place.rings)
    def _(k):
        ring_copy(k).start()

    @pl.when(not_last)
    def _():
        row_copy.wait_recv()
        diag_copy.wait_recv()

    side_copy.wait_recv()
    for part_of in range(2):
        rows = pl.ds(part_of * half, half)
        inner = back[0:half] if part_of == 0 else row_back[...]
        outer = jnp.dot(place_sel[...], side_back[part_of], preferred_element_type=F32)
        token_grad[rows] = (cot[rows].astype(F32) + (inner.astype(F32) + outer)).astype(BF16)

    result = units[place.z].astype(F32)
    from_ring[place.z] = units[place.z]

    @pl.loop(1, place.rings)
    def _(k):
        ring_arrival(k).wait_recv()

    result = from_ring[0].astype(F32)
    for z in range(1, place.rings):
        result = result + from_ring[z].astype(F32)
    weight_grad[:, 0:128] = result[0:8]
    weight_grad[:, 128:192] = result[8:16, 0:64]

    @pl.when(not_first)
    def _():
        row_copy.wait_send()
        diag_copy.wait_send()

    side_copy.wait_send()

    @pl.loop(0, place.planes)
    def _(k):
        core_copy(place.plane_index(k + 1)).wait_send()

    @pl.loop(1, place.planes)
    def _(k):
        plane_copy(k).wait_send()

    @pl.loop(1, place.rings)
    def _(k):
        ring_copy(k).wait_send()


def sum_and_return(part, back, cot, lats, lons):
    tokens, features = cot.shape
    half = tokens // 2
    cols = half // SHIFT_ROWS
    planes, rings = Y * X, Z_HI * lons
    columns = part.shape[-1]
    place_sel = np.zeros((half, 32), np.float32)
    for r in range(SHIFT_ROWS):
        for c in range(SHIFT_COLS):
            place_sel[r * cols + cols - SHIFT_COLS + c, r * SHIFT_COLS + c] = 1
    return pl.pallas_call(
        functools.partial(sum_kernel, lats, lons),
        out_shape=(
            jax.ShapeDtypeStruct((tokens, features), BF16),
            jax.ShapeDtypeStruct((8, columns // lons), F32),
        ),
        in_specs=[pl.BlockSpec(memory_space=VMEM)] * 4,
        out_specs=[pl.BlockSpec(memory_space=VMEM)] * 2,
        scratch_shapes=[
            VMEM((planes, 16, columns), BF16),
            VMEM((planes, 16, columns), BF16),
            VMEM((planes, 16, columns), BF16),
            VMEM((16, columns), F32),
            VMEM((rings, 16, 128), BF16),
            VMEM((rings, 16, 128), BF16),
            VMEM((half, features), BF16),
            VMEM((2, 32, features), BF16),
            pltpu.SemaphoreType.DMA((planes,)),
            pltpu.SemaphoreType.DMA((planes,)),
            pltpu.SemaphoreType.DMA((planes,)),
            pltpu.SemaphoreType.DMA((planes,)),
            pltpu.SemaphoreType.DMA((rings,)),
            pltpu.SemaphoreType.DMA((rings,)),
            pltpu.SemaphoreType.DMA((3,)),
            pltpu.SemaphoreType.DMA((3,)),
        ],
        compiler_params=pltpu.CompilerParams(
            collective_id=1, has_side_effects=True, vmem_limit_bytes=32 * 2**20
        ),
        name="sum_and_return",
    )(part, back, cot, jnp.asarray(place_sel, BF16))


PAD = 80
GROUP = 8


def contract(left, right, dims):
    return lax.dot_general(left, right, (dims, ((), ())), preferred_element_type=F32)


def compute_kernel(
    counts, tok, cot, row_tok, row_cot, side, w, take_own, take_row, take_side, row_of, head_mask,
    give, part, back, hidden, normed, spread, out_grad, qkv, qkv_grad,
):
    windows = tok.shape[0] // (WIN_ROWS * WIN_COLS)
    features = tok.shape[1]
    width = GROUP * HEAD_DIM
    lat = lax.axis_index("lat")
    own_count = counts[lat]
    previous = jnp.where(lat > 0, counts[jnp.maximum(lat - 1, 0)], 0)
    rows = row_of[...]
    limit = jnp.where(rows < SHIFT_ROWS, previous - SHIFT_ROWS, own_count + SHIFT_ROWS)
    valid = jnp.where(rows < jnp.minimum(limit, WIN_ROWS), 1.0, 0.0)

    framed = (
        jnp.dot(take_own[...], tok[...], preferred_element_type=F32)
        + jnp.dot(take_row[...], row_tok[...], preferred_element_type=F32)
        + jnp.dot(take_side[0], side[0], preferred_element_type=F32)
        + jnp.dot(take_side[1], side[1], preferred_element_type=F32)
    )
    center = framed - jnp.mean(framed, axis=-1, keepdims=True)
    inverse = lax.rsqrt(jnp.mean(center * center, axis=-1, keepdims=True) + EPSILON)
    normal = center * inverse
    normed[...] = normal
    spread[...] = jnp.broadcast_to(inverse, spread.shape)
    hidden[...] = normal.astype(BF16)
    framed = (
        jnp.dot(take_own[...], cot[...], preferred_element_type=F32)
        + jnp.dot(take_row[...], row_cot[...], preferred_element_type=F32)
        + jnp.dot(take_side[2], side[0], preferred_element_type=F32)
        + jnp.dot(take_side[3], side[1], preferred_element_type=F32)
    )
    for j in range(features // 128):
        lanes = slice(j * 128, j * 128 + 128)
        out_grad[:, lanes] = jnp.where(valid > 0.0, framed[:, lanes], 0.0).astype(BF16)

    for j in range(3):
        lanes = slice(j * features, (j + 1) * features)
        qkv[:, lanes] = jnp.dot(hidden[...], w[:, lanes], preferred_element_type=F32).astype(BF16)

    factor = HEAD_DIM ** (-0.5)
    allowed = jnp.concatenate([valid[0:PAD]] * (GROUP * PAD // 128), axis=1) > 0.0
    mask = head_mask[...]

    for window in range(windows):
        at = slice(window * PAD, window * PAD + PAD)
        for group in range(features // width):
            lanes = [slice(j * features + group * width, j * features + (group + 1) * width) for j in range(3)]
            query, keyed, valued = (qkv[at, lane] for lane in lanes)
            grad = out_grad[at, lanes[0]]
            query = jnp.concatenate([query] * GROUP, axis=0) * mask
            grad = jnp.concatenate([grad] * GROUP, axis=0) * mask
            scores = contract(keyed, query, ((1,), (1,))) * factor
            scores = jnp.where(allowed, scores, -1000000000.0)
            exponent = jnp.exp(scores - jnp.max(scores, axis=0, keepdims=True))
            probs = exponent * (1.0 / jnp.sum(exponent, axis=0, keepdims=True))
            weight = contract(valued, grad, ((1,), (1,)))
            mixed = jnp.sum(probs * weight, axis=0, keepdims=True)
            score_grad = (probs * (weight - mixed) * factor).astype(BF16)
            value_grad = jnp.dot(probs.astype(BF16), grad, preferred_element_type=F32)
            key_grad = jnp.dot(score_grad, query, preferred_element_type=F32)
            turned = contract(score_grad, keyed, ((0,), (0,)))
            query_grad = turned[0:PAD] * mask[0:PAD].astype(F32)
            for h in range(1, GROUP):
                rows_h = slice(h * PAD, h * PAD + PAD)
                query_grad = query_grad + turned[rows_h] * mask[rows_h].astype(F32)
            for lane, value in zip(lanes, (query_grad, key_grad, value_grad)):
                qkv_grad[at, lane] = value.astype(BF16)

    turned_hidden = hidden[...].T
    planes = part.shape[1]
    for j in range(3 * features // width):
        lanes = slice(j * width, (j + 1) * width)
        piece = jnp.dot(turned_hidden, qkv_grad[:, lanes], preferred_element_type=F32)
        for core in range(CORES):
            for p in range(planes):
                first = (p * CORES + core) * 8
                both = [piece[z * planes * CORES * 8 + first :][0:8] for z in range(Z_HI)]
                part[core, p, :, lanes] = jnp.concatenate(both, axis=0).astype(BF16)

    hidden_grad = contract(qkv_grad[...], w[...], ((1,), (1,)))
    normal = normed[...]
    mean_grad = jnp.mean(hidden_grad, axis=-1, keepdims=True)
    mean_mixed = jnp.mean(hidden_grad * normal, axis=-1, keepdims=True)
    frame_grad = spread[...] * (hidden_grad - mean_grad - normal * mean_mixed)
    back[...] = jnp.dot(give[...], frame_grad.astype(BF16), preferred_element_type=F32).astype(BF16)


def frame_tables(cols):
    windows = cols // WIN_COLS
    total = windows * PAD
    half = SHIFT_ROWS * cols
    own = np.zeros((total, 2 * half), np.float32)
    row = np.zeros((total, half), np.float32)
    side = np.zeros((4, total, 48), np.float32)
    give = np.zeros((2 * half + 64, total), np.float32)
    row_of = np.full((total, 128), WIN_ROWS, np.int32)
    for window in range(windows):
        for r in range(WIN_ROWS):
            for c in range(WIN_COLS):
                t = window * PAD + r * WIN_COLS + c
                row_of[t] = r
                rr, g = r - SHIFT_ROWS, window * WIN_COLS + c - SHIFT_COLS
                upper = rr < 0
                if g >= 0:
                    if upper:
                        row[t, r * cols + g] = 1
                        give[half + r * cols + g, t] = 1
                    else:
                        own[t, rr * cols + g] = 1
                        give[rr * cols + g, t] = 1
                else:
                    at = (r % SHIFT_ROWS) * SHIFT_COLS + g + SHIFT_COLS
                    side[int(upper), t, at] = 1
                    side[2 + int(upper), t, 18 + at] = 1
                    give[2 * half + 32 * int(upper) + at, t] = 1
    return own, row, side, give, row_of


def compute(counts, tok, cot, row_tok, row_cot, side, w):
    tokens, features = tok.shape
    cols = tokens // (2 * SHIFT_ROWS)
    take_own, take_row, take_side, give, row_of = frame_tables(cols)
    total = take_own.shape[0]
    width = GROUP * HEAD_DIM
    head_mask = np.zeros((GROUP, PAD, GROUP, HEAD_DIM), np.float32)
    for h in range(GROUP):
        head_mask[h, :, h] = 1
    operands = (
        tok, cot, row_tok, row_cot, side, w,
        jnp.asarray(take_own, BF16), jnp.asarray(take_row, BF16), jnp.asarray(take_side, BF16),
        jnp.asarray(row_of), jnp.asarray(head_mask.reshape(GROUP * PAD, width), BF16),
        jnp.asarray(give, BF16),
    )
    columns = w.shape[1]
    planes = w.shape[0] // (8 * CORES * Z_HI)
    return pl.pallas_call(
        compute_kernel,
        out_shape=(
            jax.ShapeDtypeStruct((CORES, planes, 8 * Z_HI, columns), BF16),
            jax.ShapeDtypeStruct((give.shape[0], features), BF16),
        ),
        in_specs=[pl.BlockSpec(memory_space=pltpu.SMEM)] + [pl.BlockSpec(memory_space=VMEM)] * len(operands),
        out_specs=[pl.BlockSpec(memory_space=VMEM)] * 2,
        scratch_shapes=[
            VMEM((total, features), BF16),
            VMEM((total, features), F32),
            VMEM((total, features), F32),
            VMEM((total, features), BF16),
            VMEM((total, columns), BF16),
            VMEM((total, columns), BF16),
        ],
        compiler_params=pltpu.CompilerParams(vmem_limit_bytes=40 * 2**20),
        name="windows",
    )(counts, *operands)


def on_device(lats, lons, tokens, cotangent, qkv_weight, band_rows):
    tok = tokens.reshape(-1, tokens.shape[-1])
    cot = cotangent.reshape(-1, tokens.shape[-1])
    w, row_tok, row_cot, side = gather(tok, cot, qkv_weight, lats, lons)
    part, back = compute(band_rows, tok, cot, row_tok, row_cot, side, w)
    token_grad, weight_gradient = sum_and_return(part, back, cot, lats, lons)
    return token_grad.reshape(tokens.shape), weight_gradient


def solution(mesh):
    return jax.shard_map(
        functools.partial(on_device, mesh.shape["lat"], mesh.shape["lon"]),
        mesh=mesh,
        in_specs=(P("lat", "lon", None), P("lat", "lon", None), P("lat", "lon"), P()),
        out_specs=(P("lat", "lon", None), P("lat", "lon")),
        check_vma=False,
    )
```

```python
import functools

import jax
import jax.numpy as jnp
import numpy as np
from jax import lax
from jax.experimental import pallas as pl
from jax.experimental.pallas import tpu as pltpu
from jax.sharding import PartitionSpec as P

MESH = pl.DeviceIdType.MESH
VMEM = pltpu.VMEM
BF16 = jnp.bfloat16
F32 = jnp.float32

WIN_ROWS = 6
WIN_COLS = 12
SHIFT_ROWS = 3
SHIFT_COLS = 6
HEAD_DIM = 32
EPSILON = 1e-05

Z_HI, Y, X, CORES = 2, 4, 4, 2


class Place:
    def __init__(self, lats, lons):
        self.lats, self.lons = lats, lons
        self.planes = Y * X
        self.rings = Z_HI * lons
        self.lat = lax.axis_index("lat")
        self.lon = lax.axis_index("lon")
        self.z_hi = self.lat // (self.planes * CORES)
        self.p = (self.lat % (self.planes * CORES)) // CORES
        self.core = self.lat % CORES
        self.z = self.z_hi * lons + self.lon

    def ring_at(self, z):
        return ((z // self.lons) * self.planes * CORES + self.p * CORES + self.core, z % self.lons)

    def plane_at(self, p):
        return (self.z_hi * self.planes * CORES + p * CORES + self.core, self.lon)

    def ring_index(self, k):
        return (self.z + k) % self.rings

    def plane_index(self, k):
        x = (self.p % X + k % X) % X
        y = (self.p // X + k // X) % Y
        return y * X + x

    def partner(self):
        return (self.lat + 1 - 2 * self.core, self.lon)

    def east(self):
        return (self.lon + 1) % self.lons

    def west(self):
        return (self.lon + self.lons - 1) % self.lons


def remote(src, dst, send, recv, device):
    return pltpu.make_async_remote_copy(
        src_ref=src, dst_ref=dst, send_sem=send, recv_sem=recv, device_id=device, device_id_type=MESH
    )


OUT_COLUMNS = ((X - 1, Y - 1), (0, Y - 1), (X - 1, 0), (0, 0), (X - 2, Y - 1), (0, 1))
BACK_COLUMNS = ((0, 0), (X - 1, 0), (0, Y - 1))
PIECE = 48

PAD = 80
GROUP = 8
HALVES = 2


class Relays:
    def __init__(self, place):
        self.last_low = place.planes * CORES - 1
        self.first_high = place.planes * CORES
        self.low_end = place.lat == self.last_low
        self.high_end = place.lat == self.first_high
        self.out = [(y * X + x) * CORES + CORES - 1 for x, y in OUT_COLUMNS]
        self.back = [self.first_high + (y * X + x) * CORES for x, y in BACK_COLUMNS]


def enter(place, relays):
    barrier = pltpu.get_barrier_semaphore()

    def signal(device):
        pl.semaphore_signal(barrier, inc=1, device_id=device, device_id_type=MESH)

    half = place.rings // 2

    @pl.loop(0, half)
    def _(k):
        signal(place.ring_at(place.ring_index(half - k)))

        @pl.when(k < half - 1)
        def _():
            signal(place.ring_at(place.ring_index(half + 1 + k)))

    @pl.loop(1, place.planes)
    def _(k):
        signal(place.plane_at(place.plane_index(k)))

    signal(place.partner())
    signal((place.lat, place.east()))
    signal((place.lat, place.west()))
    not_first = place.lat > 0
    not_last = place.lat < place.lats - 1

    @pl.when(not_first)
    def _():
        signal((place.lat - 1, place.lon))
        signal((place.lat - 1, place.west()))

    @pl.when(not_last)
    def _():
        signal((place.lat + 1, place.lon))
        signal((place.lat + 1, place.east()))

    count = place.rings + place.planes + 1
    count = count + jnp.where(not_first, 2, 0) + jnp.where(not_last, 2, 0)
    for ends, relay_of, far_end in (
        (relays.high_end, relays.out, relays.first_high),
        (relays.low_end, relays.back, relays.last_low),
    ):
        for lat in relay_of[1:]:
            @pl.when(ends)
            def _():
                signal((lat, place.lon))

            @pl.when(place.lat == lat)
            def _():
                signal((far_end, place.lon))

            count = count + jnp.where(place.lat == lat, 1, 0)
        count = count + jnp.where(ends, len(relay_of) - 1, 0)
    pl.semaphore_wait(barrier, count)


def contract(left, right, dims):
    return lax.dot_general(left, right, (dims, ((), ())), preferred_element_type=F32)


def kernel(
    lats, lons, names, *refs
):
    r = dict(zip(names, refs))
    place = Place(lats, lons)
    relays = Relays(place)
    tok, cot = r["tok"], r["cot"]
    half_rows = tok.shape[0] // 2
    features = tok.shape[1]
    width = GROUP * HEAD_DIM
    planes, rings = place.planes, place.rings
    lane_of = lax.broadcasted_iota(jnp.int32, (8, 128), 1)
    not_first = place.lat > 0
    not_last = place.lat < lats - 1
    either_end = jnp.logical_or(relays.low_end, relays.high_end)

    loads = [
        pltpu.make_async_copy(r["hbm_" + name], r[name], r["load_sem"].at[i])
        for i, name in enumerate(LOADED)
    ]
    for load in loads:
        load.start()

    wide, unit, units = r["wide"], r["unit"], r["units"]
    wide[...] = jnp.zeros_like(wide)
    wide[:, 0 : r["w_in"].shape[1]] = r["w_in"][...].astype(F32)
    unit[...] = jnp.concatenate([wide[:, 0:128], wide[:, 128:256]], axis=0).astype(BF16)
    units[place.z] = unit[...]
    for load in loads:
        load.wait()

    packed, side, sel = r["packed"], r["side"], r["sel"]
    for part_of in range(2):
        rows = pl.ds(part_of * half_rows, half_rows)
        packed[part_of] = (
            jnp.dot(sel[0], tok[rows], preferred_element_type=F32)
            + jnp.dot(sel[1], cot[rows], preferred_element_type=F32)
        ).astype(BF16)

    @pl.when(jnp.logical_not(not_first))
    def _():
        side[1] = jnp.zeros(side.shape[1:], BF16)
        r["row_tok"][...] = jnp.zeros_like(r["row_tok"])
        r["row_cot"][...] = jnp.zeros_like(r["row_cot"])

    @pl.when(jnp.logical_not(not_last))
    def _():
        r["row_back"][...] = jnp.zeros_like(r["row_back"])
        r["side_back"][1] = jnp.zeros(r["side_back"].shape[1:], BF16)

    enter(place, relays)

    def ring_copy(k):
        return remote(
            unit, units.at[place.z], r["ring_send"].at[k], r["ring_recv"].at[place.z],
            place.ring_at(place.ring_index(k)),
        )

    def ring_arrival(k):
        z = place.ring_index(k)
        return remote(unit, units.at[z], r["ring_send"].at[k], r["ring_recv"].at[z], place.ring_at(z))

    @pl.loop(1, rings)
    def _(k):
        ring_copy(k).start()

    halo_send, halo_recv = r["halo_send"], r["halo_recv"]
    side_copy = remote(packed.at[0], side.at[0], halo_send.at[0], halo_recv.at[0], (place.lat, place.east()))
    diag_copy = remote(
        packed.at[1], side.at[1], halo_send.at[1], halo_recv.at[1], (place.lat + 1, place.east())
    )

    def out_piece(i):
        rows = pl.ds((i % 3) * PIECE, PIECE)
        source = (tok if i < 3 else cot).at[pl.ds(half_rows + (i % 3) * PIECE, PIECE)]
        return source, (r["row_tok"] if i < 3 else r["row_cot"]).at[rows]

    def back_piece(i):
        source = r["back"].at[pl.ds(half_rows + i * PIECE, PIECE)]
        return source, r["row_back"].at[pl.ds(i * PIECE, PIECE)]

    class Crossing:
        def __init__(self, piece, relay_of, end, target, far_end, send, recv, sends, receives, relay, relay_sem):
            self.count = len(relay_of)
            self.relay_of, self.end, self.sends, self.receives = relay_of, end, sends, receives
            self.direct, self.via, self.onward = [], [], []
            for i in range(self.count):
                source, landing = piece(i)
                self.direct.append(remote(source, landing, send.at[i], recv.at[i], (target, place.lon)))
                self.via.append(
                    remote(source, relay, send.at[i], relay_sem.at[0], (relay_of[i], place.lon))
                )
                self.onward.append(remote(relay, landing, relay_sem.at[1], recv.at[i], (far_end, place.lon)))

        def start(self):
            plain = jnp.logical_and(self.sends, jnp.logical_not(self.end))

            @pl.when(self.end)
            def _():
                for i in range(1, self.count):
                    self.via[i].start()
                self.direct[0].start()

            @pl.when(plain)
            def _():
                for i in range(self.count):
                    self.direct[i].start()

        def pass_on(self):
            for i in range(1, self.count):
                @pl.when(place.lat == self.relay_of[i])
                def _():
                    self.via[i].wait_recv()
                    self.onward[i].start()

        def wait_recv(self):
            @pl.when(self.receives)
            def _():
                for i in range(self.count):
                    self.direct[i].wait_recv()

        def wait_send(self):
            @pl.when(self.sends)
            def _():
                for i in range(self.count):
                    self.direct[i].wait_send()

            for i in range(1, self.count):
                @pl.when(place.lat == self.relay_of[i])
                def _():
                    self.onward[i].wait_send()

    rows_out = Crossing(
        out_piece, relays.out, relays.low_end, place.lat + 1, relays.first_high,
        r["out_send"], r["out_recv"], not_last, not_first, r["relay"], r["relay_sem"],
    )
    rows_back = Crossing(
        back_piece, relays.back, relays.high_end, place.lat - 1, relays.last_low,
        r["back_send"], r["back_recv"], not_first, not_last, r["relay_back"], r["relay_back_sem"],
    )
    rows_out.start()
    side_copy.start()

    @pl.when(not_last)
    def _():
        diag_copy.start()

    @pl.loop(1, rings)
    def _(k):
        ring_arrival(k).wait_recv()

    blocks = r["blocks"]

    def tile_at(n):
        which, within = divmod(n, features // 128)
        half, at = divmod(within, width // 128)
        return half, pl.ds(which * width + at * 128, 128)

    for pair in range(lons // 2):
        tiles = [[], [], []]
        for z_hi in range(Z_HI):
            even = units[z_hi * lons + 2 * pair].astype(F32)
            odd = units[z_hi * lons + 2 * pair + 1].astype(F32)
            turned_top = pltpu.roll(odd[0:8], 64, 1)
            turned_low = pltpu.roll(odd[8:16], 64, 1)
            tiles[0].append(even[0:8])
            tiles[1].append(jnp.where(lane_of < 64, even[8:16], turned_top))
            tiles[2].append(jnp.where(lane_of < 64, turned_top, turned_low))
        for j in range(3):
            half, lanes = tile_at(pair * 3 + j)
            blocks[half, place.core, place.p, :, lanes] = jnp.concatenate(tiles[j], axis=0).astype(BF16)

    def plane_copy(half, k):
        own = blocks.at[half, place.core, place.p]
        return remote(
            own, own, r["plane_send"].at[half, k], r["plane_recv"].at[half, place.p],
            place.plane_at(place.plane_index(k)),
        )

    def plane_arrival(half, k):
        p = place.plane_index(k)
        block = blocks.at[half, place.core, p]
        return remote(block, block, r["plane_send"].at[half, k], r["plane_recv"].at[half, p], place.plane_at(p))

    def core_copy(half, p):
        block = blocks.at[half, place.core, p]
        return remote(block, block, r["core_send"].at[half, p], r["core_recv"].at[half, p], place.partner())

    def core_arrival(half, p):
        block = blocks.at[half, 1 - place.core, p]
        return remote(block, block, r["core_send"].at[half, p], r["core_recv"].at[half, p], place.partner())

    for half in range(HALVES):
        @pl.loop(1, planes)
        def _(k):
            plane_copy(half, k).start()

        core_copy(half, place.p).start()

    rows_out.pass_on()

    rows_out.wait_recv()
    side_copy.wait_recv()

    @pl.when(not_first)
    def _():
        diag_copy.wait_recv()

    own_count = r["counts"][place.lat]
    previous = jnp.where(not_first, r["counts"][jnp.maximum(place.lat - 1, 0)], 0)
    row_of = r["row_of"][...]
    limit = jnp.where(row_of < SHIFT_ROWS, previous - SHIFT_ROWS, own_count + SHIFT_ROWS)
    valid = jnp.where(row_of < jnp.minimum(limit, WIN_ROWS), 1.0, 0.0)
    take_own, take_row, take_side = r["take_own"], r["take_row"], r["take_side"]

    def framed_of(own, row, first):
        return (
            jnp.dot(take_own[...], own[...], preferred_element_type=F32)
            + jnp.dot(take_row[...], row[...], preferred_element_type=F32)
            + jnp.dot(take_side[first], side[0], preferred_element_type=F32)
            + jnp.dot(take_side[first + 1], side[1], preferred_element_type=F32)
        )

    hidden, normed, spread, out_grad = r["hidden"], r["normed"], r["spread"], r["out_grad"]
    framed = framed_of(tok, r["row_tok"], 0)
    center = framed - jnp.mean(framed, axis=-1, keepdims=True)
    inverse = lax.rsqrt(jnp.mean(center * center, axis=-1, keepdims=True) + EPSILON)
    normal = center * inverse
    normed[...] = normal
    spread[...] = jnp.broadcast_to(inverse, spread.shape)
    hidden[...] = normal.astype(BF16)
    r["turned_hidden"][...] = normal.astype(BF16).T
    framed = framed_of(cot, r["row_cot"], 2)
    for j in range(features // 128):
        lanes = slice(j * 128, j * 128 + 128)
        out_grad[:, lanes] = jnp.where(valid > 0.0, framed[:, lanes], 0.0).astype(BF16)

    weight, qkv, qkv_grad = r["weight"], r["qkv"], r["qkv_grad"]

    def forward_arrivals(half):
        @pl.loop(1, planes)
        def _(k):
            plane_arrival(half, k).wait_recv()
            core_copy(half, place.plane_index(k)).start()

    def collect(half):
        @pl.loop(0, planes)
        def _(k):
            p = place.plane_index(k)
            core_arrival(half, p).wait_recv()
            first = blocks[half, 0, p].astype(F32)
            second = blocks[half, 1, p].astype(F32)
            for z_hi in range(Z_HI):
                take = slice(z_hi * 8, z_hi * 8 + 8)
                at = pl.multiple_of((z_hi * planes + p) * 16, 16)
                weight[half, pl.ds(at, 16), :] = jnp.concatenate([first[take], second[take]], axis=0).astype(BF16)

    factor = HEAD_DIM ** (-0.5)
    allowed = jnp.concatenate([valid[0:PAD]] * (GROUP * PAD // 128), axis=1) > 0.0
    mask = r["head_mask"][...]
    windows = hidden.shape[0] // PAD

    def project(half):
        qkv[half] = jnp.dot(hidden[...], weight[half], preferred_element_type=F32).astype(BF16)

    def attend(half):
        for window in range(windows):
            at = slice(window * PAD, window * PAD + PAD)
            lanes = [slice(j * width, (j + 1) * width) for j in range(3)]
            query, keyed, valued = (qkv[half, at, lane] for lane in lanes)
            grad = out_grad[at, half * width : (half + 1) * width]
            query = jnp.concatenate([query] * GROUP, axis=0) * mask
            grad = jnp.concatenate([grad] * GROUP, axis=0) * mask
            scores = contract(keyed, query, ((1,), (1,))) * factor
            scores = jnp.where(allowed, scores, -1000000000.0)
            exponent = jnp.exp(scores - jnp.max(scores, axis=0, keepdims=True))
            probs = exponent * (1.0 / jnp.sum(exponent, axis=0, keepdims=True))
            weight_grad = contract(valued, grad, ((1,), (1,)))
            mixed = jnp.sum(probs * weight_grad, axis=0, keepdims=True)
            score_grad = (probs * (weight_grad - mixed) * factor).astype(BF16)
            value_grad = jnp.dot(probs.astype(BF16), grad, preferred_element_type=F32)
            key_grad = jnp.dot(score_grad, query, preferred_element_type=F32)
            turned = contract(score_grad, keyed, ((0,), (0,)))
            query_grad = turned[0:PAD] * mask[0:PAD].astype(F32)
            for h in range(1, GROUP):
                rows_h = slice(h * PAD, h * PAD + PAD)
                query_grad = query_grad + turned[rows_h] * mask[rows_h].astype(F32)
            for lane, value in zip(lanes, (query_grad, key_grad, value_grad)):
                qkv_grad[half, at, lane] = value.astype(BF16)

    part = r["part"]

    def weigh(half):
        for j in range(3):
            lanes = slice(j * width, (j + 1) * width)
            piece = jnp.dot(r["turned_hidden"][...], qkv_grad[half, :, lanes], preferred_element_type=F32)
            for core in range(CORES):
                for p in range(planes):
                    first = (p * CORES + core) * 8
                    both = [piece[z * planes * CORES * 8 + first :][0:8] for z in range(Z_HI)]
                    part[half, core, p, :, lanes] = jnp.concatenate(both, axis=0).astype(BF16)

    from_core, sums, from_plane, total = r["from_core"], r["sums"], r["from_plane"], r["total"]

    def core_part(half, p):
        return remote(
            part.at[half, 1 - place.core, p], from_core.at[half, p],
            r["core_part_send"].at[half, p], r["core_part_recv"].at[half, p], place.partner(),
        )

    def plane_part(half, k):
        p = place.plane_index(k)
        return remote(
            sums.at[half, p], from_plane.at[half, place.p],
            r["plane_part_send"].at[half, p], r["plane_part_recv"].at[half, place.p], place.plane_at(p),
        )

    def plane_part_arrival(half, k):
        p = place.plane_index(k)
        return remote(
            sums.at[half, p], from_plane.at[half, p],
            r["plane_part_send"].at[half, p], r["plane_part_recv"].at[half, p], place.plane_at(p),
        )

    def send_core(half):
        @pl.loop(0, planes)
        def _(k):
            core_part(half, place.plane_index(k + 1)).start()

    def send_plane(half):
        @pl.loop(0, planes)
        def _(k):
            p = place.plane_index(k + 1)
            core_part(half, p).wait_recv()
            sums[half, p] = (part[half, place.core, p].astype(F32) + from_core[half, p].astype(F32)).astype(BF16)

            @pl.when(k < planes - 1)
            def _():
                plane_part(half, k + 1).start()

    def add_plane(half):
        total[half] = sums[half, place.p].astype(F32)

        @pl.loop(1, planes)
        def _(k):
            plane_part_arrival(half, k).wait_recv()
            total[half] += from_plane[half, place.plane_index(k)].astype(F32)

    forward_arrivals(0)
    collect(0)
    project(0)
    attend(0)
    weigh(0)
    send_core(0)
    forward_arrivals(1)
    collect(1)
    project(1)
    send_plane(0)
    attend(1)
    weigh(1)
    send_core(1)

    back, side_back = r["back"], r["side_back"]
    hidden_grad = contract(qkv_grad[0], weight[0], ((1,), (1,))) + contract(qkv_grad[1], weight[1], ((1,), (1,)))
    normal = normed[...]
    mean_grad = jnp.mean(hidden_grad, axis=-1, keepdims=True)
    mean_mixed = jnp.mean(hidden_grad * normal, axis=-1, keepdims=True)
    frame_grad = spread[...] * (hidden_grad - mean_grad - normal * mean_mixed)
    back[...] = jnp.dot(r["give"][...], frame_grad.astype(BF16), preferred_element_type=F32).astype(BF16)
    side_return = remote(
        back.at[pl.ds(2 * half_rows, 32)], side_back.at[0], halo_send.at[2], halo_recv.at[2],
        (place.lat, place.west()),
    )
    diag_return = remote(
        back.at[pl.ds(2 * half_rows + 32, 32)], side_back.at[1], halo_send.at[3], halo_recv.at[3],
        (place.lat - 1, place.west()),
    )
    rows_back.start()
    side_return.start()

    @pl.when(not_first)
    def _():
        diag_return.start()

    send_plane(1)
    rows_back.pass_on()
    add_plane(0)
    add_plane(1)

    part_units, from_ring = r["part_units"], r["from_ring"]

    def ring_part(k):
        z = place.ring_index(k)
        return remote(
            part_units.at[z], from_ring.at[place.z], r["ring_part_send"].at[z],
            r["ring_part_recv"].at[place.z], place.ring_at(z),
        )

    def ring_part_arrival(k):
        z = place.ring_index(k)
        return remote(
            part_units.at[z], from_ring.at[z], r["ring_part_send"].at[z], r["ring_part_recv"].at[z],
            place.ring_at(z),
        )

    for pair in range(lons // 2):
        for z_hi in range(Z_HI):
            tiles = []
            for j in range(3):
                half, lanes = tile_at(pair * 3 + j)
                tiles.append(total[half, pl.ds(z_hi * 8, 8), lanes])
            turned = [pltpu.roll(tile, 64, 1) for tile in tiles]
            part_units[z_hi * lons + 2 * pair] = jnp.concatenate([tiles[0], tiles[1]], axis=0).astype(BF16)
            part_units[z_hi * lons + 2 * pair + 1] = jnp.concatenate(
                [jnp.where(lane_of < 64, turned[1], turned[2]), turned[2]], axis=0
            ).astype(BF16)

    @pl.loop(1, rings)
    def _(k):
        ring_part(k).start()

    from_ring[place.z] = part_units[place.z]

    rows_back.wait_recv()
    side_return.wait_recv()

    @pl.when(not_last)
    def _():
        diag_return.wait_recv()

    for part_of in range(2):
        rows = pl.ds(part_of * half_rows, half_rows)
        inner = back[0:half_rows] if part_of == 0 else r["row_back"][...]
        outer = jnp.dot(r["place_sel"][...], side_back[part_of], preferred_element_type=F32)
        r["token_grad"][rows] = (cot[rows].astype(F32) + (inner.astype(F32) + outer)).astype(BF16)

    @pl.loop(1, rings)
    def _(k):
        ring_part_arrival(k).wait_recv()

    result = from_ring[0].astype(F32)
    for z in range(1, rings):
        result = result + from_ring[z].astype(F32)
    r["weight_gradient"][:, 0:128] = result[0:8]
    r["weight_gradient"][:, 128:192] = result[8:16, 0:64]

    rows_out.wait_send()
    rows_back.wait_send()
    side_copy.wait_send()
    side_return.wait_send()

    @pl.when(not_last)
    def _():
        diag_copy.wait_send()

    @pl.when(not_first)
    def _():
        diag_return.wait_send()

    @pl.loop(1, rings)
    def _(k):
        ring_copy(k).wait_send()
        ring_part(k).wait_send()

    for half in range(HALVES):
        @pl.loop(1, planes)
        def _(k):
            plane_copy(half, k).wait_send()
            plane_part(half, k).wait_send()

        @pl.loop(0, planes)
        def _(k):
            core_copy(half, k).wait_send()
            core_part(half, k).wait_send()


LOADED = ("tok", "cot", "sel", "row_of", "take_own", "take_row", "take_side", "head_mask", "give", "place_sel")


def frame_tables(cols):
    windows = cols // WIN_COLS
    total = windows * PAD
    half = SHIFT_ROWS * cols
    own = np.zeros((total, 2 * half), np.float32)
    row = np.zeros((total, half), np.float32)
    side = np.zeros((4, total, 48), np.float32)
    give = np.zeros((2 * half + 64, total), np.float32)
    row_of = np.full((total, 128), WIN_ROWS, np.int32)
    for window in range(windows):
        for r in range(WIN_ROWS):
            for c in range(WIN_COLS):
                t = window * PAD + r * WIN_COLS + c
                row_of[t] = r
                rr, g = r - SHIFT_ROWS, window * WIN_COLS + c - SHIFT_COLS
                upper = rr < 0
                if g >= 0:
                    if upper:
                        row[t, r * cols + g] = 1
                        give[half + r * cols + g, t] = 1
                    else:
                        own[t, rr * cols + g] = 1
                        give[rr * cols + g, t] = 1
                else:
                    at = (r % SHIFT_ROWS) * SHIFT_COLS + g + SHIFT_COLS
                    side[int(upper), t, at] = 1
                    side[2 + int(upper), t, 18 + at] = 1
                    give[2 * half + 32 * int(upper) + at, t] = 1
    return own, row, side, give, row_of


def on_device(lats, lons, tokens, cotangent, qkv_weight, band_rows):
    features = tokens.shape[-1]
    tok = tokens.reshape(-1, features)
    cot = cotangent.reshape(-1, features)
    count = tok.shape[0]
    half = count // 2
    cols = half // SHIFT_ROWS
    planes, rings = Y * X, Z_HI * lons
    columns = qkv_weight.shape[1] * lons
    width = GROUP * HEAD_DIM
    take_own, take_row, take_side, give, row_of = frame_tables(cols)
    total = take_own.shape[0]
    sel = np.zeros((2, 48, half), np.float32)
    place_sel = np.zeros((half, 32), np.float32)
    for row in range(SHIFT_ROWS):
        for col in range(SHIFT_COLS):
            at, edge = row * SHIFT_COLS + col, row * cols + cols - SHIFT_COLS + col
            sel[0, at, edge] = 1
            sel[1, 18 + at, edge] = 1
            place_sel[edge, at] = 1
    head_mask = np.zeros((GROUP, PAD, GROUP, HEAD_DIM), np.float32)
    for h in range(GROUP):
        head_mask[h, :, h] = 1
    low = lambda table: jnp.asarray(table, BF16)
    loaded = {
        "tok": tok, "cot": cot, "sel": low(sel), "row_of": jnp.asarray(row_of), "take_own": low(take_own),
        "take_row": low(take_row), "take_side": low(take_side),
        "head_mask": low(head_mask.reshape(GROUP * PAD, width)), "give": low(give), "place_sel": low(place_sel),
    }
    dma = pltpu.SemaphoreType.DMA
    scratch = {name: VMEM(loaded[name].shape, loaded[name].dtype) for name in LOADED}
    scratch.update(
        wide=VMEM((8, 256), F32),
        unit=VMEM((16, 128), BF16),
        units=VMEM((rings, 16, 128), BF16),
        blocks=VMEM((HALVES, CORES, planes, 16, columns // HALVES), BF16),
        packed=VMEM((2, 48, features), BF16),
        side=VMEM((2, 48, features), BF16),
        row_tok=VMEM((half, features), BF16),
        row_cot=VMEM((half, features), BF16),
        relay=VMEM((PIECE, features), BF16),
        relay_back=VMEM((PIECE, features), BF16),
        weight=VMEM((HALVES, features, columns // HALVES), BF16),
        hidden=VMEM((total, features), BF16),
        turned_hidden=VMEM((features, total), BF16),
        normed=VMEM((total, features), F32),
        spread=VMEM((total, features), F32),
        out_grad=VMEM((total, features), BF16),
        qkv=VMEM((HALVES, total, columns // HALVES), BF16),
        qkv_grad=VMEM((HALVES, total, columns // HALVES), BF16),
        part=VMEM((HALVES, CORES, planes, 16, columns // HALVES), BF16),
        from_core=VMEM((HALVES, planes, 16, columns // HALVES), BF16),
        sums=VMEM((HALVES, planes, 16, columns // HALVES), BF16),
        from_plane=VMEM((HALVES, planes, 16, columns // HALVES), BF16),
        total=VMEM((HALVES, 16, columns // HALVES), F32),
        back=VMEM(give.shape[:1] + (features,), BF16),
        row_back=VMEM((half, features), BF16),
        side_back=VMEM((2, 32, features), BF16),
        part_units=VMEM((rings, 16, 128), BF16),
        from_ring=VMEM((rings, 16, 128), BF16),
        load_sem=dma((len(LOADED),)),
        relay_sem=dma((2,)),
        relay_back_sem=dma((2,)),
    )
    for name, shape in (
        ("ring", (rings,)), ("plane", (HALVES, planes)), ("core", (HALVES, planes)), ("halo", (4,)),
        ("out", (len(OUT_COLUMNS),)), ("back", (len(BACK_COLUMNS),)), ("core_part", (HALVES, planes)),
        ("plane_part", (HALVES, planes)), ("ring_part", (rings,)),
    ):
        scratch[name + "_send"] = dma(shape)
        scratch[name + "_recv"] = dma(shape)
    names = ["counts", "w_in"] + ["hbm_" + name for name in LOADED] + ["token_grad", "weight_gradient"]
    token_grad, weight_gradient = pl.pallas_call(
        functools.partial(kernel, lats, lons, names + list(scratch)),
        out_shape=(
            jax.ShapeDtypeStruct(tok.shape, BF16),
            jax.ShapeDtypeStruct(qkv_weight.shape, F32),
        ),
        in_specs=[pl.BlockSpec(memory_space=pltpu.SMEM), pl.BlockSpec(memory_space=VMEM)]
        + [pl.BlockSpec(memory_space=pl.ANY)] * len(LOADED),
        out_specs=[pl.BlockSpec(memory_space=VMEM)] * 2,
        scratch_shapes=list(scratch.values()),
        compiler_params=pltpu.CompilerParams(
            collective_id=0, has_side_effects=True, vmem_limit_bytes=56 * 2**20
        ),
        name="sub_block",
    )(band_rows, qkv_weight, *(loaded[name] for name in LOADED))
    return token_grad.reshape(tokens.shape), weight_gradient


def solution(mesh):
    return jax.shard_map(
        functools.partial(on_device, mesh.shape["lat"], mesh.shape["lon"]),
        mesh=mesh,
        in_specs=(P("lat", "lon", None), P("lat", "lon", None), P("lat", "lon"), P()),
        out_specs=(P("lat", "lon", None), P("lat", "lon")),
        check_vma=False,
    )
```

```python
import functools
import types

import jax
import jax.numpy as jnp
import numpy as np
from jax import lax
from jax.experimental import pallas as pl
from jax.experimental.pallas import tpu as pltpu
from jax.sharding import PartitionSpec as P

MESH = pl.DeviceIdType.MESH
VMEM = pltpu.VMEM
BF16 = jnp.bfloat16
F32 = jnp.float32

WIN_ROWS = 6
WIN_COLS = 12
SHIFT_ROWS = 3
SHIFT_COLS = 6
HEAD_DIM = 32
EPSILON = 1e-05

Z_HI, Y, X, CORES = 2, 4, 4, 2


class Place:
    def __init__(self, lats, lons):
        self.lats, self.lons = lats, lons
        self.planes = Y * X
        self.rings = Z_HI * lons
        self.lat = lax.axis_index("lat")
        self.lon = lax.axis_index("lon")
        self.z_hi = lax.div(self.lat, self.planes * CORES)
        self.p = lax.div(lax.rem(self.lat, self.planes * CORES), CORES)
        self.core = lax.rem(self.lat, CORES)
        self.z = self.z_hi * lons + self.lon

    def ring_at(self, z):
        return (lax.div(z, self.lons) * self.planes * CORES + self.p * CORES + self.core, lax.rem(z, self.lons))

    def plane_at(self, p):
        return (self.z_hi * self.planes * CORES + p * CORES + self.core, self.lon)

    def ring_index(self, k):
        return lax.rem(self.z + k, self.rings)

    def plane_index(self, k):
        x = lax.rem(lax.rem(self.p, X) + lax.rem(k, X), X)
        y = lax.rem(lax.div(self.p, X) + lax.div(k, X), Y)
        return y * X + x

    def partner(self):
        return (self.lat + 1 - 2 * self.core, self.lon)

    def east(self):
        return lax.rem(self.lon + 1, self.lons)

    def west(self):
        return lax.rem(self.lon + self.lons - 1, self.lons)


def remote(src, dst, send, recv, device):
    return pltpu.make_async_remote_copy(
        src_ref=src, dst_ref=dst, send_sem=send, recv_sem=recv, device_id=device, device_id_type=MESH
    )


OUT_COLUMNS = ((X - 1, Y - 1), (0, Y - 1), (X - 1, 0), (0, 0), (X - 2, Y - 1), (0, 1))
BACK_COLUMNS = ((0, 0), (X - 1, 0), (0, Y - 1))
PIECE = 48

PAD = 80
GROUP = 8
HALVES = 2


class Relays:
    def __init__(self, place):
        self.last_low = place.planes * CORES - 1
        self.first_high = place.planes * CORES
        self.low_end = place.lat == self.last_low
        self.high_end = place.lat == self.first_high
        self.out = [(y * X + x) * CORES + CORES - 1 for x, y in OUT_COLUMNS]
        self.back = [self.first_high + (y * X + x) * CORES for x, y in BACK_COLUMNS]


def far_first(k, count):
    half = count // 2
    return half + (1 - 2 * lax.rem(k, 2)) * lax.div(k + 1, 2)


def announce(place, relays):
    barrier = pltpu.get_barrier_semaphore()

    def signal(device):
        pl.semaphore_signal(barrier, inc=1, device_id=device, device_id_type=MESH)

    @pl.loop(0, place.rings - 1)
    def _(k):
        signal(place.ring_at(place.ring_index(far_first(k, place.rings))))

    @pl.loop(1, place.planes)
    def _(k):
        signal(place.plane_at(place.plane_index(k)))

    signal(place.partner())
    signal((place.lat, place.east()))
    signal((place.lat, place.west()))
    not_first = place.lat > 0
    not_last = place.lat < place.lats - 1

    @pl.when(not_first)
    def _():
        signal((place.lat - 1, place.lon))
        signal((place.lat - 1, place.west()))

    @pl.when(not_last)
    def _():
        signal((place.lat + 1, place.lon))
        signal((place.lat + 1, place.east()))

    count = place.rings + place.planes + 1
    count = count + jnp.where(not_first, 2, 0) + jnp.where(not_last, 2, 0)
    for ends, relay_of, far_end in (
        (relays.high_end, relays.out, relays.first_high),
        (relays.low_end, relays.back, relays.last_low),
    ):
        for lat in relay_of[1:]:
            @pl.when(ends)
            def _():
                signal((lat, place.lon))

            @pl.when(place.lat == lat)
            def _():
                signal((far_end, place.lon))

            count = count + jnp.where(place.lat == lat, 1, 0)
        count = count + jnp.where(ends, len(relay_of) - 1, 0)
    return count


def contract(left, right, dims):
    return lax.dot_general(left, right, (dims, ((), ())), preferred_element_type=F32)


def kernel(lats, lons, loaded, names, counts, w_in, *refs):
    sources, token_grad, weight_gradient = refs[:loaded], refs[loaded], refs[loaded + 1]
    refs = refs[loaded + 2 :]
    targets = refs[:loaded]
    r = types.SimpleNamespace(**dict(zip(names, refs)))
    place = Place(lats, lons)
    relays = Relays(place)
    tok, cot = r.tok, r.cot
    half_rows = tok.shape[0] // 2
    features = tok.shape[1]
    width = GROUP * HEAD_DIM
    planes, rings = place.planes, place.rings
    lane_of = lax.broadcasted_iota(jnp.int32, (8, 128), 1)
    not_first = place.lat > 0
    not_last = place.lat < lats - 1
    either_end = jnp.logical_or(relays.low_end, relays.high_end)

    loads = [
        pltpu.make_async_copy(source, target, r.load_sem.at[i])
        for i, (source, target) in enumerate(zip(sources, targets))
    ]
    for load in loads:
        load.start()

    expected = announce(place, relays)

    wide, unit, units = r.wide, r.unit, r.units
    wide[...] = jnp.zeros_like(wide)
    wide[:, 0 : w_in.shape[1]] = w_in[...].astype(F32)
    unit[...] = jnp.concatenate([wide[:, 0:128], wide[:, 128:256]], axis=0).astype(BF16)
    units[place.z] = unit[...]
    for load in loads:
        load.wait()

    packed, side, sel = r.packed, r.side, r.sel
    for part_of in range(2):
        rows = pl.ds(part_of * half_rows, half_rows)
        packed[part_of] = (
            jnp.dot(sel[0], tok[rows], preferred_element_type=F32)
            + jnp.dot(sel[1], cot[rows], preferred_element_type=F32)
        ).astype(BF16)

    @pl.when(jnp.logical_not(not_first))
    def _():
        side[1] = jnp.zeros(side.shape[1:], BF16)
        r.row_tok[...] = jnp.zeros_like(r.row_tok)
        r.row_cot[...] = jnp.zeros_like(r.row_cot)

    @pl.when(jnp.logical_not(not_last))
    def _():
        r.row_back[...] = jnp.zeros_like(r.row_back)
        r.side_back[1] = jnp.zeros(r.side_back.shape[1:], BF16)

    pl.semaphore_wait(pltpu.get_barrier_semaphore(), expected)

    def ring_copy(k):
        return remote(
            unit, units.at[place.z], r.ring_send.at[k], r.ring_recv.at[place.z],
            place.ring_at(place.ring_index(k)),
        )

    def ring_arrival(k):
        z = place.ring_index(k)
        return remote(unit, units.at[z], r.ring_send.at[k], r.ring_recv.at[z], place.ring_at(z))

    def send_ring():
        @pl.loop(0, rings - 1)
        def _(k):
            ring_copy(far_first(k, rings)).start()

    halo_send, halo_recv = r.halo_send, r.halo_recv
    side_copy = remote(packed.at[0], side.at[0], halo_send.at[0], halo_recv.at[0], (place.lat, place.east()))
    diag_copy = remote(
        packed.at[1], side.at[1], halo_send.at[1], halo_recv.at[1], (place.lat + 1, place.east())
    )

    def out_piece(i):
        rows = pl.ds((i % 3) * PIECE, PIECE)
        source = (tok if i < 3 else cot).at[pl.ds(half_rows + (i % 3) * PIECE, PIECE)]
        return source, (r.row_tok if i < 3 else r.row_cot).at[rows]

    def back_piece(i):
        source = r.back.at[pl.ds(half_rows + i * PIECE, PIECE)]
        return source, r.row_back.at[pl.ds(i * PIECE, PIECE)]

    class Crossing:
        def __init__(self, piece, relay_of, end, target, far_end, send, recv, sends, receives, relay, relay_sem):
            self.count = len(relay_of)
            self.relay_of, self.end, self.sends, self.receives = relay_of, end, sends, receives
            self.direct, self.via, self.onward = [], [], []
            for i in range(self.count):
                source, landing = piece(i)
                self.direct.append(remote(source, landing, send.at[i], recv.at[i], (target, place.lon)))
                self.via.append(
                    remote(source, relay, send.at[i], relay_sem.at[0], (relay_of[i], place.lon))
                )
                self.onward.append(remote(relay, landing, relay_sem.at[1], recv.at[i], (far_end, place.lon)))

        def start(self):
            plain = jnp.logical_and(self.sends, jnp.logical_not(self.end))

            @pl.when(self.end)
            def _():
                for i in range(1, self.count):
                    self.via[i].start()
                self.direct[0].start()

            @pl.when(plain)
            def _():
                for i in range(self.count):
                    self.direct[i].start()

        def pass_on(self):
            for i in range(1, self.count):
                @pl.when(place.lat == self.relay_of[i])
                def _():
                    self.via[i].wait_recv()
                    self.onward[i].start()

        def wait_recv(self):
            @pl.when(self.receives)
            def _():
                for i in range(self.count):
                    self.direct[i].wait_recv()

        def wait_send(self):
            @pl.when(self.sends)
            def _():
                for i in range(self.count):
                    self.direct[i].wait_send()

            for i in range(1, self.count):
                @pl.when(place.lat == self.relay_of[i])
                def _():
                    self.onward[i].wait_send()

    rows_out = Crossing(
        out_piece, relays.out, relays.low_end, place.lat + 1, relays.first_high,
        r.out_send, r.out_recv, not_last, not_first, r.relay, r.relay_sem,
    )
    rows_back = Crossing(
        back_piece, relays.back, relays.high_end, place.lat - 1, relays.last_low,
        r.back_send, r.back_recv, not_first, not_last, r.relay_back, r.relay_back_sem,
    )
    def send_halos():
        rows_out.start()
        side_copy.start()

        @pl.when(not_last)
        def _():
            diag_copy.start()

    blocks = r.blocks

    def tile_at(n):
        which, within = divmod(n, features // 128)
        half, at = divmod(within, width // 128)
        return half, pl.ds(which * width + at * 128, 128)

    def join_ring():
        @pl.loop(1, rings)
        def _(k):
            ring_arrival(k).wait_recv()

        for pair in range(lons // 2):
            tiles = [[], [], []]
            for z_hi in range(Z_HI):
                even = units[z_hi * lons + 2 * pair].astype(F32)
                odd = units[z_hi * lons + 2 * pair + 1].astype(F32)
                turned_top = pltpu.roll(odd[0:8], 64, 1)
                turned_low = pltpu.roll(odd[8:16], 64, 1)
                tiles[0].append(even[0:8])
                tiles[1].append(jnp.where(lane_of < 64, even[8:16], turned_top))
                tiles[2].append(jnp.where(lane_of < 64, turned_top, turned_low))
            for j in range(3):
                half, lanes = tile_at(pair * 3 + j)
                blocks[half, place.core, place.p, :, lanes] = jnp.concatenate(tiles[j], axis=0).astype(BF16)

    def plane_copy(half, k):
        own = blocks.at[half, place.core, place.p]
        return remote(
            own, own, r.plane_send.at[half, k], r.plane_recv.at[half, place.p],
            place.plane_at(place.plane_index(k)),
        )

    def plane_arrival(half, k):
        p = place.plane_index(k)
        block = blocks.at[half, place.core, p]
        return remote(block, block, r.plane_send.at[half, k], r.plane_recv.at[half, p], place.plane_at(p))

    def core_copy(half, p):
        block = blocks.at[half, place.core, p]
        return remote(block, block, r.core_send.at[half, p], r.core_recv.at[half, p], place.partner())

    def core_arrival(half, p):
        block = blocks.at[half, 1 - place.core, p]
        return remote(block, block, r.core_send.at[half, p], r.core_recv.at[half, p], place.partner())

    def send_blocks(half):
        @pl.loop(1, planes)
        def _(k):
            plane_copy(half, k).start()

        core_copy(half, place.p).start()

    own_count = counts[place.lat]
    previous = jnp.where(not_first, counts[jnp.maximum(place.lat - 1, 0)], 0)
    row_of = r.row_of[...]
    limit = jnp.where(row_of < SHIFT_ROWS, previous - SHIFT_ROWS, own_count + SHIFT_ROWS)
    valid = jnp.where(row_of < jnp.minimum(limit, WIN_ROWS), 1.0, 0.0)
    take_own, take_row, take_side = r.take_own, r.take_row, r.take_side

    def framed_of(own, row, first):
        return (
            jnp.dot(take_own[...], own[...], preferred_element_type=F32)
            + jnp.dot(take_row[...], row[...], preferred_element_type=F32)
            + jnp.dot(take_side[first], side[0], preferred_element_type=F32)
            + jnp.dot(take_side[first + 1], side[1], preferred_element_type=F32)
        )

    hidden, normed, spread, out_grad = r.hidden, r.normed, r.spread, r.out_grad
    def frame():
        rows_out.wait_recv()
        side_copy.wait_recv()

        @pl.when(not_first)
        def _():
            diag_copy.wait_recv()

        framed = framed_of(tok, r.row_tok, 0)
        center = framed - jnp.mean(framed, axis=-1, keepdims=True)
        inverse = lax.rsqrt(jnp.mean(center * center, axis=-1, keepdims=True) + EPSILON)
        normal = center * inverse
        normed[...] = normal
        spread[...] = jnp.broadcast_to(inverse, spread.shape)
        hidden[...] = normal.astype(BF16)
        r.turned_hidden[...] = normal.astype(BF16).T
        framed = framed_of(cot, r.row_cot, 2)
        for j in range(features // 128):
            lanes = slice(j * 128, j * 128 + 128)
            out_grad[:, lanes] = jnp.where(valid > 0.0, framed[:, lanes], 0.0).astype(BF16)

    weight, qkv, qkv_grad = r.weight, r.qkv, r.qkv_grad

    def forward_arrivals(half):
        @pl.loop(1, planes)
        def _(k):
            plane_arrival(half, k).wait_recv()
            core_copy(half, place.plane_index(k)).start()

    def collect(half):
        @pl.loop(0, planes)
        def _(k):
            p = place.plane_index(k)
            core_arrival(half, p).wait_recv()
            first = blocks[half, 0, p].astype(F32)
            second = blocks[half, 1, p].astype(F32)
            for z_hi in range(Z_HI):
                take = slice(z_hi * 8, z_hi * 8 + 8)
                at = pl.multiple_of((z_hi * planes + p) * 16, 16)
                weight[half, pl.ds(at, 16), :] = jnp.concatenate([first[take], second[take]], axis=0).astype(BF16)

    factor = HEAD_DIM ** (-0.5)
    allowed = jnp.concatenate([valid[0:PAD]] * (GROUP * PAD // 128), axis=1) > 0.0
    mask = r.head_mask[...]
    windows = hidden.shape[0] // PAD

    def project(half):
        qkv[half] = jnp.dot(hidden[...], weight[half], preferred_element_type=F32).astype(BF16)

    def attend(half):
        for window in range(windows):
            at = slice(window * PAD, window * PAD + PAD)
            lanes = [slice(j * width, (j + 1) * width) for j in range(3)]
            query, keyed, valued = (qkv[half, at, lane] for lane in lanes)
            grad = out_grad[at, half * width : (half + 1) * width]
            query = jnp.concatenate([query] * GROUP, axis=0) * mask
            grad = jnp.concatenate([grad] * GROUP, axis=0) * mask
            scores = contract(keyed, query, ((1,), (1,))) * factor
            scores = jnp.where(allowed, scores, -1000000000.0)
            exponent = jnp.exp(scores - jnp.max(scores, axis=0, keepdims=True))
            probs = exponent * (1.0 / jnp.sum(exponent, axis=0, keepdims=True))
            weight_grad = contract(valued, grad, ((1,), (1,)))
            mixed = jnp.sum(probs * weight_grad, axis=0, keepdims=True)
            score_grad = (probs * (weight_grad - mixed) * factor).astype(BF16)
            value_grad = jnp.dot(probs.astype(BF16), grad, preferred_element_type=F32)
            key_grad = jnp.dot(score_grad, query, preferred_element_type=F32)
            turned = contract(score_grad, keyed, ((0,), (0,)))
            query_grad = turned[0:PAD] * mask[0:PAD].astype(F32)
            for h in range(1, GROUP):
                rows_h = slice(h * PAD, h * PAD + PAD)
                query_grad = query_grad + turned[rows_h] * mask[rows_h].astype(F32)
            for lane, value in zip(lanes, (query_grad, key_grad, value_grad)):
                qkv_grad[half, at, lane] = value.astype(BF16)

    part = r.part

    def weigh(half):
        for j in range(3):
            lanes = slice(j * width, (j + 1) * width)
            piece = jnp.dot(r.turned_hidden[...], qkv_grad[half, :, lanes], preferred_element_type=F32)
            for core in range(CORES):
                for p in range(planes):
                    first = (p * CORES + core) * 8
                    both = [piece[z * planes * CORES * 8 + first :][0:8] for z in range(Z_HI)]
                    part[half, core, p, :, lanes] = jnp.concatenate(both, axis=0).astype(BF16)

    from_core, sums, from_plane, total = r.from_core, r.sums, r.from_plane, r.total

    def core_part(half, p):
        return remote(
            part.at[half, 1 - place.core, p], from_core.at[half, p],
            r.core_part_send.at[half, p], r.core_part_recv.at[half, p], place.partner(),
        )

    def plane_part(half, k):
        p = place.plane_index(k)
        return remote(
            sums.at[half, p], from_plane.at[half, place.p],
            r.plane_part_send.at[half, p], r.plane_part_recv.at[half, place.p], place.plane_at(p),
        )

    def plane_part_arrival(half, k):
        p = place.plane_index(k)
        return remote(
            sums.at[half, p], from_plane.at[half, p],
            r.plane_part_send.at[half, p], r.plane_part_recv.at[half, p], place.plane_at(p),
        )

    def send_core(half):
        @pl.loop(0, planes)
        def _(k):
            core_part(half, place.plane_index(k + 1)).start()

    def send_plane(half):
        @pl.loop(0, planes)
        def _(k):
            p = place.plane_index(k + 1)
            core_part(half, p).wait_recv()
            sums[half, p] = (part[half, place.core, p].astype(F32) + from_core[half, p].astype(F32)).astype(BF16)

            @pl.when(k < planes - 1)
            def _():
                plane_part(half, k + 1).start()

    def add_plane(half):
        total[half] = sums[half, place.p].astype(F32)

        @pl.loop(1, planes)
        def _(k):
            plane_part_arrival(half, k).wait_recv()
            total[half] += from_plane[half, place.plane_index(k)].astype(F32)

    back, side_back = r.back, r.side_back
    side_return = remote(
        back.at[pl.ds(2 * half_rows, 32)], side_back.at[0], halo_send.at[2], halo_recv.at[2],
        (place.lat, place.west()),
    )
    diag_return = remote(
        back.at[pl.ds(2 * half_rows + 32, 32)], side_back.at[1], halo_send.at[3], halo_recv.at[3],
        (place.lat - 1, place.west()),
    )
    def differentiate():
        hidden_grad = contract(qkv_grad[0], weight[0], ((1,), (1,))) + contract(qkv_grad[1], weight[1], ((1,), (1,)))
        normal = normed[...]
        mean_grad = jnp.mean(hidden_grad, axis=-1, keepdims=True)
        mean_mixed = jnp.mean(hidden_grad * normal, axis=-1, keepdims=True)
        frame_grad = spread[...] * (hidden_grad - mean_grad - normal * mean_mixed)
        back[...] = jnp.dot(r.give[...], frame_grad.astype(BF16), preferred_element_type=F32).astype(BF16)

    def return_halos():
        rows_back.start()
        side_return.start()

        @pl.when(not_first)
        def _():
            diag_return.start()

    part_units, from_ring = r.part_units, r.from_ring

    def ring_part(k):
        z = place.ring_index(k)
        return remote(
            part_units.at[z], from_ring.at[place.z], r.ring_part_send.at[z],
            r.ring_part_recv.at[place.z], place.ring_at(z),
        )

    def ring_part_arrival(k):
        z = place.ring_index(k)
        return remote(
            part_units.at[z], from_ring.at[z], r.ring_part_send.at[z], r.ring_part_recv.at[z],
            place.ring_at(z),
        )

    def send_ring_parts():
        for pair in range(lons // 2):
            for z_hi in range(Z_HI):
                tiles = []
                for j in range(3):
                    half, lanes = tile_at(pair * 3 + j)
                    tiles.append(total[half, pl.ds(z_hi * 8, 8), lanes])
                turned = [pltpu.roll(tile, 64, 1) for tile in tiles]
                part_units[z_hi * lons + 2 * pair] = jnp.concatenate([tiles[0], tiles[1]], axis=0).astype(BF16)
                part_units[z_hi * lons + 2 * pair + 1] = jnp.concatenate(
                    [jnp.where(lane_of < 64, turned[1], turned[2]), turned[2]], axis=0
                ).astype(BF16)

        @pl.loop(0, rings - 1)
        def _(k):
            ring_part(far_first(k, rings)).start()

        from_ring[place.z] = part_units[place.z]

    def finish_tokens():
        rows_back.wait_recv()
        side_return.wait_recv()

        @pl.when(not_last)
        def _():
            diag_return.wait_recv()

        for part_of in range(2):
            rows = pl.ds(part_of * half_rows, half_rows)
            inner = back[0:half_rows] if part_of == 0 else r.row_back[...]
            outer = jnp.dot(r.place_sel[...], side_back[part_of], preferred_element_type=F32)
            token_grad[rows] = (cot[rows].astype(F32) + (inner.astype(F32) + outer)).astype(BF16)

    def finish_weight():
        @pl.loop(1, rings)
        def _(k):
            ring_part_arrival(k).wait_recv()

        result = from_ring[0].astype(F32)
        for z in range(1, rings):
            result = result + from_ring[z].astype(F32)
        weight_gradient[:, 0:128] = result[0:8]
        weight_gradient[:, 128:192] = result[8:16, 0:64]

    def drain():
        rows_out.wait_send()
        rows_back.wait_send()
        side_copy.wait_send()
        side_return.wait_send()

        @pl.when(not_last)
        def _():
            diag_copy.wait_send()

        @pl.when(not_first)
        def _():
            diag_return.wait_send()

        @pl.loop(1, rings)
        def _(k):
            ring_copy(k).wait_send()
            ring_part(k).wait_send()

        for half in range(HALVES):
            @pl.loop(1, planes)
            def _(k):
                plane_copy(half, k).wait_send()
                plane_part(half, k).wait_send()

            @pl.loop(0, planes)
            def _(k):
                core_copy(half, k).wait_send()
                core_part(half, k).wait_send()

    send_ring()
    send_halos()
    join_ring()
    send_blocks(0)
    send_blocks(1)
    rows_out.pass_on()
    frame()
    forward_arrivals(0)
    collect(0)
    project(0)
    attend(0)
    weigh(0)
    send_core(0)
    forward_arrivals(1)
    collect(1)
    project(1)
    send_plane(0)
    attend(1)
    weigh(1)
    send_core(1)
    differentiate()
    return_halos()
    send_plane(1)
    rows_back.pass_on()
    add_plane(0)
    add_plane(1)
    send_ring_parts()
    finish_tokens()
    finish_weight()
    drain()


def frame_tables(cols):
    windows = cols // WIN_COLS
    total = windows * PAD
    half = SHIFT_ROWS * cols
    own = np.zeros((total, 2 * half), np.float32)
    row = np.zeros((total, half), np.float32)
    side = np.zeros((4, total, 48), np.float32)
    give = np.zeros((2 * half + 64, total), np.float32)
    row_of = np.full((total, 128), WIN_ROWS, np.int32)
    for window in range(windows):
        for r in range(WIN_ROWS):
            for c in range(WIN_COLS):
                t = window * PAD + r * WIN_COLS + c
                row_of[t] = r
                rr, g = r - SHIFT_ROWS, window * WIN_COLS + c - SHIFT_COLS
                upper = rr < 0
                if g >= 0:
                    if upper:
                        row[t, r * cols + g] = 1
                        give[half + r * cols + g, t] = 1
                    else:
                        own[t, rr * cols + g] = 1
                        give[rr * cols + g, t] = 1
                else:
                    at = (r % SHIFT_ROWS) * SHIFT_COLS + g + SHIFT_COLS
                    side[int(upper), t, at] = 1
                    side[2 + int(upper), t, 18 + at] = 1
                    give[2 * half + 32 * int(upper) + at, t] = 1
    return own, row, side, give, row_of


def on_device(lats, lons, tokens, cotangent, qkv_weight, band_rows):
    features = tokens.shape[-1]
    tok = tokens.reshape(-1, features)
    cot = cotangent.reshape(-1, features)
    count = tok.shape[0]
    half = count // 2
    cols = half // SHIFT_ROWS
    planes, rings = Y * X, Z_HI * lons
    columns = qkv_weight.shape[1] * lons
    width = GROUP * HEAD_DIM
    take_own, take_row, take_side, give, row_of = frame_tables(cols)
    total = take_own.shape[0]
    sel = np.zeros((2, 48, half), np.float32)
    place_sel = np.zeros((half, 32), np.float32)
    for row in range(SHIFT_ROWS):
        for col in range(SHIFT_COLS):
            at, edge = row * SHIFT_COLS + col, row * cols + cols - SHIFT_COLS + col
            sel[0, at, edge] = 1
            sel[1, 18 + at, edge] = 1
            place_sel[edge, at] = 1
    head_mask = np.zeros((GROUP, PAD, GROUP, HEAD_DIM), np.float32)
    for h in range(GROUP):
        head_mask[h, :, h] = 1
    low = lambda table: jnp.asarray(table, BF16)
    loaded = dict(
        tok=tok, cot=cot, sel=low(sel), row_of=jnp.asarray(row_of), take_own=low(take_own), take_row=low(take_row),
        take_side=low(take_side), head_mask=low(head_mask.reshape(GROUP * PAD, width)), give=low(give),
        place_sel=low(place_sel),
    )
    dma = pltpu.SemaphoreType.DMA
    scratch = {name: VMEM(array.shape, array.dtype) for name, array in loaded.items()}
    scratch.update(
        wide=VMEM((8, 256), F32),
        unit=VMEM((16, 128), BF16),
        units=VMEM((rings, 16, 128), BF16),
        blocks=VMEM((HALVES, CORES, planes, 16, columns // HALVES), BF16),
        packed=VMEM((2, 48, features), BF16),
        side=VMEM((2, 48, features), BF16),
        row_tok=VMEM((half, features), BF16),
        row_cot=VMEM((half, features), BF16),
        relay=VMEM((PIECE, features), BF16),
        relay_back=VMEM((PIECE, features), BF16),
        weight=VMEM((HALVES, features, columns // HALVES), BF16),
        hidden=VMEM((total, features), BF16),
        turned_hidden=VMEM((features, total), BF16),
        normed=VMEM((total, features), F32),
        spread=VMEM((total, features), F32),
        out_grad=VMEM((total, features), BF16),
        qkv=VMEM((HALVES, total, columns // HALVES), BF16),
        qkv_grad=VMEM((HALVES, total, columns // HALVES), BF16),
        part=VMEM((HALVES, CORES, planes, 16, columns // HALVES), BF16),
        from_core=VMEM((HALVES, planes, 16, columns // HALVES), BF16),
        sums=VMEM((HALVES, planes, 16, columns // HALVES), BF16),
        from_plane=VMEM((HALVES, planes, 16, columns // HALVES), BF16),
        total=VMEM((HALVES, 16, columns // HALVES), F32),
        back=VMEM(give.shape[:1] + (features,), BF16),
        row_back=VMEM((half, features), BF16),
        side_back=VMEM((2, 32, features), BF16),
        part_units=VMEM((rings, 16, 128), BF16),
        from_ring=VMEM((rings, 16, 128), BF16),
        load_sem=dma((len(loaded),)),
        relay_sem=dma((2,)),
        relay_back_sem=dma((2,)),
    )
    both = dict(
        ring=(rings,), plane=(HALVES, planes), core=(HALVES, planes), halo=(4,), out=(len(OUT_COLUMNS),),
        back=(len(BACK_COLUMNS),), core_part=(HALVES, planes), plane_part=(HALVES, planes), ring_part=(rings,),
    )
    for name, shape in both.items():
        scratch[name + "_send"] = dma(shape)
        scratch[name + "_recv"] = dma(shape)
    token_grad, weight_gradient = pl.pallas_call(
        functools.partial(kernel, lats, lons, len(loaded), list(scratch)),
        out_shape=(
            jax.ShapeDtypeStruct(tok.shape, BF16),
            jax.ShapeDtypeStruct(qkv_weight.shape, F32),
        ),
        in_specs=[pl.BlockSpec(memory_space=pltpu.SMEM), pl.BlockSpec(memory_space=VMEM)]
        + [pl.BlockSpec(memory_space=pl.ANY)] * len(loaded),
        out_specs=[pl.BlockSpec(memory_space=VMEM)] * 2,
        scratch_shapes=list(scratch.values()),
        compiler_params=pltpu.CompilerParams(
            collective_id=0, has_side_effects=True, vmem_limit_bytes=56 * 2**20
        ),
        name="sub_block",
    )(band_rows, qkv_weight, *loaded.values())
    return token_grad.reshape(tokens.shape), weight_gradient


def solution(mesh):
    return jax.shard_map(
        functools.partial(on_device, mesh.shape["lat"], mesh.shape["lon"]),
        mesh=mesh,
        in_specs=(P("lat", "lon", None), P("lat", "lon", None), P("lat", "lon"), P()),
        out_specs=(P("lat", "lon", None), P("lat", "lon")),
        check_vma=False,
    )
```

```python
import functools
import types

import jax
import jax.numpy as jnp
import numpy as np
from jax import lax
from jax.experimental import pallas as pl
from jax.experimental.pallas import tpu as pltpu
from jax.sharding import PartitionSpec as P

MESH = pl.DeviceIdType.MESH
VMEM = pltpu.VMEM
BF16 = jnp.bfloat16
F32 = jnp.float32

WIN_ROWS = 6
WIN_COLS = 12
SHIFT_ROWS = 3
SHIFT_COLS = 6
HEAD_DIM = 32
EPSILON = 1e-05

Z_HI, Y, X, CORES = 2, 4, 4, 2


class Place:
    def __init__(self, lats, lons):
        self.lats, self.lons = lats, lons
        self.planes = Y * X
        self.rings = Z_HI * lons
        self.lat = lax.axis_index("lat")
        self.lon = lax.axis_index("lon")
        self.z_hi = lax.div(self.lat, self.planes * CORES)
        self.p = lax.div(lax.rem(self.lat, self.planes * CORES), CORES)
        self.core = lax.rem(self.lat, CORES)
        self.z = self.z_hi * lons + self.lon

    def ring_at(self, z):
        return (lax.div(z, self.lons) * self.planes * CORES + self.p * CORES + self.core, lax.rem(z, self.lons))

    def plane_at(self, p):
        return (self.z_hi * self.planes * CORES + p * CORES + self.core, self.lon)

    def ring_index(self, k):
        return lax.rem(self.z + k, self.rings)

    def plane_index(self, k):
        x = lax.rem(lax.rem(self.p, X) + lax.rem(k, X), X)
        y = lax.rem(lax.div(self.p, X) + lax.div(k, X), Y)
        return y * X + x

    def partner(self):
        return (self.lat + 1 - 2 * self.core, self.lon)

    def east(self):
        return lax.rem(self.lon + 1, self.lons)

    def west(self):
        return lax.rem(self.lon + self.lons - 1, self.lons)


def remote(src, dst, send, recv, device):
    return pltpu.make_async_remote_copy(
        src_ref=src, dst_ref=dst, send_sem=send, recv_sem=recv, device_id=device, device_id_type=MESH
    )


OUT_ROWS = (
    (0, Y - 1), (X - 1, 0), (0, 0), (1, 0), (0, 1), (X - 2, 0), (0, Y - 2), (1, Y - 1), (X - 1, 1),
)
OUT_CORNER = ((X - 2, Y - 1), (X - 1, Y - 2), (1, 1))
BACK_ROWS = (
    (X - 1, 0), (0, Y - 1), (X - 1, Y - 1), (X - 2, Y - 1), (X - 1, Y - 2), (1, Y - 1), (X - 1, 1), (X - 2, 0),
    (0, Y - 2),
)
BACK_CORNER = ((1, 0), (X - 2, Y - 2))
TILE = 16

PAD = 80
GROUP = 4


class Relays:
    def __init__(self, place):
        self.last_low = place.planes * CORES - 1
        self.first_high = place.planes * CORES
        self.low_end = place.lat == self.last_low
        self.high_end = place.lat == self.first_high

        def low(columns):
            return [(y * X + x) * CORES + CORES - 1 for x, y in columns]

        def high(columns):
            return [self.first_high + (y * X + x) * CORES for x, y in columns]

        self.out_rows, self.out_corner = low(OUT_ROWS), low(OUT_CORNER)
        self.back_rows, self.back_corner = high(BACK_ROWS), high(BACK_CORNER)


def far_first(k, count):
    half = count // 2
    return half + (1 - 2 * lax.rem(k, 2)) * lax.div(k + 1, 2)


def announce(place, relays):
    barrier = pltpu.get_barrier_semaphore()

    def signal(device):
        pl.semaphore_signal(barrier, inc=1, device_id=device, device_id_type=MESH)

    count = place.rings + place.planes - 1

    for ends, groups in (
        (relays.high_end, ((relays.out_rows, place.lon), (relays.out_corner, place.west()))),
        (relays.low_end, ((relays.back_rows, place.lon), (relays.back_corner, place.east()))),
    ):
        for lats, lon in groups:
            @pl.when(ends)
            def _():
                for lat in lats:
                    signal((lat, lon))

            for lat in lats:
                count = count + jnp.where(place.lat == lat, 1, 0)

    above = jnp.logical_and(place.lat > 0, jnp.logical_not(relays.high_end))
    below = jnp.logical_and(place.lat < place.lats - 1, jnp.logical_not(relays.low_end))

    @pl.when(above)
    def _():
        signal((place.lat - 1, place.lon))
        signal((place.lat - 1, place.west()))

    @pl.when(below)
    def _():
        signal((place.lat + 1, place.lon))
        signal((place.lat + 1, place.east()))

    count = count + jnp.where(above, 2, 0) + jnp.where(below, 2, 0)

    @pl.loop(0, place.rings - 1)
    def _(k):
        signal(place.ring_at(place.ring_index(far_first(k, place.rings))))

    @pl.loop(1, place.planes)
    def _(k):
        signal(place.plane_at(place.plane_index(k)))

    signal(place.partner())
    return count


def contract(left, right, dims):
    return lax.dot_general(left, right, (dims, ((), ())), preferred_element_type=F32)


def kernel(lats, lons, loaded, names, *refs):
    sources, returned, weight_gradient = refs[:loaded], refs[loaded], refs[loaded + 1]
    refs = refs[loaded + 2 :]
    targets = refs[:loaded]
    r = types.SimpleNamespace(**dict(zip(names, refs)))
    place = Place(lats, lons)
    relays = Relays(place)
    tok, cot = r.tok, r.cot
    half_rows = tok.shape[0] // 2
    features = tok.shape[1]
    width = GROUP * HEAD_DIM
    groups = features // width
    planes, rings = place.planes, place.rings
    lane_of = lax.broadcasted_iota(jnp.int32, (8, 128), 1)
    not_first = place.lat > 0
    not_last = place.lat < lats - 1

    loads = [
        pltpu.make_async_copy(source, target, r.load_sem.at[i])
        for i, (source, target) in enumerate(zip(sources, targets))
    ]
    for load in loads:
        load.start()

    expected = announce(place, relays)

    wide, unit, units = r.wide, r.unit, r.units
    wide[...] = jnp.zeros_like(wide)
    loads[0].wait()
    wide[:, 0 : r.w_in.shape[1]] = r.w_in[...].astype(F32)
    unit[...] = jnp.concatenate([wide[:, 0:128], wide[:, 128:256]], axis=0).astype(BF16)
    units[place.z] = unit[...]
    for load in loads[1:]:
        load.wait()

    packed, side, sel = r.packed, r.side, r.sel
    for part_of in range(2):
        rows = pl.ds(part_of * half_rows, half_rows)
        packed[part_of] = (
            jnp.dot(sel[0], tok[rows], preferred_element_type=F32)
            + jnp.dot(sel[1], cot[rows], preferred_element_type=F32)
        ).astype(BF16)

    @pl.when(jnp.logical_not(not_first))
    def _():
        side[1] = jnp.zeros(side.shape[1:], BF16)
        r.row_tok[...] = jnp.zeros_like(r.row_tok)
        r.row_cot[...] = jnp.zeros_like(r.row_cot)

    @pl.when(jnp.logical_not(not_last))
    def _():
        r.row_back[...] = jnp.zeros_like(r.row_back)
        r.side_back[1] = jnp.zeros(r.side_back.shape[1:], BF16)

    pl.semaphore_wait(pltpu.get_barrier_semaphore(), expected)

    def ring_copy(k):
        return remote(
            unit, units.at[place.z], r.ring_send.at[0], r.ring_recv.at[0], place.ring_at(place.ring_index(k))
        )

    others = pl.ds(0, rings - 1)
    ring_all = remote(units.at[others], units.at[others], r.ring_send.at[0], r.ring_recv.at[0], place.partner())

    def send_ring():
        @pl.loop(0, rings - 1)
        def _(k):
            ring_copy(far_first(k, rings)).start()

    halo_send, halo_recv = r.halo_send, r.halo_recv
    side_copy = remote(packed.at[0], side.at[0], halo_send.at[0], halo_recv.at[0], (place.lat, place.east()))

    class Crossing:
        def __init__(self, sources, landings, lats, end, sends, receives, target, far, send, recv, relay, relay_sem):
            self.lats, self.end, self.sends, self.receives = lats, end, sends, receives
            self.direct, self.via, self.onward = [], [[] for _ in lats], [[] for _ in lats]
            for j, (source, landing) in enumerate(zip(sources, landings)):
                self.direct.append(remote(source, landing, send.at[j], recv.at[j], target))
                passing = relay.at[pl.ds(j * TILE, TILE)]
                for i, lat in enumerate(lats):
                    rows = pl.ds(i * TILE, TILE)
                    self.via[i].append(
                        remote(source.at[rows], passing, send.at[j], relay_sem.at[0], (lat, place.lon))
                    )
                    self.onward[i].append(
                        remote(passing, landing.at[rows], relay_sem.at[1], recv.at[j], far)
                    )
            self.passing = remote(relay, relay, relay_sem.at[1], relay_sem.at[0], place.partner())

        def start_relayed(self):
            @pl.when(self.end)
            def _():
                for copies in self.via:
                    for copy in copies:
                        copy.start()

        def start(self):
            @pl.when(jnp.logical_and(self.sends, jnp.logical_not(self.end)))
            def _():
                for copy in self.direct:
                    copy.start()

        def pass_on(self):
            is_relay = functools.reduce(jnp.logical_or, [place.lat == lat for lat in self.lats])

            @pl.when(is_relay)
            def _():
                self.passing.wait_recv()

            for lat, copies in zip(self.lats, self.onward):
                @pl.when(place.lat == lat)
                def _():
                    for copy in copies:
                        copy.start()

        def wait_recv(self):
            @pl.when(self.receives)
            def _():
                for copy in self.direct:
                    copy.wait_recv()

        def wait_send(self):
            @pl.when(self.sends)
            def _():
                for copy in self.direct:
                    copy.wait_send()

            is_relay = functools.reduce(jnp.logical_or, [place.lat == lat for lat in self.lats])

            @pl.when(is_relay)
            def _():
                self.passing.wait_send()

    back, side_back = r.back, r.side_back
    last_rows = pl.ds(half_rows, half_rows)
    rows_out = Crossing(
        [tok.at[last_rows], cot.at[last_rows]], [r.row_tok, r.row_cot], relays.out_rows, relays.low_end,
        not_last, not_first, (place.lat + 1, place.lon), (relays.first_high, place.lon),
        r.out_send, r.out_recv, r.relay, r.relay_sem,
    )
    corner_out = Crossing(
        [packed.at[1]], [side.at[1]], relays.out_corner, relays.low_end,
        not_last, not_first, (place.lat + 1, place.east()), (relays.first_high, place.east()),
        r.corner_send, r.corner_recv, r.corner, r.corner_sem,
    )
    rows_back = Crossing(
        [back.at[last_rows]], [r.row_back], relays.back_rows, relays.high_end,
        not_first, not_last, (place.lat - 1, place.lon), (relays.last_low, place.lon),
        r.back_send, r.back_recv, r.relay_back, r.relay_back_sem,
    )
    corner_back = Crossing(
        [back.at[pl.ds(2 * half_rows + 32, 32)]], [side_back.at[1]], relays.back_corner, relays.high_end,
        not_first, not_last, (place.lat - 1, place.west()), (relays.last_low, place.west()),
        r.corner_back_send, r.corner_back_recv, r.corner_back, r.corner_back_sem,
    )
    side_return = remote(
        back.at[pl.ds(2 * half_rows, 32)], side_back.at[0], halo_send.at[1], halo_recv.at[1],
        (place.lat, place.west()),
    )

    def send_relayed():
        rows_out.start_relayed()
        corner_out.start_relayed()

    def send_halos():
        rows_out.start()
        corner_out.start()
        side_copy.start()

    def pass_on():
        rows_out.pass_on()
        corner_out.pass_on()

    blocks = r.blocks

    def tile_at(n):
        which, group = divmod(n, groups)
        return group, pl.ds(which * width, width)

    def join_ring():
        ring_all.wait_recv()

        for pair in range(lons // 2):
            tiles = [[], [], []]
            for z_hi in range(Z_HI):
                even = units[z_hi * lons + 2 * pair].astype(F32)
                odd = units[z_hi * lons + 2 * pair + 1].astype(F32)
                turned_top = pltpu.roll(odd[0:8], 64, 1)
                turned_low = pltpu.roll(odd[8:16], 64, 1)
                tiles[0].append(even[0:8])
                tiles[1].append(jnp.where(lane_of < 64, even[8:16], turned_top))
                tiles[2].append(jnp.where(lane_of < 64, turned_top, turned_low))
            for j in range(3):
                group, lanes = tile_at(pair * 3 + j)
                blocks[group, place.core, place.p, :, lanes] = jnp.concatenate(tiles[j], axis=0).astype(BF16)

    def plane_copy(group, k):
        own = blocks.at[group, place.core, place.p]
        return remote(
            own, own, r.plane_send.at[group], r.plane_recv.at[group], place.plane_at(place.plane_index(k))
        )

    def plane_all(group):
        others = blocks.at[group, place.core, pl.ds(0, planes - 1)]
        return remote(others, others, r.plane_send.at[group], r.plane_recv.at[group], place.partner())

    def core_copy(group):
        block = blocks.at[group, place.core]
        return remote(block, block, r.core_send.at[group], r.core_recv.at[group], place.partner())

    def core_arrival(group):
        block = blocks.at[group, 1 - place.core]
        return remote(block, block, r.core_send.at[group], r.core_recv.at[group], place.partner())

    def send_blocks(group):
        @pl.loop(1, planes)
        def _(k):
            plane_copy(group, k).start()

    own_count = r.counts[place.lat]
    previous = jnp.where(not_first, r.counts[jnp.maximum(place.lat - 1, 0)], 0)
    row_of = r.row_of[...]
    limit = jnp.where(row_of < SHIFT_ROWS, previous - SHIFT_ROWS, own_count + SHIFT_ROWS)
    valid = jnp.where(row_of < jnp.minimum(limit, WIN_ROWS), 1.0, 0.0)
    take_own, take_row, take_side = r.take_own, r.take_row, r.take_side

    def framed_of(own, row, first):
        return (
            jnp.dot(take_own[...], own[...], preferred_element_type=F32)
            + jnp.dot(take_row[...], row[...], preferred_element_type=F32)
            + jnp.dot(take_side[first], side[0], preferred_element_type=F32)
            + jnp.dot(take_side[first + 1], side[1], preferred_element_type=F32)
        )

    hidden, normed, spread, out_grad = r.hidden, r.normed, r.spread, r.out_grad
    def frame():
        rows_out.wait_recv()
        corner_out.wait_recv()
        side_copy.wait_recv()

        framed = framed_of(tok, r.row_tok, 0)
        center = framed - jnp.mean(framed, axis=-1, keepdims=True)
        inverse = lax.rsqrt(jnp.mean(center * center, axis=-1, keepdims=True) + EPSILON)
        normal = center * inverse
        normed[...] = normal
        spread[...] = jnp.broadcast_to(inverse, spread.shape)
        hidden[...] = normal.astype(BF16)
        r.turned_hidden[...] = normal.astype(BF16).T
        framed = framed_of(cot, r.row_cot, 2)
        for j in range(features // 128):
            lanes = slice(j * 128, j * 128 + 128)
            out_grad[:, lanes] = jnp.where(valid > 0.0, framed[:, lanes], 0.0).astype(BF16)

    weight, qkv, qkv_grad = r.weight, r.qkv, r.qkv_grad

    def forward_arrivals(group):
        plane_all(group).wait_recv()
        core_copy(group).start()

    def collect(group):
        core_arrival(group).wait_recv()
        for p in range(planes):
            first = blocks[group, 0, p].astype(F32)
            second = blocks[group, 1, p].astype(F32)
            for z_hi in range(Z_HI):
                take = slice(z_hi * 8, z_hi * 8 + 8)
                rows = pl.ds((z_hi * planes + p) * 16, 16)
                weight[group, rows, :] = jnp.concatenate([first[take], second[take]], axis=0).astype(BF16)

    factor = HEAD_DIM ** (-0.5)
    whole, rest = divmod(GROUP * PAD, 128)
    allowed = jnp.concatenate([valid[0:PAD]] * whole + [valid[0:PAD, 0:rest]], axis=1) > 0.0
    mask = r.head_mask[...]
    windows = hidden.shape[0] // PAD

    def project(group):
        qkv[group] = jnp.dot(hidden[...], weight[group], preferred_element_type=F32).astype(BF16)

    def attend(group):
        for window in range(windows):
            at = slice(window * PAD, window * PAD + PAD)
            lanes = [slice(j * width, (j + 1) * width) for j in range(3)]
            query, keyed, valued = (qkv[group, at, lane] for lane in lanes)
            grad = out_grad[at, group * width : (group + 1) * width]
            query = jnp.concatenate([query] * GROUP, axis=0) * mask
            grad = jnp.concatenate([grad] * GROUP, axis=0) * mask
            scores = contract(keyed, query, ((1,), (1,))) * factor
            scores = jnp.where(allowed, scores, -1000000000.0)
            exponent = jnp.exp(scores - jnp.max(scores, axis=0, keepdims=True))
            probs = exponent * (1.0 / jnp.sum(exponent, axis=0, keepdims=True))
            weight_grad = contract(valued, grad, ((1,), (1,)))
            mixed = jnp.sum(probs * weight_grad, axis=0, keepdims=True)
            score_grad = (probs * (weight_grad - mixed) * factor).astype(BF16)
            value_grad = jnp.dot(probs.astype(BF16), grad, preferred_element_type=F32)
            key_grad = jnp.dot(score_grad, query, preferred_element_type=F32)
            turned = contract(score_grad, keyed, ((0,), (0,)))
            query_grad = turned[0:PAD] * mask[0:PAD].astype(F32)
            for h in range(1, GROUP):
                rows_h = slice(h * PAD, h * PAD + PAD)
                query_grad = query_grad + turned[rows_h] * mask[rows_h].astype(F32)
            for lane, value in zip(lanes, (query_grad, key_grad, value_grad)):
                qkv_grad[group, at, lane] = value.astype(BF16)

    part = r.part

    def weigh(group):
        for j in range(3):
            lanes = slice(j * width, (j + 1) * width)
            piece = jnp.dot(r.turned_hidden[...], qkv_grad[group, :, lanes], preferred_element_type=F32)
            for core in range(CORES):
                for p in range(planes):
                    first = (p * CORES + core) * 8
                    both = [piece[z * planes * CORES * 8 + first :][0:8] for z in range(Z_HI)]
                    part[group, core, p, :, lanes] = jnp.concatenate(both, axis=0).astype(BF16)

    from_core, sums, from_plane, total = r.from_core, r.sums, r.from_plane, r.total

    def core_part(group):
        return remote(
            part.at[group, 1 - place.core], from_core.at[group],
            r.core_part_send.at[group], r.core_part_recv.at[group], place.partner(),
        )

    def plane_part(group, k):
        p = place.plane_index(k)
        return remote(
            sums.at[group, p], from_plane.at[group, place.p],
            r.plane_part_send.at[group], r.plane_part_recv.at[group], place.plane_at(p),
        )

    def plane_part_all(group):
        others = pl.ds(0, planes - 1)
        return remote(
            sums.at[group, others], from_plane.at[group, others],
            r.plane_part_send.at[group], r.plane_part_recv.at[group], place.partner(),
        )

    def send_core(group):
        core_part(group).start()

    def send_plane(group):
        core_part(group).wait_recv()
        sums[group] = (part[group, place.core].astype(F32) + from_core[group].astype(F32)).astype(BF16)

        @pl.loop(1, planes)
        def _(k):
            plane_part(group, k).start()

        from_plane[group, place.p] = sums[group, place.p]

    def add_plane(group):
        plane_part_all(group).wait_recv()
        total[group] = jnp.sum(from_plane[group].astype(F32), axis=0)

    def accumulate(group):
        term = contract(qkv_grad[group], weight[group], ((1,), (1,)))
        if group == 0:
            r.hidden_grad[...] = term
        else:
            r.hidden_grad[...] += term

    def differentiate():
        hidden_grad = r.hidden_grad[...]
        normal = normed[...]
        mean_grad = jnp.mean(hidden_grad, axis=-1, keepdims=True)
        mean_mixed = jnp.mean(hidden_grad * normal, axis=-1, keepdims=True)
        frame_grad = spread[...] * (hidden_grad - mean_grad - normal * mean_mixed)
        back[...] = jnp.dot(r.give[...], frame_grad.astype(BF16), preferred_element_type=F32).astype(BF16)

    def return_relayed():
        rows_back.start_relayed()
        corner_back.start_relayed()

    def return_halos():
        rows_back.start()
        corner_back.start()
        side_return.start()

    def pass_back():
        rows_back.pass_on()
        corner_back.pass_on()

    part_units, from_ring = r.part_units, r.from_ring

    def ring_part(k):
        z = place.ring_index(k)
        return remote(
            part_units.at[z], from_ring.at[place.z], r.ring_part_send.at[0], r.ring_part_recv.at[0],
            place.ring_at(z),
        )

    ring_part_all = remote(
        part_units.at[others], from_ring.at[others], r.ring_part_send.at[0], r.ring_part_recv.at[0],
        place.partner(),
    )

    def send_ring_parts():
        for pair in range(lons // 2):
            for z_hi in range(Z_HI):
                tiles = []
                for j in range(3):
                    group, lanes = tile_at(pair * 3 + j)
                    tiles.append(total[group, pl.ds(z_hi * 8, 8), lanes])
                turned = [pltpu.roll(tile, 64, 1) for tile in tiles]
                part_units[z_hi * lons + 2 * pair] = jnp.concatenate([tiles[0], tiles[1]], axis=0).astype(BF16)
                part_units[z_hi * lons + 2 * pair + 1] = jnp.concatenate(
                    [jnp.where(lane_of < 64, turned[1], turned[2]), turned[2]], axis=0
                ).astype(BF16)

        @pl.loop(0, rings - 1)
        def _(k):
            ring_part(far_first(k, rings)).start()

        from_ring[place.z] = part_units[place.z]

    def finish_tokens():
        rows_back.wait_recv()
        corner_back.wait_recv()
        side_return.wait_recv()

        for part_of in range(2):
            rows = pl.ds(part_of * half_rows, half_rows)
            inner = back[0:half_rows] if part_of == 0 else r.row_back[...]
            outer = jnp.dot(r.place_sel[...], side_back[part_of], preferred_element_type=F32)
            returned[rows] = (inner.astype(F32) + outer).astype(BF16)

    def finish_weight():
        ring_part_all.wait_recv()

        result = from_ring[0].astype(F32)
        for z in range(1, rings):
            result = result + from_ring[z].astype(F32)
        weight_gradient[:, 0:128] = result[0:8]
        weight_gradient[:, 128:192] = result[8:16, 0:64]

    def drain():
        rows_out.wait_send()
        rows_back.wait_send()
        corner_out.wait_send()
        corner_back.wait_send()
        side_copy.wait_send()
        side_return.wait_send()
        ring_all.wait_send()
        ring_part_all.wait_send()
        for group in range(groups):
            plane_all(group).wait_send()
            plane_part_all(group).wait_send()
            core_copy(group).wait_send()
            core_part(group).wait_send()

    send_relayed()
    send_ring()
    send_halos()
    pass_on()
    join_ring()
    for group in range(groups):
        send_blocks(group)
    frame()
    forward_arrivals(0)
    for group in range(groups):
        collect(group)
        project(group)
        attend(group)
        if group > 0:
            send_plane(group - 1)
        if group < groups - 1:
            forward_arrivals(group + 1)
        weigh(group)
        send_core(group)
        accumulate(group)
    differentiate()
    return_relayed()
    send_plane(groups - 1)
    return_halos()
    for group in range(groups - 1):
        add_plane(group)
    pass_back()
    add_plane(groups - 1)
    send_ring_parts()
    finish_tokens()
    finish_weight()
    drain()


def frame_tables(cols):
    windows = cols // WIN_COLS
    total = windows * PAD
    half = SHIFT_ROWS * cols
    own = np.zeros((total, 2 * half), np.float32)
    row = np.zeros((total, half), np.float32)
    side = np.zeros((4, total, 48), np.float32)
    give = np.zeros((2 * half + 64, total), np.float32)
    row_of = np.full((total, 128), WIN_ROWS, np.int32)
    for window in range(windows):
        for r in range(WIN_ROWS):
            for c in range(WIN_COLS):
                t = window * PAD + r * WIN_COLS + c
                row_of[t] = r
                rr, g = r - SHIFT_ROWS, window * WIN_COLS + c - SHIFT_COLS
                upper = rr < 0
                if g >= 0:
                    if upper:
                        row[t, r * cols + g] = 1
                        give[half + r * cols + g, t] = 1
                    else:
                        own[t, rr * cols + g] = 1
                        give[rr * cols + g, t] = 1
                else:
                    at = (r % SHIFT_ROWS) * SHIFT_COLS + g + SHIFT_COLS
                    side[int(upper), t, at] = 1
                    side[2 + int(upper), t, 18 + at] = 1
                    give[2 * half + 32 * int(upper) + at, t] = 1
    return own, row, side, give, row_of


def on_device(lats, lons, tokens, cotangent, qkv_weight, band_rows):
    features = tokens.shape[-1]
    tok = tokens.reshape(-1, features)
    cot = cotangent.reshape(-1, features)
    count = tok.shape[0]
    half = count // 2
    cols = half // SHIFT_ROWS
    planes, rings = Y * X, Z_HI * lons
    columns = qkv_weight.shape[1] * lons
    width = GROUP * HEAD_DIM
    groups = features // width
    take_own, take_row, take_side, give, row_of = frame_tables(cols)
    total = take_own.shape[0]
    sel = np.zeros((2, 48, half), np.float32)
    place_sel = np.zeros((half, 32), np.float32)
    for row in range(SHIFT_ROWS):
        for col in range(SHIFT_COLS):
            at, edge = row * SHIFT_COLS + col, row * cols + cols - SHIFT_COLS + col
            sel[0, at, edge] = 1
            sel[1, 18 + at, edge] = 1
            place_sel[edge, at] = 1
    head_mask = np.zeros((GROUP, PAD, GROUP, HEAD_DIM), np.float32)
    for h in range(GROUP):
        head_mask[h, :, h] = 1
    low = lambda table: jnp.asarray(table, BF16)
    loaded = dict(
        w_in=qkv_weight, counts=band_rows, tok=tok, cot=cot, sel=low(sel), row_of=jnp.asarray(row_of), take_own=low(take_own), take_row=low(take_row),
        take_side=low(take_side), head_mask=low(head_mask.reshape(GROUP * PAD, width)), give=low(give),
        place_sel=low(place_sel),
    )
    dma = pltpu.SemaphoreType.DMA
    scratch = {name: VMEM(array.shape, array.dtype) for name, array in loaded.items()}
    scratch.update(counts=pltpu.SMEM(band_rows.shape, band_rows.dtype))
    scratch.update(
        wide=VMEM((8, 256), F32),
        unit=VMEM((16, 128), BF16),
        units=VMEM((rings, 16, 128), BF16),
        blocks=VMEM((groups, CORES, planes, 16, columns // groups), BF16),
        packed=VMEM((2, 48, features), BF16),
        side=VMEM((2, 48, features), BF16),
        row_tok=VMEM((half, features), BF16),
        row_cot=VMEM((half, features), BF16),
        relay=VMEM((2 * TILE, features), BF16),
        corner=VMEM((TILE, features), BF16),
        relay_back=VMEM((TILE, features), BF16),
        corner_back=VMEM((TILE, features), BF16),
        weight=VMEM((groups, features, columns // groups), BF16),
        hidden=VMEM((total, features), BF16),
        turned_hidden=VMEM((features, total), BF16),
        normed=VMEM((total, features), F32),
        spread=VMEM((total, features), F32),
        hidden_grad=VMEM((total, features), F32),
        out_grad=VMEM((total, features), BF16),
        qkv=VMEM((groups, total, columns // groups), BF16),
        qkv_grad=VMEM((groups, total, columns // groups), BF16),
        part=VMEM((groups, CORES, planes, 16, columns // groups), BF16),
        from_core=VMEM((groups, planes, 16, columns // groups), BF16),
        sums=VMEM((groups, planes, 16, columns // groups), BF16),
        from_plane=VMEM((groups, planes, 16, columns // groups), BF16),
        total=VMEM((groups, 16, columns // groups), F32),
        back=VMEM(give.shape[:1] + (features,), BF16),
        row_back=VMEM((half, features), BF16),
        side_back=VMEM((2, 32, features), BF16),
        part_units=VMEM((rings, 16, 128), BF16),
        from_ring=VMEM((rings, 16, 128), BF16),
        load_sem=dma((len(loaded),)),
        relay_sem=dma((2,)),
        corner_sem=dma((2,)),
        relay_back_sem=dma((2,)),
        corner_back_sem=dma((2,)),
    )
    both = dict(
        ring=(1,), plane=(groups,), core=(groups,), halo=(2,), out=(2,),
        corner=(1,), back=(1,), corner_back=(1,), core_part=(groups,), plane_part=(groups,), ring_part=(1,),
    )
    for name, shape in both.items():
        scratch[name + "_send"] = dma(shape)
        scratch[name + "_recv"] = dma(shape)
    returned, weight_gradient = pl.pallas_call(
        functools.partial(kernel, lats, lons, len(loaded), list(scratch)),
        out_shape=(
            jax.ShapeDtypeStruct(tok.shape, BF16),
            jax.ShapeDtypeStruct(qkv_weight.shape, F32),
        ),
        in_specs=[pl.BlockSpec(memory_space=pl.ANY)] * len(loaded),
        out_specs=[pl.BlockSpec(memory_space=VMEM)] * 2,
        scratch_shapes=list(scratch.values()),
        compiler_params=pltpu.CompilerParams(
            collective_id=0, has_side_effects=True, vmem_limit_bytes=56 * 2**20
        ),
        name="sub_block",
    )(*loaded.values())
    token_grad = cotangent.astype(F32) + returned.reshape(tokens.shape).astype(F32)
    return token_grad.astype(BF16), weight_gradient


def solution(mesh):
    return jax.shard_map(
        functools.partial(on_device, mesh.shape["lat"], mesh.shape["lon"]),
        mesh=mesh,
        in_specs=(P("lat", "lon", None), P("lat", "lon", None), P("lat", "lon"), P()),
        out_specs=(P("lat", "lon", None), P("lat", "lon")),
        check_vma=False,
    )
```

```python
import functools
import types

import jax
import jax.numpy as jnp
import numpy as np
from jax import lax
from jax.experimental import pallas as pl
from jax.experimental.pallas import tpu as pltpu
from jax.sharding import PartitionSpec as P

MESH = pl.DeviceIdType.MESH
VMEM = pltpu.VMEM
BF16 = jnp.bfloat16
F32 = jnp.float32

WIN_ROWS = 6
WIN_COLS = 12
SHIFT_ROWS = 3
SHIFT_COLS = 6
HEAD_DIM = 32
EPSILON = 1e-05

Z_HI, Y, X, CORES = 2, 4, 4, 2


class Place:
    def __init__(self, lats, lons):
        self.lats, self.lons = lats, lons
        self.planes = Y * X
        self.rings = Z_HI * lons
        self.lat = lax.axis_index("lat")
        self.lon = lax.axis_index("lon")
        self.z_hi = lax.div(self.lat, self.planes * CORES)
        self.p = lax.div(lax.rem(self.lat, self.planes * CORES), CORES)
        self.core = lax.rem(self.lat, CORES)
        self.z = self.z_hi * lons + self.lon
        self.ring = [None] + [self._ring(k) for k in range(1, self.rings)]
        self.plane = [None] + [self._plane(k) for k in range(1, self.planes)]

    def _ring(self, k):
        z = lax.rem(self.z + k, self.rings)
        lat = lax.div(z, self.lons) * self.planes * CORES + self.p * CORES + self.core
        return z, (lat, lax.rem(z, self.lons))

    def _plane(self, k):
        x = lax.rem(lax.rem(self.p, X) + k % X, X)
        y = lax.rem(lax.div(self.p, X) + k // X, Y)
        p = y * X + x
        return p, (self.z_hi * self.planes * CORES + p * CORES + self.core, self.lon)

    def partner(self):
        return (self.lat + 1 - 2 * self.core, self.lon)

    def east(self):
        return lax.rem(self.lon + 1, self.lons)

    def west(self):
        return lax.rem(self.lon + self.lons - 1, self.lons)


def remote(src, dst, send, recv, device):
    return pltpu.make_async_remote_copy(
        src_ref=src, dst_ref=dst, send_sem=send, recv_sem=recv, device_id=device, device_id_type=MESH
    )


OUT_ROWS = (
    (0, Y - 1), (X - 1, 0), (0, 0), (1, 0), (0, 1), (X - 2, 0), (0, Y - 2), (1, Y - 1), (X - 1, 1),
)
OUT_CORNER = ((X - 2, Y - 1), (X - 1, Y - 2), (1, 1))
BACK_ROWS = (
    (X - 1, 0), (0, Y - 1), (X - 1, Y - 1), (X - 2, Y - 1), (X - 1, Y - 2), (1, Y - 1), (X - 1, 1), (X - 2, 0),
    (0, Y - 2),
)
BACK_CORNER = ((1, 0), (X - 2, Y - 2))
TILE = 16

PAD = 80
GROUP = 4


class Relays:
    def __init__(self, place):
        self.last_low = place.planes * CORES - 1
        self.first_high = place.planes * CORES
        self.low_end = place.lat == self.last_low
        self.high_end = place.lat == self.first_high

        def low(columns):
            return [(y * X + x) * CORES + CORES - 1 for x, y in columns]

        def high(columns):
            return [self.first_high + (y * X + x) * CORES for x, y in columns]

        self.out_rows, self.out_corner = low(OUT_ROWS), low(OUT_CORNER)
        self.back_rows, self.back_corner = high(BACK_ROWS), high(BACK_CORNER)


def far_first(count):
    return sorted(range(1, count), key=lambda k: -min(k, count - k))


def announce(place, relays):
    barrier = pltpu.get_barrier_semaphore()

    def signal(device):
        pl.semaphore_signal(barrier, inc=1, device_id=device, device_id_type=MESH)

    count = place.rings + place.planes - 1

    for ends, groups in (
        (relays.high_end, ((relays.out_rows, place.lon), (relays.out_corner, place.west()))),
        (relays.low_end, ((relays.back_rows, place.lon), (relays.back_corner, place.east()))),
    ):
        for lats, lon in groups:
            @pl.when(ends)
            def _():
                for lat in lats:
                    signal((lat, lon))

            for lat in lats:
                count = count + jnp.where(place.lat == lat, 1, 0)

    above = jnp.logical_and(place.lat > 0, jnp.logical_not(relays.high_end))
    below = jnp.logical_and(place.lat < place.lats - 1, jnp.logical_not(relays.low_end))

    @pl.when(above)
    def _():
        signal((place.lat - 1, place.lon))
        signal((place.lat - 1, place.west()))

    @pl.when(below)
    def _():
        signal((place.lat + 1, place.lon))
        signal((place.lat + 1, place.east()))

    count = count + jnp.where(above, 2, 0) + jnp.where(below, 2, 0)

    for k in far_first(place.rings):
        signal(place.ring[k][1])

    for k in range(1, place.planes):
        signal(place.plane[k][1])

    signal(place.partner())
    return count


def contract(left, right, dims):
    return lax.dot_general(left, right, (dims, ((), ())), preferred_element_type=F32)


def kernel(lats, lons, loaded, names, *refs):
    sources, returned, weight_gradient = refs[:loaded], refs[loaded], refs[loaded + 1]
    refs = refs[loaded + 2 :]
    targets = refs[:loaded]
    r = types.SimpleNamespace(**dict(zip(names, refs)))
    place = Place(lats, lons)
    relays = Relays(place)
    tok, cot = r.tok, r.cot
    half_rows = tok.shape[0] // 2
    features = tok.shape[1]
    width = GROUP * HEAD_DIM
    groups = features // width
    planes, rings = place.planes, place.rings
    lane_of = lax.broadcasted_iota(jnp.int32, (8, 128), 1)
    not_first = place.lat > 0
    not_last = place.lat < lats - 1

    loads = [
        pltpu.make_async_copy(source, target, r.load_sem.at[i])
        for i, (source, target) in enumerate(zip(sources, targets))
    ]
    for load in loads:
        load.start()

    expected = announce(place, relays)

    wide, unit, units = r.wide, r.unit, r.units
    wide[...] = jnp.zeros_like(wide)
    loads[0].wait()
    wide[:, 0 : r.w_in.shape[1]] = r.w_in[...].astype(F32)
    unit[...] = jnp.concatenate([wide[:, 0:128], wide[:, 128:256]], axis=0).astype(BF16)
    units[place.z] = unit[...]
    for load in loads[1:]:
        load.wait()

    packed, side, sel = r.packed, r.side, r.sel
    for part_of in range(2):
        rows = pl.ds(part_of * half_rows, half_rows)
        packed[part_of] = (
            jnp.dot(sel[0], tok[rows], preferred_element_type=F32)
            + jnp.dot(sel[1], cot[rows], preferred_element_type=F32)
        ).astype(BF16)

    @pl.when(jnp.logical_not(not_first))
    def _():
        side[1] = jnp.zeros(side.shape[1:], BF16)
        r.row_tok[...] = jnp.zeros_like(r.row_tok)
        r.row_cot[...] = jnp.zeros_like(r.row_cot)

    @pl.when(jnp.logical_not(not_last))
    def _():
        r.row_back[...] = jnp.zeros_like(r.row_back)
        r.side_back[1] = jnp.zeros(r.side_back.shape[1:], BF16)

    pl.semaphore_wait(pltpu.get_barrier_semaphore(), expected)

    def ring_copy(k):
        return remote(
            unit, units.at[place.z], r.ring_send.at[0], r.ring_recv.at[0], place.ring[k][1]
        )

    others = pl.ds(0, rings - 1)
    ring_all = remote(units.at[others], units.at[others], r.ring_send.at[0], r.ring_recv.at[0], place.partner())

    def send_ring():
        for k in far_first(rings):
            ring_copy(k).start()

    halo_send, halo_recv = r.halo_send, r.halo_recv
    side_copy = remote(packed.at[0], side.at[0], halo_send.at[0], halo_recv.at[0], (place.lat, place.east()))

    class Crossing:
        def __init__(self, sources, landings, lats, end, sends, receives, target, far, send, recv, relay, relay_sem):
            self.lats, self.end, self.sends, self.receives = lats, end, sends, receives
            self.direct, self.via, self.onward = [], [[] for _ in lats], [[] for _ in lats]
            for j, (source, landing) in enumerate(zip(sources, landings)):
                self.direct.append(remote(source, landing, send.at[j], recv.at[j], target))
                passing = relay.at[pl.ds(j * TILE, TILE)]
                for i, lat in enumerate(lats):
                    rows = pl.ds(i * TILE, TILE)
                    self.via[i].append(
                        remote(source.at[rows], passing, send.at[j], relay_sem.at[0], (lat, place.lon))
                    )
                    self.onward[i].append(
                        remote(passing, landing.at[rows], relay_sem.at[1], recv.at[j], far)
                    )
            self.passing = remote(relay, relay, relay_sem.at[1], relay_sem.at[0], place.partner())

        def start_relayed(self):
            @pl.when(self.end)
            def _():
                for copies in self.via:
                    for copy in copies:
                        copy.start()

        def start(self):
            @pl.when(jnp.logical_and(self.sends, jnp.logical_not(self.end)))
            def _():
                for copy in self.direct:
                    copy.start()

        def pass_on(self):
            is_relay = functools.reduce(jnp.logical_or, [place.lat == lat for lat in self.lats])

            @pl.when(is_relay)
            def _():
                self.passing.wait_recv()

            for lat, copies in zip(self.lats, self.onward):
                @pl.when(place.lat == lat)
                def _():
                    for copy in copies:
                        copy.start()

        def wait_recv(self):
            @pl.when(self.receives)
            def _():
                for copy in self.direct:
                    copy.wait_recv()

        def wait_send(self):
            @pl.when(self.sends)
            def _():
                for copy in self.direct:
                    copy.wait_send()

            is_relay = functools.reduce(jnp.logical_or, [place.lat == lat for lat in self.lats])

            @pl.when(is_relay)
            def _():
                self.passing.wait_send()

    back, side_back = r.back, r.side_back
    last_rows = pl.ds(half_rows, half_rows)
    rows_out = Crossing(
        [tok.at[last_rows], cot.at[last_rows]], [r.row_tok, r.row_cot], relays.out_rows, relays.low_end,
        not_last, not_first, (place.lat + 1, place.lon), (relays.first_high, place.lon),
        r.out_send, r.out_recv, r.relay, r.relay_sem,
    )
    corner_out = Crossing(
        [packed.at[1]], [side.at[1]], relays.out_corner, relays.low_end,
        not_last, not_first, (place.lat + 1, place.east()), (relays.first_high, place.east()),
        r.corner_send, r.corner_recv, r.corner, r.corner_sem,
    )
    rows_back = Crossing(
        [back.at[last_rows]], [r.row_back], relays.back_rows, relays.high_end,
        not_first, not_last, (place.lat - 1, place.lon), (relays.last_low, place.lon),
        r.back_send, r.back_recv, r.relay_back, r.relay_back_sem,
    )
    corner_back = Crossing(
        [back.at[pl.ds(2 * half_rows + 32, 32)]], [side_back.at[1]], relays.back_corner, relays.high_end,
        not_first, not_last, (place.lat - 1, place.west()), (relays.last_low, place.west()),
        r.corner_back_send, r.corner_back_recv, r.corner_back, r.corner_back_sem,
    )
    side_return = remote(
        back.at[pl.ds(2 * half_rows, 32)], side_back.at[0], halo_send.at[1], halo_recv.at[1],
        (place.lat, place.west()),
    )

    def send_relayed():
        rows_out.start_relayed()
        corner_out.start_relayed()

    def send_halos():
        rows_out.start()
        corner_out.start()
        side_copy.start()

    def pass_on():
        rows_out.pass_on()
        corner_out.pass_on()

    blocks = r.blocks

    def tile_at(n):
        which, group = divmod(n, groups)
        return group, pl.ds(which * width, width)

    def join_ring():
        ring_all.wait_recv()

        for pair in range(lons // 2):
            tiles = [[], [], []]
            for z_hi in range(Z_HI):
                even = units[z_hi * lons + 2 * pair].astype(F32)
                odd = units[z_hi * lons + 2 * pair + 1].astype(F32)
                turned_top = pltpu.roll(odd[0:8], 64, 1)
                turned_low = pltpu.roll(odd[8:16], 64, 1)
                tiles[0].append(even[0:8])
                tiles[1].append(jnp.where(lane_of < 64, even[8:16], turned_top))
                tiles[2].append(jnp.where(lane_of < 64, turned_top, turned_low))
            for j in range(3):
                group, lanes = tile_at(pair * 3 + j)
                blocks[group, place.core, place.p, :, lanes] = jnp.concatenate(tiles[j], axis=0).astype(BF16)

    def plane_copy(group, k):
        own = blocks.at[group, place.core, place.p]
        return remote(
            own, own, r.plane_send.at[group], r.plane_recv.at[group], place.plane[k][1]
        )

    def plane_all(group):
        others = blocks.at[group, place.core, pl.ds(0, planes - 1)]
        return remote(others, others, r.plane_send.at[group], r.plane_recv.at[group], place.partner())

    def core_copy(group):
        block = blocks.at[group, place.core]
        return remote(block, block, r.core_send.at[group], r.core_recv.at[group], place.partner())

    def core_arrival(group):
        block = blocks.at[group, 1 - place.core]
        return remote(block, block, r.core_send.at[group], r.core_recv.at[group], place.partner())

    def send_blocks(group):
        for k in range(1, planes):
            plane_copy(group, k).start()

    own_count = r.counts[place.lat]
    previous = jnp.where(not_first, r.counts[jnp.maximum(place.lat - 1, 0)], 0)
    row_of = r.row_of[...]
    limit = jnp.where(row_of < SHIFT_ROWS, previous - SHIFT_ROWS, own_count + SHIFT_ROWS)
    valid = jnp.where(row_of < jnp.minimum(limit, WIN_ROWS), 1.0, 0.0)
    take_own, take_row, take_side = r.take_own, r.take_row, r.take_side

    def framed_of(own, row, first):
        return (
            jnp.dot(take_own[...], own[...], preferred_element_type=F32)
            + jnp.dot(take_row[...], row[...], preferred_element_type=F32)
            + jnp.dot(take_side[first], side[0], preferred_element_type=F32)
            + jnp.dot(take_side[first + 1], side[1], preferred_element_type=F32)
        )

    hidden, normed, spread, out_grad = r.hidden, r.normed, r.spread, r.out_grad
    def frame():
        rows_out.wait_recv()
        corner_out.wait_recv()
        side_copy.wait_recv()

        framed = framed_of(tok, r.row_tok, 0)
        center = framed - jnp.mean(framed, axis=-1, keepdims=True)
        inverse = lax.rsqrt(jnp.mean(center * center, axis=-1, keepdims=True) + EPSILON)
        normal = center * inverse
        normed[...] = normal
        spread[...] = jnp.broadcast_to(inverse, spread.shape)
        hidden[...] = normal.astype(BF16)
        r.turned_hidden[...] = normal.astype(BF16).T
        framed = framed_of(cot, r.row_cot, 2)
        for j in range(features // 128):
            lanes = slice(j * 128, j * 128 + 128)
            out_grad[:, lanes] = jnp.where(valid > 0.0, framed[:, lanes], 0.0).astype(BF16)

    weight, qkv, qkv_grad = r.weight, r.qkv, r.qkv_grad

    def forward_arrivals(group):
        plane_all(group).wait_recv()
        core_copy(group).start()

    def collect(group):
        core_arrival(group).wait_recv()
        for p in range(planes):
            first = blocks[group, 0, p].astype(F32)
            second = blocks[group, 1, p].astype(F32)
            for z_hi in range(Z_HI):
                take = slice(z_hi * 8, z_hi * 8 + 8)
                rows = pl.ds((z_hi * planes + p) * 16, 16)
                weight[group, rows, :] = jnp.concatenate([first[take], second[take]], axis=0).astype(BF16)

    factor = HEAD_DIM ** (-0.5)
    whole, rest = divmod(GROUP * PAD, 128)
    allowed = jnp.concatenate([valid[0:PAD]] * whole + [valid[0:PAD, 0:rest]], axis=1) > 0.0
    mask = r.head_mask[...]
    windows = hidden.shape[0] // PAD

    def project(group):
        qkv[group] = jnp.dot(hidden[...], weight[group], preferred_element_type=F32).astype(BF16)

    def attend(group):
        for window in range(windows):
            at = slice(window * PAD, window * PAD + PAD)
            lanes = [slice(j * width, (j + 1) * width) for j in range(3)]
            query, keyed, valued = (qkv[group, at, lane] for lane in lanes)
            grad = out_grad[at, group * width : (group + 1) * width]
            query = jnp.concatenate([query] * GROUP, axis=0) * mask
            grad = jnp.concatenate([grad] * GROUP, axis=0) * mask
            scores = contract(keyed, query, ((1,), (1,))) * factor
            scores = jnp.where(allowed, scores, -1000000000.0)
            exponent = jnp.exp(scores - jnp.max(scores, axis=0, keepdims=True))
            probs = exponent * (1.0 / jnp.sum(exponent, axis=0, keepdims=True))
            weight_grad = contract(valued, grad, ((1,), (1,)))
            mixed = jnp.sum(probs * weight_grad, axis=0, keepdims=True)
            score_grad = (probs * (weight_grad - mixed) * factor).astype(BF16)
            value_grad = jnp.dot(probs.astype(BF16), grad, preferred_element_type=F32)
            key_grad = jnp.dot(score_grad, query, preferred_element_type=F32)
            turned = contract(score_grad, keyed, ((0,), (0,)))
            query_grad = turned[0:PAD] * mask[0:PAD].astype(F32)
            for h in range(1, GROUP):
                rows_h = slice(h * PAD, h * PAD + PAD)
                query_grad = query_grad + turned[rows_h] * mask[rows_h].astype(F32)
            for lane, value in zip(lanes, (query_grad, key_grad, value_grad)):
                qkv_grad[group, at, lane] = value.astype(BF16)

    part = r.part

    def weigh(group):
        for j in range(3):
            lanes = slice(j * width, (j + 1) * width)
            piece = jnp.dot(r.turned_hidden[...], qkv_grad[group, :, lanes], preferred_element_type=F32)
            for core in range(CORES):
                for p in range(planes):
                    first = (p * CORES + core) * 8
                    both = [piece[z * planes * CORES * 8 + first :][0:8] for z in range(Z_HI)]
                    part[group, core, p, :, lanes] = jnp.concatenate(both, axis=0).astype(BF16)

    from_core, sums, from_plane, total = r.from_core, r.sums, r.from_plane, r.total

    def core_part(group):
        return remote(
            part.at[group, 1 - place.core], from_core.at[group],
            r.core_part_send.at[group], r.core_part_recv.at[group], place.partner(),
        )

    def plane_part(group, k):
        p, device = place.plane[k]
        return remote(
            sums.at[group, p], from_plane.at[group, place.p],
            r.plane_part_send.at[group], r.plane_part_recv.at[group], device,
        )

    def plane_part_all(group):
        others = pl.ds(0, planes - 1)
        return remote(
            sums.at[group, others], from_plane.at[group, others],
            r.plane_part_send.at[group], r.plane_part_recv.at[group], place.partner(),
        )

    def send_core(group):
        core_part(group).start()

    def send_plane(group):
        core_part(group).wait_recv()
        sums[group] = (part[group, place.core].astype(F32) + from_core[group].astype(F32)).astype(BF16)

        for k in range(1, planes):
            plane_part(group, k).start()

        from_plane[group, place.p] = sums[group, place.p]

    def add_plane(group):
        plane_part_all(group).wait_recv()
        total[group] = jnp.sum(from_plane[group].astype(F32), axis=0)

    def accumulate(group):
        term = contract(qkv_grad[group], weight[group], ((1,), (1,)))
        if group == 0:
            r.hidden_grad[...] = term
        else:
            r.hidden_grad[...] += term

    def differentiate():
        hidden_grad = r.hidden_grad[...]
        normal = normed[...]
        mean_grad = jnp.mean(hidden_grad, axis=-1, keepdims=True)
        mean_mixed = jnp.mean(hidden_grad * normal, axis=-1, keepdims=True)
        frame_grad = spread[...] * (hidden_grad - mean_grad - normal * mean_mixed)
        back[...] = jnp.dot(r.give[...], frame_grad.astype(BF16), preferred_element_type=F32).astype(BF16)

    def return_relayed():
        rows_back.start_relayed()
        corner_back.start_relayed()

    def return_halos():
        rows_back.start()
        corner_back.start()
        side_return.start()

    def pass_back():
        rows_back.pass_on()
        corner_back.pass_on()

    part_units, from_ring = r.part_units, r.from_ring

    def ring_part(k):
        z, device = place.ring[k]
        return remote(
            part_units.at[z], from_ring.at[place.z], r.ring_part_send.at[0], r.ring_part_recv.at[0], device
        )

    ring_part_all = remote(
        part_units.at[others], from_ring.at[others], r.ring_part_send.at[0], r.ring_part_recv.at[0],
        place.partner(),
    )

    def send_ring_parts():
        for pair in range(lons // 2):
            for z_hi in range(Z_HI):
                tiles = []
                for j in range(3):
                    group, lanes = tile_at(pair * 3 + j)
                    tiles.append(total[group, pl.ds(z_hi * 8, 8), lanes])
                turned = [pltpu.roll(tile, 64, 1) for tile in tiles]
                part_units[z_hi * lons + 2 * pair] = jnp.concatenate([tiles[0], tiles[1]], axis=0).astype(BF16)
                part_units[z_hi * lons + 2 * pair + 1] = jnp.concatenate(
                    [jnp.where(lane_of < 64, turned[1], turned[2]), turned[2]], axis=0
                ).astype(BF16)

        for k in far_first(rings):
            ring_part(k).start()

        from_ring[place.z] = part_units[place.z]

    returned_copy = pltpu.make_async_copy(r.returned, returned, r.store_sem.at[0])
    weight_copy = pltpu.make_async_copy(r.weight_gradient, weight_gradient, r.store_sem.at[1])

    def finish_tokens():
        rows_back.wait_recv()
        corner_back.wait_recv()
        side_return.wait_recv()

        for part_of in range(2):
            rows = pl.ds(part_of * half_rows, half_rows)
            inner = back[0:half_rows] if part_of == 0 else r.row_back[...]
            outer = jnp.dot(r.place_sel[...], side_back[part_of], preferred_element_type=F32)
            r.returned[rows] = (inner.astype(F32) + outer).astype(BF16)
        returned_copy.start()

    def finish_weight():
        ring_part_all.wait_recv()

        result = from_ring[0].astype(F32)
        for z in range(1, rings):
            result = result + from_ring[z].astype(F32)
        r.weight_gradient[:, 0:128] = result[0:8]
        r.weight_gradient[:, 128:192] = result[8:16, 0:64]
        weight_copy.start()

    def drain():
        returned_copy.wait()
        weight_copy.wait()
        rows_out.wait_send()
        rows_back.wait_send()
        corner_out.wait_send()
        corner_back.wait_send()
        side_copy.wait_send()
        side_return.wait_send()
        ring_all.wait_send()
        ring_part_all.wait_send()
        for group in range(groups):
            plane_all(group).wait_send()
            plane_part_all(group).wait_send()
            core_copy(group).wait_send()
            core_part(group).wait_send()

    send_relayed()
    send_ring()
    send_halos()
    pass_on()
    join_ring()
    for group in range(groups):
        send_blocks(group)
    forward_arrivals(0)
    forward_arrivals(1)
    frame()
    for group in range(groups):
        collect(group)
        project(group)
        attend(group)
        if group > 0:
            send_plane(group - 1)
        if group < groups - 2:
            forward_arrivals(group + 2)
        weigh(group)
        send_core(group)
        accumulate(group)
    differentiate()
    return_relayed()
    send_plane(groups - 1)
    return_halos()
    for group in range(groups - 1):
        add_plane(group)
    pass_back()
    add_plane(groups - 1)
    send_ring_parts()
    finish_tokens()
    finish_weight()
    drain()


def finish_kernel(returned, cot, weight, token_grad, weight_gradient, first, second, total, load_sem, store_sem):
    parts = first.shape[0]
    rows = first.shape[1]
    weight_copy = pltpu.make_async_copy(weight, weight_gradient, store_sem.at[parts])
    weight_copy.start()
    loads, stores = [], []
    for i in range(parts):
        at = pl.ds(i * rows, rows)
        loads.append(
            (
                pltpu.make_async_copy(returned.at[at], first.at[i], load_sem.at[i, 0]),
                pltpu.make_async_copy(cot.at[at], second.at[i], load_sem.at[i, 1]),
            )
        )
        stores.append(pltpu.make_async_copy(total.at[i], token_grad.at[at], store_sem.at[i]))
    for pair in loads:
        for load in pair:
            load.start()
    for i in range(parts):
        for load in loads[i]:
            load.wait()
        total[i] = (second[i].astype(F32) + first[i].astype(F32)).astype(BF16)
        stores[i].start()
    for store in stores:
        store.wait()
    weight_copy.wait()


def finish(returned, cot, weight):
    parts = 3
    block = VMEM((parts, cot.shape[0] // parts, cot.shape[1]), BF16)
    return pl.pallas_call(
        finish_kernel,
        out_shape=(
            jax.ShapeDtypeStruct(cot.shape, BF16),
            jax.ShapeDtypeStruct(weight.shape, F32),
        ),
        in_specs=[pl.BlockSpec(memory_space=pl.ANY)] * 3,
        out_specs=[pl.BlockSpec(memory_space=pl.ANY)] * 2,
        scratch_shapes=[
            block, block, block, pltpu.SemaphoreType.DMA((parts, 2)), pltpu.SemaphoreType.DMA((parts + 1,)),
        ],
        compiler_params=pltpu.CompilerParams(vmem_limit_bytes=56 * 2**20),
        name="finish",
    )(returned, cot, weight)


def frame_tables(cols):
    windows = cols // WIN_COLS
    total = windows * PAD
    half = SHIFT_ROWS * cols
    own = np.zeros((total, 2 * half), np.float32)
    row = np.zeros((total, half), np.float32)
    side = np.zeros((4, total, 48), np.float32)
    give = np.zeros((2 * half + 64, total), np.float32)
    row_of = np.full((total, 128), WIN_ROWS, np.int32)
    for window in range(windows):
        for r in range(WIN_ROWS):
            for c in range(WIN_COLS):
                t = window * PAD + r * WIN_COLS + c
                row_of[t] = r
                rr, g = r - SHIFT_ROWS, window * WIN_COLS + c - SHIFT_COLS
                upper = rr < 0
                if g >= 0:
                    if upper:
                        row[t, r * cols + g] = 1
                        give[half + r * cols + g, t] = 1
                    else:
                        own[t, rr * cols + g] = 1
                        give[rr * cols + g, t] = 1
                else:
                    at = (r % SHIFT_ROWS) * SHIFT_COLS + g + SHIFT_COLS
                    side[int(upper), t, at] = 1
                    side[2 + int(upper), t, 18 + at] = 1
                    give[2 * half + 32 * int(upper) + at, t] = 1
    return own, row, side, give, row_of


def on_device(lats, lons, tokens, cotangent, qkv_weight, band_rows):
    features = tokens.shape[-1]
    tok = tokens.reshape(-1, features)
    cot = cotangent.reshape(-1, features)
    count = tok.shape[0]
    half = count // 2
    cols = half // SHIFT_ROWS
    planes, rings = Y * X, Z_HI * lons
    columns = qkv_weight.shape[1] * lons
    width = GROUP * HEAD_DIM
    groups = features // width
    take_own, take_row, take_side, give, row_of = frame_tables(cols)
    total = take_own.shape[0]
    sel = np.zeros((2, 48, half), np.float32)
    place_sel = np.zeros((half, 32), np.float32)
    for row in range(SHIFT_ROWS):
        for col in range(SHIFT_COLS):
            at, edge = row * SHIFT_COLS + col, row * cols + cols - SHIFT_COLS + col
            sel[0, at, edge] = 1
            sel[1, 18 + at, edge] = 1
            place_sel[edge, at] = 1
    head_mask = np.zeros((GROUP, PAD, GROUP, HEAD_DIM), np.float32)
    for h in range(GROUP):
        head_mask[h, :, h] = 1
    low = lambda table: jnp.asarray(table, BF16)
    loaded = dict(
        w_in=qkv_weight, counts=band_rows, tok=tok, cot=cot, sel=low(sel), row_of=jnp.asarray(row_of), take_own=low(take_own), take_row=low(take_row),
        take_side=low(take_side), head_mask=low(head_mask.reshape(GROUP * PAD, width)), give=low(give),
        place_sel=low(place_sel),
    )
    dma = pltpu.SemaphoreType.DMA
    scratch = {name: VMEM(array.shape, array.dtype) for name, array in loaded.items()}
    scratch.update(counts=pltpu.SMEM(band_rows.shape, band_rows.dtype))
    scratch.update(
        wide=VMEM((8, 256), F32),
        unit=VMEM((16, 128), BF16),
        units=VMEM((rings, 16, 128), BF16),
        blocks=VMEM((groups, CORES, planes, 16, columns // groups), BF16),
        packed=VMEM((2, 48, features), BF16),
        side=VMEM((2, 48, features), BF16),
        row_tok=VMEM((half, features), BF16),
        row_cot=VMEM((half, features), BF16),
        relay=VMEM((2 * TILE, features), BF16),
        corner=VMEM((TILE, features), BF16),
        relay_back=VMEM((TILE, features), BF16),
        corner_back=VMEM((TILE, features), BF16),
        weight=VMEM((groups, features, columns // groups), BF16),
        hidden=VMEM((total, features), BF16),
        turned_hidden=VMEM((features, total), BF16),
        normed=VMEM((total, features), F32),
        spread=VMEM((total, features), F32),
        hidden_grad=VMEM((total, features), F32),
        out_grad=VMEM((total, features), BF16),
        qkv=VMEM((groups, total, columns // groups), BF16),
        qkv_grad=VMEM((groups, total, columns // groups), BF16),
        part=VMEM((groups, CORES, planes, 16, columns // groups), BF16),
        from_core=VMEM((groups, planes, 16, columns // groups), BF16),
        sums=VMEM((groups, planes, 16, columns // groups), BF16),
        from_plane=VMEM((groups, planes, 16, columns // groups), BF16),
        total=VMEM((groups, 16, columns // groups), F32),
        back=VMEM(give.shape[:1] + (features,), BF16),
        row_back=VMEM((half, features), BF16),
        side_back=VMEM((2, 32, features), BF16),
        part_units=VMEM((rings, 16, 128), BF16),
        from_ring=VMEM((rings, 16, 128), BF16),
        returned=VMEM(tok.shape, BF16),
        weight_gradient=VMEM(qkv_weight.shape, F32),
        load_sem=dma((len(loaded),)),
        store_sem=dma((2,)),
        relay_sem=dma((2,)),
        corner_sem=dma((2,)),
        relay_back_sem=dma((2,)),
        corner_back_sem=dma((2,)),
    )
    both = dict(
        ring=(1,), plane=(groups,), core=(groups,), halo=(2,), out=(2,),
        corner=(1,), back=(1,), corner_back=(1,), core_part=(groups,), plane_part=(groups,), ring_part=(1,),
    )
    for name, shape in both.items():
        scratch[name + "_send"] = dma(shape)
        scratch[name + "_recv"] = dma(shape)
    returned, weight_gradient = pl.pallas_call(
        functools.partial(kernel, lats, lons, len(loaded), list(scratch)),
        out_shape=(
            jax.ShapeDtypeStruct(tok.shape, BF16),
            jax.ShapeDtypeStruct(qkv_weight.shape, F32),
        ),
        in_specs=[pl.BlockSpec(memory_space=pl.ANY)] * len(loaded),
        out_specs=[pl.BlockSpec(memory_space=pl.ANY)] * 2,
        scratch_shapes=list(scratch.values()),
        compiler_params=pltpu.CompilerParams(
            collective_id=0, has_side_effects=True, vmem_limit_bytes=56 * 2**20
        ),
        name="sub_block",
    )(*loaded.values())
    token_grad, weight_gradient = finish(returned, cot, weight_gradient)
    return token_grad.reshape(tokens.shape), weight_gradient


def solution(mesh):
    return jax.shard_map(
        functools.partial(on_device, mesh.shape["lat"], mesh.shape["lon"]),
        mesh=mesh,
        in_specs=(P("lat", "lon", None), P("lat", "lon", None), P("lat", "lon"), P()),
        out_specs=(P("lat", "lon", None), P("lat", "lon")),
        check_vma=False,
    )
```

```python
import functools
import types

import jax
import jax.numpy as jnp
import numpy as np
from jax import lax
from jax.experimental import pallas as pl
from jax.experimental.pallas import tpu as pltpu
from jax.sharding import PartitionSpec as P

MESH = pl.DeviceIdType.MESH
VMEM = pltpu.VMEM
BF16 = jnp.bfloat16
F32 = jnp.float32

WIN_ROWS = 6
WIN_COLS = 12
SHIFT_ROWS = 3
SHIFT_COLS = 6
HEAD_DIM = 32
EPSILON = 1e-05
LOG2_E = 1.4426950408889634

Z_HI, Y, X, CORES = 2, 4, 4, 2


class Place:
    def __init__(self, lats, lons):
        self.lats, self.lons = lats, lons
        self.planes = Y * X
        self.rings = Z_HI * lons
        self.lat = lax.axis_index("lat")
        self.lon = lax.axis_index("lon")
        self.z_hi = lax.div(self.lat, self.planes * CORES)
        self.p = lax.div(lax.rem(self.lat, self.planes * CORES), CORES)
        self.core = lax.rem(self.lat, CORES)
        self.z = self.z_hi * lons + self.lon
        self.ring = [None] + [self._ring(k) for k in range(1, self.rings)]
        self.plane = [None] + [self._plane(k) for k in range(1, self.planes)]

    def _ring(self, k):
        z = lax.rem(self.z + k, self.rings)
        lat = lax.div(z, self.lons) * self.planes * CORES + self.p * CORES + self.core
        return z, (lat, lax.rem(z, self.lons))

    def _plane(self, k):
        x = lax.rem(lax.rem(self.p, X) + k % X, X)
        y = lax.rem(lax.div(self.p, X) + k // X, Y)
        p = y * X + x
        return p, (self.z_hi * self.planes * CORES + p * CORES + self.core, self.lon)

    def partner(self):
        return (self.lat + 1 - 2 * self.core, self.lon)

    def east(self):
        return lax.rem(self.lon + 1, self.lons)

    def west(self):
        return lax.rem(self.lon + self.lons - 1, self.lons)


def remote(src, dst, send, recv, device):
    return pltpu.make_async_remote_copy(
        src_ref=src, dst_ref=dst, send_sem=send, recv_sem=recv, device_id=device, device_id_type=MESH
    )


OUT_ROWS = (
    (0, Y - 1), (X - 1, 0), (0, 0), (1, 0), (0, 1), (X - 2, 0), (0, Y - 2), (1, Y - 1), (X - 1, 1),
)
OUT_CORNER = ((X - 2, Y - 1), (X - 1, Y - 2), (1, 1))
BACK_ROWS = (
    (X - 1, 0), (0, Y - 1), (X - 1, Y - 1), (X - 2, Y - 1), (X - 1, Y - 2), (1, Y - 1), (X - 1, 1), (X - 2, 0),
    (0, Y - 2),
)
BACK_CORNER = ((1, 0), (X - 2, Y - 2))
TILE = 16

PAD = 80
GROUP = 4


class Relays:
    def __init__(self, place):
        self.last_low = place.planes * CORES - 1
        self.first_high = place.planes * CORES
        self.low_end = place.lat == self.last_low
        self.high_end = place.lat == self.first_high

        def low(columns):
            return [(y * X + x) * CORES + CORES - 1 for x, y in columns]

        def high(columns):
            return [self.first_high + (y * X + x) * CORES for x, y in columns]

        self.out_rows, self.out_corner = low(OUT_ROWS), low(OUT_CORNER)
        self.back_rows, self.back_corner = high(BACK_ROWS), high(BACK_CORNER)


def far_first(count):
    return sorted(range(1, count), key=lambda k: -min(k, count - k))


def announce(place, relays):
    barrier = pltpu.get_barrier_semaphore()

    def signal(device):
        pl.semaphore_signal(barrier, inc=1, device_id=device, device_id_type=MESH)

    count = place.rings + place.planes - 1

    for ends, groups in (
        (relays.high_end, ((relays.out_rows, place.lon), (relays.out_corner, place.west()))),
        (relays.low_end, ((relays.back_rows, place.lon), (relays.back_corner, place.east()))),
    ):
        for lats, lon in groups:
            @pl.when(ends)
            def _():
                for lat in lats:
                    signal((lat, lon))

            for lat in lats:
                count = count + jnp.where(place.lat == lat, 1, 0)

    above = jnp.logical_and(place.lat > 0, jnp.logical_not(relays.high_end))
    below = jnp.logical_and(place.lat < place.lats - 1, jnp.logical_not(relays.low_end))

    @pl.when(above)
    def _():
        signal((place.lat - 1, place.lon))
        signal((place.lat - 1, place.west()))

    @pl.when(below)
    def _():
        signal((place.lat + 1, place.lon))
        signal((place.lat + 1, place.east()))

    count = count + jnp.where(above, 2, 0) + jnp.where(below, 2, 0)

    for k in far_first(place.rings):
        signal(place.ring[k][1])

    for k in range(1, place.planes):
        signal(place.plane[k][1])

    signal(place.partner())
    return count


def contract(left, right, dims):
    return lax.dot_general(left, right, (dims, ((), ())), preferred_element_type=F32)


def kernel(lats, lons, loaded, names, *refs):
    sources, returned, weight_gradient = refs[:loaded], refs[loaded], refs[loaded + 1]
    refs = refs[loaded + 2 :]
    targets = refs[:loaded]
    r = types.SimpleNamespace(**dict(zip(names, refs)))
    place = Place(lats, lons)
    relays = Relays(place)
    tok, cot = r.tok, r.cot
    half_rows = tok.shape[0] // 2
    features = tok.shape[1]
    width = GROUP * HEAD_DIM
    groups = features // width
    planes, rings = place.planes, place.rings
    lane_of = lax.broadcasted_iota(jnp.int32, (8, 128), 1)
    not_first = place.lat > 0
    not_last = place.lat < lats - 1

    loads = [
        pltpu.make_async_copy(source, target, r.load_sem.at[i])
        for i, (source, target) in enumerate(zip(sources, targets))
    ]
    expected = announce(place, relays)
    for load in loads:
        load.start()

    wide, unit, units = r.wide, r.unit, r.units
    wide[...] = jnp.zeros_like(wide)
    loads[0].wait()
    wide[:, 0 : r.w_in.shape[1]] = r.w_in[...].astype(F32)
    unit[...] = jnp.concatenate([wide[:, 0:128], wide[:, 128:256]], axis=0).astype(BF16)
    units[place.z] = unit[...]
    for load in loads[1:]:
        load.wait()

    packed, side, sel = r.packed, r.side, r.sel
    for part_of in range(2):
        rows = pl.ds(part_of * half_rows, half_rows)
        packed[part_of] = (
            jnp.dot(sel[0], tok[rows], preferred_element_type=F32)
            + jnp.dot(sel[1], cot[rows], preferred_element_type=F32)
        ).astype(BF16)

    @pl.when(jnp.logical_not(not_first))
    def _():
        side[1] = jnp.zeros(side.shape[1:], BF16)
        r.row_tok[...] = jnp.zeros_like(r.row_tok)
        r.row_cot[...] = jnp.zeros_like(r.row_cot)

    @pl.when(jnp.logical_not(not_last))
    def _():
        r.row_back[...] = jnp.zeros_like(r.row_back)
        r.side_back[1] = jnp.zeros(r.side_back.shape[1:], BF16)

    pl.semaphore_wait(pltpu.get_barrier_semaphore(), expected)

    def ring_copy(k):
        return remote(
            unit, units.at[place.z], r.ring_send.at[0], r.ring_recv.at[0], place.ring[k][1]
        )

    others = pl.ds(0, rings - 1)
    ring_all = remote(units.at[others], units.at[others], r.ring_send.at[0], r.ring_recv.at[0], place.partner())

    def send_ring():
        for k in far_first(rings):
            ring_copy(k).start()

    halo_send, halo_recv = r.halo_send, r.halo_recv
    side_copy = remote(packed.at[0], side.at[0], halo_send.at[0], halo_recv.at[0], (place.lat, place.east()))

    class Crossing:
        def __init__(self, sources, landings, lats, end, sends, receives, target, far, send, recv, relay, relay_sem):
            self.lats, self.end, self.sends, self.receives = lats, end, sends, receives
            self.direct, self.via, self.onward = [], [[] for _ in lats], [[] for _ in lats]
            for j, (source, landing) in enumerate(zip(sources, landings)):
                self.direct.append(remote(source, landing, send.at[j], recv.at[j], target))
                passing = relay.at[pl.ds(j * TILE, TILE)]
                for i, lat in enumerate(lats):
                    rows = pl.ds(i * TILE, TILE)
                    self.via[i].append(
                        remote(source.at[rows], passing, send.at[j], relay_sem.at[0], (lat, place.lon))
                    )
                    self.onward[i].append(
                        remote(passing, landing.at[rows], relay_sem.at[1], recv.at[j], far)
                    )
            self.passing = remote(relay, relay, relay_sem.at[1], relay_sem.at[0], place.partner())

        def start_relayed(self):
            @pl.when(self.end)
            def _():
                for copies in self.via:
                    for copy in copies:
                        copy.start()

        def start(self):
            @pl.when(jnp.logical_and(self.sends, jnp.logical_not(self.end)))
            def _():
                for copy in self.direct:
                    copy.start()

        def pass_on(self):
            is_relay = functools.reduce(jnp.logical_or, [place.lat == lat for lat in self.lats])

            @pl.when(is_relay)
            def _():
                self.passing.wait_recv()

            for lat, copies in zip(self.lats, self.onward):
                @pl.when(place.lat == lat)
                def _():
                    for copy in copies:
                        copy.start()

        def wait_recv(self):
            @pl.when(self.receives)
            def _():
                for copy in self.direct:
                    copy.wait_recv()

        def wait_send(self):
            @pl.when(self.sends)
            def _():
                for copy in self.direct:
                    copy.wait_send()

            is_relay = functools.reduce(jnp.logical_or, [place.lat == lat for lat in self.lats])

            @pl.when(is_relay)
            def _():
                self.passing.wait_send()

    back, side_back = r.back, r.side_back
    last_rows = pl.ds(half_rows, half_rows)
    rows_out = Crossing(
        [tok.at[last_rows], cot.at[last_rows]], [r.row_tok, r.row_cot], relays.out_rows, relays.low_end,
        not_last, not_first, (place.lat + 1, place.lon), (relays.first_high, place.lon),
        r.out_send, r.out_recv, r.relay, r.relay_sem,
    )
    corner_out = Crossing(
        [packed.at[1]], [side.at[1]], relays.out_corner, relays.low_end,
        not_last, not_first, (place.lat + 1, place.east()), (relays.first_high, place.east()),
        r.corner_send, r.corner_recv, r.corner, r.corner_sem,
    )
    rows_back = Crossing(
        [back.at[last_rows]], [r.row_back], relays.back_rows, relays.high_end,
        not_first, not_last, (place.lat - 1, place.lon), (relays.last_low, place.lon),
        r.back_send, r.back_recv, r.relay_back, r.relay_back_sem,
    )
    corner_back = Crossing(
        [back.at[pl.ds(2 * half_rows + 32, 32)]], [side_back.at[1]], relays.back_corner, relays.high_end,
        not_first, not_last, (place.lat - 1, place.west()), (relays.last_low, place.west()),
        r.corner_back_send, r.corner_back_recv, r.corner_back, r.corner_back_sem,
    )
    side_return = remote(
        back.at[pl.ds(2 * half_rows, 32)], side_back.at[0], halo_send.at[1], halo_recv.at[1],
        (place.lat, place.west()),
    )

    def send_relayed():
        rows_out.start_relayed()
        corner_out.start_relayed()

    def send_halos():
        rows_out.start()
        corner_out.start()
        side_copy.start()

    def pass_on():
        rows_out.pass_on()
        corner_out.pass_on()

    blocks = r.blocks

    def tile_at(n):
        which, group = divmod(n, groups)
        return group, pl.ds(which * width, width)

    def join_ring():
        ring_all.wait_recv()

        for pair in range(lons // 2):
            tiles = [[], [], []]
            for z_hi in range(Z_HI):
                even = units[z_hi * lons + 2 * pair].astype(F32)
                odd = units[z_hi * lons + 2 * pair + 1].astype(F32)
                turned_top = pltpu.roll(odd[0:8], 64, 1)
                turned_low = pltpu.roll(odd[8:16], 64, 1)
                tiles[0].append(even[0:8])
                tiles[1].append(jnp.where(lane_of < 64, even[8:16], turned_top))
                tiles[2].append(jnp.where(lane_of < 64, turned_top, turned_low))
            for j in range(3):
                group, lanes = tile_at(pair * 3 + j)
                blocks[group, place.core, place.p, :, lanes] = jnp.concatenate(tiles[j], axis=0).astype(BF16)

    def plane_copy(group, k):
        own = blocks.at[group, place.core, place.p]
        return remote(
            own, own, r.plane_send.at[group], r.plane_recv.at[group], place.plane[k][1]
        )

    def plane_all(group):
        others = blocks.at[group, place.core, pl.ds(0, planes - 1)]
        return remote(others, others, r.plane_send.at[group], r.plane_recv.at[group], place.partner())

    def core_copy(group):
        block = blocks.at[group, place.core]
        return remote(block, block, r.core_send.at[group], r.core_recv.at[group], place.partner())

    def core_arrival(group):
        block = blocks.at[group, 1 - place.core]
        return remote(block, block, r.core_send.at[group], r.core_recv.at[group], place.partner())

    def send_blocks(group):
        for k in range(1, planes):
            plane_copy(group, k).start()

    own_count = r.counts[place.lat]
    previous = jnp.where(not_first, r.counts[jnp.maximum(place.lat - 1, 0)], 0)
    row_of = r.row_of[...]
    limit = jnp.where(row_of < SHIFT_ROWS, previous - SHIFT_ROWS, own_count + SHIFT_ROWS)
    valid = jnp.where(row_of < jnp.minimum(limit, WIN_ROWS), 1.0, 0.0)
    take_own, take_row, take_side = r.take_own, r.take_row, r.take_side

    def framed_of(own, row, first):
        return (
            jnp.dot(take_own[...], own[...], preferred_element_type=F32)
            + jnp.dot(take_row[...], row[...], preferred_element_type=F32)
            + jnp.dot(take_side[first], side[0], preferred_element_type=F32)
            + jnp.dot(take_side[first + 1], side[1], preferred_element_type=F32)
        )

    hidden, normed, spread, out_grad = r.hidden, r.normed, r.spread, r.out_grad
    def frame():
        rows_out.wait_recv()
        corner_out.wait_recv()
        side_copy.wait_recv()

        framed = framed_of(tok, r.row_tok, 0)
        center = framed - jnp.mean(framed, axis=-1, keepdims=True)
        inverse = lax.rsqrt(jnp.mean(center * center, axis=-1, keepdims=True) + EPSILON)
        normal = center * inverse
        normed[...] = normal
        spread[...] = jnp.broadcast_to(inverse, spread.shape)
        hidden[...] = normal.astype(BF16)
        r.turned_hidden[...] = normal.astype(BF16).T
        framed = framed_of(cot, r.row_cot, 2)
        for j in range(features // 128):
            lanes = slice(j * 128, j * 128 + 128)
            out_grad[:, lanes] = jnp.where(valid > 0.0, framed[:, lanes], 0.0).astype(BF16)

    weight, qkv, qkv_grad = r.weight, r.qkv, r.qkv_grad

    def forward_arrivals(group):
        plane_all(group).wait_recv()
        core_copy(group).start()

    def collect(group):
        core_arrival(group).wait_recv()
        for p in range(planes):
            first = blocks[group, 0, p].astype(F32)
            second = blocks[group, 1, p].astype(F32)
            for z_hi in range(Z_HI):
                take = slice(z_hi * 8, z_hi * 8 + 8)
                rows = pl.ds((z_hi * planes + p) * 16, 16)
                weight[group, rows, :] = jnp.concatenate([first[take], second[take]], axis=0).astype(BF16)

    factor = HEAD_DIM ** (-0.5)
    whole, rest = divmod(GROUP * PAD, 128)
    allowed = jnp.concatenate([valid[0:PAD]] * whole + [valid[0:PAD, 0:rest]], axis=1) > 0.0
    mask = r.head_mask[...]
    windows = hidden.shape[0] // PAD

    def project(group):
        qkv[group] = jnp.dot(hidden[...], weight[group], preferred_element_type=F32).astype(BF16)

    def attend(group):
        for window in range(windows):
            at = slice(window * PAD, window * PAD + PAD)
            lanes = [slice(j * width, (j + 1) * width) for j in range(3)]
            query, keyed, valued = (qkv[group, at, lane] for lane in lanes)
            grad = out_grad[at, group * width : (group + 1) * width]
            query = jnp.concatenate([query] * GROUP, axis=0) * mask
            grad = jnp.concatenate([grad] * GROUP, axis=0) * mask
            scores = jnp.where(allowed, contract(keyed, query, ((1,), (1,))), -1000000000.0 / factor)
            exponent = jnp.exp2((scores - jnp.max(scores, axis=0, keepdims=True)) * (factor * LOG2_E))
            probs = exponent * (1.0 / jnp.sum(exponent, axis=0, keepdims=True))
            weight_grad = contract(valued, grad, ((1,), (1,)))
            mixed = jnp.sum(probs * weight_grad, axis=0, keepdims=True)
            score_grad = (probs * (weight_grad - mixed) * factor).astype(BF16)
            value_grad = jnp.dot(probs.astype(BF16), grad, preferred_element_type=F32)
            key_grad = jnp.dot(score_grad, query, preferred_element_type=F32)
            turned = contract(score_grad, keyed, ((0,), (0,)))
            query_grad = turned[0:PAD] * mask[0:PAD].astype(F32)
            for h in range(1, GROUP):
                rows_h = slice(h * PAD, h * PAD + PAD)
                query_grad = query_grad + turned[rows_h] * mask[rows_h].astype(F32)
            for lane, value in zip(lanes, (query_grad, key_grad, value_grad)):
                qkv_grad[group, at, lane] = value.astype(BF16)

    part = r.part

    def weigh(group):
        for j in range(3):
            lanes = slice(j * width, (j + 1) * width)
            piece = jnp.dot(r.turned_hidden[...], qkv_grad[group, :, lanes], preferred_element_type=F32)
            for core in range(CORES):
                for p in range(planes):
                    first = (p * CORES + core) * 8
                    both = [piece[z * planes * CORES * 8 + first :][0:8] for z in range(Z_HI)]
                    part[group, core, p, :, lanes] = jnp.concatenate(both, axis=0).astype(BF16)

    spans = ((0, 1), (1, 2), (2, 3), (3, 4))
    from_core, sums, from_plane, total = r.from_core, r.sums, r.from_plane, r.total

    def core_part(group):
        return remote(
            part.at[group, 1 - place.core], from_core.at[group],
            r.core_part_send.at[group], r.core_part_recv.at[group], place.partner(),
        )

    def plane_part(first, last, k):
        p, device = place.plane[k]
        span = pl.ds(first, last - first)
        return remote(
            sums.at[p, span], from_plane.at[place.p, span],
            r.plane_part_send.at[first], r.plane_part_recv.at[first], device,
        )

    def plane_part_all(first, last):
        others, span = pl.ds(0, planes - 1), pl.ds(first, last - first)
        return remote(
            sums.at[others, span], from_plane.at[others, span],
            r.plane_part_send.at[first], r.plane_part_recv.at[first], place.partner(),
        )

    def send_core(group):
        core_part(group).start()

    def send_plane(first, last):
        for group in range(first, last):
            core_part(group).wait_recv()
            sums[:, group] = (part[group, place.core].astype(F32) + from_core[group].astype(F32)).astype(BF16)
        for k in range(1, planes):
            plane_part(first, last, k).start()
        for group in range(first, last):
            from_plane[place.p, group] = sums[place.p, group]

    def add_plane(first, last):
        plane_part_all(first, last).wait_recv()
        for group in range(first, last):
            total[group] = jnp.sum(from_plane[:, group].astype(F32), axis=0)

    def accumulate(group):
        term = contract(qkv_grad[group], weight[group], ((1,), (1,)))
        if group == 0:
            r.hidden_grad[...] = term
        else:
            r.hidden_grad[...] += term

    def differentiate():
        hidden_grad = r.hidden_grad[...]
        normal = normed[...]
        mean_grad = jnp.mean(hidden_grad, axis=-1, keepdims=True)
        mean_mixed = jnp.mean(hidden_grad * normal, axis=-1, keepdims=True)
        frame_grad = spread[...] * (hidden_grad - mean_grad - normal * mean_mixed)
        back[...] = jnp.dot(r.give[...], frame_grad.astype(BF16), preferred_element_type=F32).astype(BF16)

    def return_relayed():
        rows_back.start_relayed()
        corner_back.start_relayed()

    def return_halos():
        rows_back.start()
        corner_back.start()
        side_return.start()

    def pass_back():
        rows_back.pass_on()
        corner_back.pass_on()

    part_units, from_ring = r.part_units, r.from_ring

    def ring_part(k):
        z, device = place.ring[k]
        return remote(
            part_units.at[z], from_ring.at[place.z], r.ring_part_send.at[0], r.ring_part_recv.at[0], device
        )

    ring_part_all = remote(
        part_units.at[others], from_ring.at[others], r.ring_part_send.at[0], r.ring_part_recv.at[0],
        place.partner(),
    )

    def send_ring_parts():
        for pair in range(lons // 2):
            for z_hi in range(Z_HI):
                tiles = []
                for j in range(3):
                    group, lanes = tile_at(pair * 3 + j)
                    tiles.append(total[group, pl.ds(z_hi * 8, 8), lanes])
                turned = [pltpu.roll(tile, 64, 1) for tile in tiles]
                part_units[z_hi * lons + 2 * pair] = jnp.concatenate([tiles[0], tiles[1]], axis=0).astype(BF16)
                part_units[z_hi * lons + 2 * pair + 1] = jnp.concatenate(
                    [jnp.where(lane_of < 64, turned[1], turned[2]), turned[2]], axis=0
                ).astype(BF16)

        for k in far_first(rings):
            ring_part(k).start()

        from_ring[place.z] = part_units[place.z]

    returned_copy = pltpu.make_async_copy(r.returned, returned, r.store_sem.at[0])
    weight_copy = pltpu.make_async_copy(r.weight_gradient, weight_gradient, r.store_sem.at[1])

    def finish_tokens():
        rows_back.wait_recv()
        corner_back.wait_recv()
        side_return.wait_recv()

        for part_of in range(2):
            rows = pl.ds(part_of * half_rows, half_rows)
            inner = back[0:half_rows] if part_of == 0 else r.row_back[...]
            outer = jnp.dot(r.place_sel[...], side_back[part_of], preferred_element_type=F32)
            r.returned[rows] = (inner.astype(F32) + outer).astype(BF16)
        returned_copy.start()

    def finish_weight():
        ring_part_all.wait_recv()

        result = from_ring[0].astype(F32)
        for z in range(1, rings):
            result = result + from_ring[z].astype(F32)
        r.weight_gradient[:, 0:128] = result[0:8]
        r.weight_gradient[:, 128:192] = result[8:16, 0:64]
        weight_copy.start()

    def drain():
        returned_copy.wait()
        weight_copy.wait()
        rows_out.wait_send()
        rows_back.wait_send()
        corner_out.wait_send()
        corner_back.wait_send()
        side_copy.wait_send()
        side_return.wait_send()
        ring_all.wait_send()
        ring_part_all.wait_send()
        for group in range(groups):
            plane_all(group).wait_send()
            core_copy(group).wait_send()
            core_part(group).wait_send()
        for first, last in spans:
            plane_part_all(first, last).wait_send()

    send_relayed()
    send_ring()
    send_halos()
    pass_on()
    join_ring()
    for group in range(groups):
        send_blocks(group)
    forward_arrivals(0)
    forward_arrivals(1)
    frame()
    for group in range(groups):
        collect(group)
        project(group)
        attend(group)
        if group > 0:
            send_plane(*spans[group - 1])
        if group < groups - 2:
            forward_arrivals(group + 2)
        weigh(group)
        send_core(group)
    for group in range(groups):
        accumulate(group)
    differentiate()
    return_relayed()
    send_plane(*spans[3])
    return_halos()
    pass_back()
    for span in spans:
        add_plane(*span)
    send_ring_parts()
    finish_tokens()
    finish_weight()
    drain()


def finish_kernel(returned, cot, weight, token_grad, weight_gradient, first, second, total, held, load_sem, store_sem):
    parts = first.shape[0]
    rows = first.shape[1]
    weight_load = pltpu.make_async_copy(weight, held, store_sem.at[parts])
    weight_store = pltpu.make_async_copy(held, weight_gradient, store_sem.at[parts + 1])
    weight_load.start()
    loads, stores = [], []
    for i in range(parts):
        at = pl.ds(i * rows, rows)
        loads.append(
            (
                pltpu.make_async_copy(returned.at[at], first.at[i], load_sem.at[i, 0]),
                pltpu.make_async_copy(cot.at[at], second.at[i], load_sem.at[i, 1]),
            )
        )
        stores.append(pltpu.make_async_copy(total.at[i], token_grad.at[at], store_sem.at[i]))
    for pair in loads:
        for load in pair:
            load.start()
    weight_load.wait()
    weight_store.start()
    for i in range(parts):
        for load in loads[i]:
            load.wait()
        total[i] = (second[i].astype(F32) + first[i].astype(F32)).astype(BF16)
        stores[i].start()
    for store in stores:
        store.wait()
    weight_store.wait()


def finish(returned, cot, weight):
    parts = 3
    block = VMEM((parts, cot.shape[0] // parts, cot.shape[1]), BF16)
    return pl.pallas_call(
        finish_kernel,
        out_shape=(
            jax.ShapeDtypeStruct(cot.shape, BF16),
            jax.ShapeDtypeStruct(weight.shape, F32),
        ),
        in_specs=[pl.BlockSpec(memory_space=pl.ANY)] * 3,
        out_specs=[pl.BlockSpec(memory_space=pl.ANY)] * 2,
        scratch_shapes=[
            block, block, block, VMEM(weight.shape, F32),
            pltpu.SemaphoreType.DMA((parts, 2)), pltpu.SemaphoreType.DMA((parts + 2,)),
        ],
        compiler_params=pltpu.CompilerParams(vmem_limit_bytes=56 * 2**20),
        name="finish",
    )(returned, cot, weight)


def frame_tables(cols):
    windows = cols // WIN_COLS
    total = windows * PAD
    half = SHIFT_ROWS * cols
    own = np.zeros((total, 2 * half), np.float32)
    row = np.zeros((total, half), np.float32)
    side = np.zeros((4, total, 48), np.float32)
    give = np.zeros((2 * half + 64, total), np.float32)
    row_of = np.full((total, 128), WIN_ROWS, np.int32)
    for window in range(windows):
        for r in range(WIN_ROWS):
            for c in range(WIN_COLS):
                t = window * PAD + r * WIN_COLS + c
                row_of[t] = r
                rr, g = r - SHIFT_ROWS, window * WIN_COLS + c - SHIFT_COLS
                upper = rr < 0
                if g >= 0:
                    if upper:
                        row[t, r * cols + g] = 1
                        give[half + r * cols + g, t] = 1
                    else:
                        own[t, rr * cols + g] = 1
                        give[rr * cols + g, t] = 1
                else:
                    at = (r % SHIFT_ROWS) * SHIFT_COLS + g + SHIFT_COLS
                    side[int(upper), t, at] = 1
                    side[2 + int(upper), t, 18 + at] = 1
                    give[2 * half + 32 * int(upper) + at, t] = 1
    return own, row, side, give, row_of


def on_device(lats, lons, tokens, cotangent, qkv_weight, band_rows):
    features = tokens.shape[-1]
    tok = tokens.reshape(-1, features)
    cot = cotangent.reshape(-1, features)
    count = tok.shape[0]
    half = count // 2
    cols = half // SHIFT_ROWS
    planes, rings = Y * X, Z_HI * lons
    columns = qkv_weight.shape[1] * lons
    width = GROUP * HEAD_DIM
    groups = features // width
    take_own, take_row, take_side, give, row_of = frame_tables(cols)
    total = take_own.shape[0]
    sel = np.zeros((2, 48, half), np.float32)
    place_sel = np.zeros((half, 32), np.float32)
    for row in range(SHIFT_ROWS):
        for col in range(SHIFT_COLS):
            at, edge = row * SHIFT_COLS + col, row * cols + cols - SHIFT_COLS + col
            sel[0, at, edge] = 1
            sel[1, 18 + at, edge] = 1
            place_sel[edge, at] = 1
    head_mask = np.zeros((GROUP, PAD, GROUP, HEAD_DIM), np.float32)
    for h in range(GROUP):
        head_mask[h, :, h] = 1
    low = lambda table: jnp.asarray(table, BF16)
    loaded = dict(
        w_in=qkv_weight, counts=band_rows, tok=tok, cot=cot, sel=low(sel), row_of=jnp.asarray(row_of), take_own=low(take_own), take_row=low(take_row),
        take_side=low(take_side), head_mask=low(head_mask.reshape(GROUP * PAD, width)), give=low(give),
        place_sel=low(place_sel),
    )
    dma = pltpu.SemaphoreType.DMA
    scratch = {name: VMEM(array.shape, array.dtype) for name, array in loaded.items()}
    scratch.update(counts=pltpu.SMEM(band_rows.shape, band_rows.dtype))
    scratch.update(
        wide=VMEM((8, 256), F32),
        unit=VMEM((16, 128), BF16),
        units=VMEM((rings, 16, 128), BF16),
        blocks=VMEM((groups, CORES, planes, 16, columns // groups), BF16),
        packed=VMEM((2, 48, features), BF16),
        side=VMEM((2, 48, features), BF16),
        row_tok=VMEM((half, features), BF16),
        row_cot=VMEM((half, features), BF16),
        relay=VMEM((2 * TILE, features), BF16),
        corner=VMEM((TILE, features), BF16),
        relay_back=VMEM((TILE, features), BF16),
        corner_back=VMEM((TILE, features), BF16),
        weight=VMEM((groups, features, columns // groups), BF16),
        hidden=VMEM((total, features), BF16),
        turned_hidden=VMEM((features, total), BF16),
        normed=VMEM((total, features), F32),
        spread=VMEM((total, features), F32),
        hidden_grad=VMEM((total, features), F32),
        out_grad=VMEM((total, features), BF16),
        qkv=VMEM((groups, total, columns // groups), BF16),
        qkv_grad=VMEM((groups, total, columns // groups), BF16),
        part=VMEM((groups, CORES, planes, 16, columns // groups), BF16),
        from_core=VMEM((groups, planes, 16, columns // groups), BF16),
        sums=VMEM((planes, groups, 16, columns // groups), BF16),
        from_plane=VMEM((planes, groups, 16, columns // groups), BF16),
        total=VMEM((groups, 16, columns // groups), F32),
        back=VMEM(give.shape[:1] + (features,), BF16),
        row_back=VMEM((half, features), BF16),
        side_back=VMEM((2, 32, features), BF16),
        part_units=VMEM((rings, 16, 128), BF16),
        from_ring=VMEM((rings, 16, 128), BF16),
        returned=VMEM(tok.shape, BF16),
        weight_gradient=VMEM(qkv_weight.shape, F32),
        load_sem=dma((len(loaded),)),
        store_sem=dma((2,)),
        relay_sem=dma((2,)),
        corner_sem=dma((2,)),
        relay_back_sem=dma((2,)),
        corner_back_sem=dma((2,)),
    )
    both = dict(
        ring=(1,), plane=(groups,), core=(groups,), halo=(2,), out=(2,),
        corner=(1,), back=(1,), corner_back=(1,), core_part=(groups,), plane_part=(groups,), ring_part=(1,),
    )
    for name, shape in both.items():
        scratch[name + "_send"] = dma(shape)
        scratch[name + "_recv"] = dma(shape)
    returned, weight_gradient = pl.pallas_call(
        functools.partial(kernel, lats, lons, len(loaded), list(scratch)),
        out_shape=(
            jax.ShapeDtypeStruct(tok.shape, BF16),
            jax.ShapeDtypeStruct(qkv_weight.shape, F32),
        ),
        in_specs=[pl.BlockSpec(memory_space=pl.ANY)] * len(loaded),
        out_specs=[pl.BlockSpec(memory_space=pl.ANY)] * 2,
        scratch_shapes=list(scratch.values()),
        compiler_params=pltpu.CompilerParams(
            collective_id=0, has_side_effects=True, vmem_limit_bytes=56 * 2**20
        ),
        name="sub_block",
    )(*loaded.values())
    token_grad, weight_gradient = finish(returned, cot, weight_gradient)
    return token_grad.reshape(tokens.shape), weight_gradient


def solution(mesh):
    return jax.shard_map(
        functools.partial(on_device, mesh.shape["lat"], mesh.shape["lon"]),
        mesh=mesh,
        in_specs=(P("lat", "lon", None), P("lat", "lon", None), P("lat", "lon"), P()),
        out_specs=(P("lat", "lon", None), P("lat", "lon")),
        check_vma=False,
    )
```

```python
import functools
import types

import jax
import jax.numpy as jnp
import numpy as np
from jax import lax
from jax.experimental import pallas as pl
from jax.experimental.pallas import tpu as pltpu
from jax.sharding import PartitionSpec as P

MESH = pl.DeviceIdType.MESH
VMEM = pltpu.VMEM
BF16 = jnp.bfloat16
F32 = jnp.float32

WIN_ROWS = 6
WIN_COLS = 12
SHIFT_ROWS = 3
SHIFT_COLS = 6
HEAD_DIM = 32
EPSILON = 1e-05
LOG2_E = 1.4426950408889634

Z_HI, Y, X, CORES = 2, 4, 4, 2


class Place:
    def __init__(self, lats, lons):
        self.lats, self.lons = lats, lons
        self.planes = Y * X
        self.rings = Z_HI * lons
        self.lat = lax.axis_index("lat")
        self.lon = lax.axis_index("lon")
        self.z_hi = lax.div(self.lat, self.planes * CORES)
        self.p = lax.div(lax.rem(self.lat, self.planes * CORES), CORES)
        self.core = lax.rem(self.lat, CORES)
        self.z = self.z_hi * lons + self.lon
        self.ring = [None] + [self._ring(k) for k in range(1, self.rings)]
        self.plane = [None] + [self._plane(k % Y * X + k // Y) for k in range(1, self.planes)]

    def _ring(self, k):
        z = lax.rem(self.z + k, self.rings)
        lat = lax.div(z, self.lons) * self.planes * CORES + self.p * CORES + self.core
        return z, (lat, lax.rem(z, self.lons))

    def _plane(self, k):
        x = lax.rem(lax.rem(self.p, X) + k % X, X)
        y = lax.rem(lax.div(self.p, X) + k // X, Y)
        p = y * X + x
        return p, (self.z_hi * self.planes * CORES + p * CORES + self.core, self.lon)

    def partner(self):
        return (self.lat + 1 - 2 * self.core, self.lon)

    def east(self):
        return lax.rem(self.lon + 1, self.lons)

    def west(self):
        return lax.rem(self.lon + self.lons - 1, self.lons)


def remote(src, dst, send, recv, device):
    return pltpu.make_async_remote_copy(
        src_ref=src, dst_ref=dst, send_sem=send, recv_sem=recv, device_id=device, device_id_type=MESH
    )


OUT_ROWS = (
    (0, Y - 1), (X - 1, 0), (0, 0), (1, 0), (0, 1), (X - 2, 0), (0, Y - 2), (1, Y - 1), (X - 1, 1),
)
OUT_CORNER = ((X - 2, Y - 1), (X - 1, Y - 2), (1, 1))
BACK_ROWS = (
    (X - 1, 0), (0, Y - 1), (X - 1, Y - 1), (X - 2, Y - 1), (X - 1, Y - 2), (1, Y - 1), (X - 1, 1), (X - 2, 0),
    (0, Y - 2),
)
BACK_CORNER = ((1, 0), (X - 2, Y - 2))
TILE = 16

PAD = 80
GROUP = 4


class Relays:
    def __init__(self, place):
        self.last_low = place.planes * CORES - 1
        self.first_high = place.planes * CORES
        self.low_end = place.lat == self.last_low
        self.high_end = place.lat == self.first_high

        def low(columns):
            return [(y * X + x) * CORES + CORES - 1 for x, y in columns]

        def high(columns):
            return [self.first_high + (y * X + x) * CORES for x, y in columns]

        self.out_rows, self.out_corner = low(OUT_ROWS), low(OUT_CORNER)
        self.back_rows, self.back_corner = high(BACK_ROWS), high(BACK_CORNER)


def far_first(count):
    return sorted(range(1, count), key=lambda k: -min(k, count - k))


def announce(place, relays):
    barrier = pltpu.get_barrier_semaphore()

    def signal(device):
        pl.semaphore_signal(barrier, inc=1, device_id=device, device_id_type=MESH)

    count = place.rings + place.planes - 1

    for ends, groups in (
        (relays.high_end, ((relays.out_rows, place.lon), (relays.out_corner, place.west()))),
        (relays.low_end, ((relays.back_rows, place.lon), (relays.back_corner, place.east()))),
    ):
        for lats, lon in groups:
            @pl.when(ends)
            def _():
                for lat in lats:
                    signal((lat, lon))

            for lat in lats:
                count = count + jnp.where(place.lat == lat, 1, 0)

    above = jnp.logical_and(place.lat > 0, jnp.logical_not(relays.high_end))
    below = jnp.logical_and(place.lat < place.lats - 1, jnp.logical_not(relays.low_end))

    @pl.when(above)
    def _():
        signal((place.lat - 1, place.lon))
        signal((place.lat - 1, place.west()))

    @pl.when(below)
    def _():
        signal((place.lat + 1, place.lon))
        signal((place.lat + 1, place.east()))

    count = count + jnp.where(above, 2, 0) + jnp.where(below, 2, 0)

    for k in far_first(place.rings):
        signal(place.ring[k][1])

    for k in range(1, place.planes):
        signal(place.plane[k][1])

    signal(place.partner())
    return count


def contract(left, right, dims):
    return lax.dot_general(left, right, (dims, ((), ())), preferred_element_type=F32)


def kernel(lats, lons, loaded, names, *refs):
    sources, token_sum, weight_gradient = refs[:loaded], refs[loaded], refs[loaded + 1]
    refs = refs[loaded + 2 :]
    targets = refs[:loaded]
    r = types.SimpleNamespace(**dict(zip(names, refs)))
    place = Place(lats, lons)
    relays = Relays(place)
    tok, cot = r.tok, r.cot
    half_rows = tok.shape[0] // 2
    features = tok.shape[1]
    width = GROUP * HEAD_DIM
    groups = features // width
    planes, rings = place.planes, place.rings
    lane_of = lax.broadcasted_iota(jnp.int32, (8, 128), 1)
    not_first = place.lat > 0
    not_last = place.lat < lats - 1

    loads = [
        pltpu.make_async_copy(source, target, r.load_sem.at[i])
        for i, (source, target) in enumerate(zip(sources, targets))
    ]
    expected = announce(place, relays)
    for load in loads:
        load.start()

    wide, unit, units = r.wide, r.unit, r.units
    wide[...] = jnp.zeros_like(wide)
    loads[0].wait()
    wide[:, 0 : r.w_in.shape[1]] = r.w_in[...].astype(F32)
    unit[...] = jnp.concatenate([wide[:, 0:128], wide[:, 128:256]], axis=0).astype(BF16)
    units[place.z] = unit[...]
    for load in loads[1:]:
        load.wait()

    packed, side, sel = r.packed, r.side, r.sel
    for part_of in range(2):
        rows = pl.ds(part_of * half_rows, half_rows)
        packed[part_of] = (
            jnp.dot(sel[0], tok[rows], preferred_element_type=F32)
            + jnp.dot(sel[1], cot[rows], preferred_element_type=F32)
        ).astype(BF16)

    @pl.when(jnp.logical_not(not_first))
    def _():
        side[1] = jnp.zeros(side.shape[1:], BF16)
        r.row_tok[...] = jnp.zeros_like(r.row_tok)
        r.row_cot[...] = jnp.zeros_like(r.row_cot)

    @pl.when(jnp.logical_not(not_last))
    def _():
        r.row_back[...] = jnp.zeros_like(r.row_back)
        r.side_back[1] = jnp.zeros(r.side_back.shape[1:], BF16)

    pl.semaphore_wait(pltpu.get_barrier_semaphore(), expected)

    def ring_copy(k):
        return remote(
            unit, units.at[place.z], r.ring_send.at[0], r.ring_recv.at[0], place.ring[k][1]
        )

    others = pl.ds(0, rings - 1)
    ring_all = remote(units.at[others], units.at[others], r.ring_send.at[0], r.ring_recv.at[0], place.partner())

    def send_ring():
        for k in far_first(rings):
            ring_copy(k).start()

    halo_send, halo_recv = r.halo_send, r.halo_recv
    side_copy = remote(packed.at[0], side.at[0], halo_send.at[0], halo_recv.at[0], (place.lat, place.east()))

    class Crossing:
        def __init__(self, sources, landings, lats, end, sends, receives, target, far, send, recv, relay, relay_sem):
            self.lats, self.end, self.sends, self.receives = lats, end, sends, receives
            self.direct, self.via, self.onward = [], [[] for _ in lats], [[] for _ in lats]
            for j, (source, landing) in enumerate(zip(sources, landings)):
                self.direct.append(remote(source, landing, send.at[j], recv.at[j], target))
                passing = relay.at[pl.ds(j * TILE, TILE)]
                for i, lat in enumerate(lats):
                    rows = pl.ds(i * TILE, TILE)
                    self.via[i].append(
                        remote(source.at[rows], passing, send.at[j], relay_sem.at[0], (lat, place.lon))
                    )
                    self.onward[i].append(
                        remote(passing, landing.at[rows], relay_sem.at[1], recv.at[j], far)
                    )
            self.passing = remote(relay, relay, relay_sem.at[1], relay_sem.at[0], place.partner())

        def start_relayed(self):
            @pl.when(self.end)
            def _():
                for copies in self.via:
                    for copy in copies:
                        copy.start()

        def start(self):
            @pl.when(jnp.logical_and(self.sends, jnp.logical_not(self.end)))
            def _():
                for copy in self.direct:
                    copy.start()

        def pass_on(self):
            is_relay = functools.reduce(jnp.logical_or, [place.lat == lat for lat in self.lats])

            @pl.when(is_relay)
            def _():
                self.passing.wait_recv()

            for lat, copies in zip(self.lats, self.onward):
                @pl.when(place.lat == lat)
                def _():
                    for copy in copies:
                        copy.start()

        def wait_recv(self):
            @pl.when(self.receives)
            def _():
                for copy in self.direct:
                    copy.wait_recv()

        def wait_send(self):
            @pl.when(self.sends)
            def _():
                for copy in self.direct:
                    copy.wait_send()

            is_relay = functools.reduce(jnp.logical_or, [place.lat == lat for lat in self.lats])

            @pl.when(is_relay)
            def _():
                self.passing.wait_send()

    back, side_back = r.back, r.side_back
    last_rows = pl.ds(half_rows, half_rows)
    rows_out = Crossing(
        [tok.at[last_rows], cot.at[last_rows]], [r.row_tok, r.row_cot], relays.out_rows, relays.low_end,
        not_last, not_first, (place.lat + 1, place.lon), (relays.first_high, place.lon),
        r.out_send, r.out_recv, r.relay, r.relay_sem,
    )
    corner_out = Crossing(
        [packed.at[1]], [side.at[1]], relays.out_corner, relays.low_end,
        not_last, not_first, (place.lat + 1, place.east()), (relays.first_high, place.east()),
        r.corner_send, r.corner_recv, r.corner, r.corner_sem,
    )
    rows_back = Crossing(
        [back.at[last_rows]], [r.row_back], relays.back_rows, relays.high_end,
        not_first, not_last, (place.lat - 1, place.lon), (relays.last_low, place.lon),
        r.back_send, r.back_recv, r.relay_back, r.relay_back_sem,
    )
    corner_back = Crossing(
        [back.at[pl.ds(2 * half_rows + 32, 32)]], [side_back.at[1]], relays.back_corner, relays.high_end,
        not_first, not_last, (place.lat - 1, place.west()), (relays.last_low, place.west()),
        r.corner_back_send, r.corner_back_recv, r.corner_back, r.corner_back_sem,
    )
    side_return = remote(
        back.at[pl.ds(2 * half_rows, 32)], side_back.at[0], halo_send.at[1], halo_recv.at[1],
        (place.lat, place.west()),
    )

    def send_relayed():
        rows_out.start_relayed()
        corner_out.start_relayed()

    def send_halos():
        rows_out.start()
        corner_out.start()
        side_copy.start()

    def pass_on():
        rows_out.pass_on()
        corner_out.pass_on()

    blocks = r.blocks

    def tile_at(n):
        which, group = divmod(n, groups)
        return group, pl.ds(which * width, width)

    def join_ring():
        ring_all.wait_recv()

        for pair in range(lons // 2):
            tiles = [[], [], []]
            for z_hi in range(Z_HI):
                even = units[z_hi * lons + 2 * pair].astype(F32)
                odd = units[z_hi * lons + 2 * pair + 1].astype(F32)
                turned_top = pltpu.roll(odd[0:8], 64, 1)
                turned_low = pltpu.roll(odd[8:16], 64, 1)
                tiles[0].append(even[0:8])
                tiles[1].append(jnp.where(lane_of < 64, even[8:16], turned_top))
                tiles[2].append(jnp.where(lane_of < 64, turned_top, turned_low))
            for j in range(3):
                group, lanes = tile_at(pair * 3 + j)
                blocks[group, place.core, place.p, :, lanes] = jnp.concatenate(tiles[j], axis=0).astype(BF16)

    def plane_copy(group, k):
        own = blocks.at[group, place.core, place.p]
        return remote(
            own, own, r.plane_send.at[group], r.plane_recv.at[group], place.plane[k][1]
        )

    def plane_all(group):
        others = blocks.at[group, place.core, pl.ds(0, planes - 1)]
        return remote(others, others, r.plane_send.at[group], r.plane_recv.at[group], place.partner())

    def core_copy(group):
        block = blocks.at[group, place.core]
        return remote(block, block, r.core_send.at[group], r.core_recv.at[group], place.partner())

    def core_arrival(group):
        block = blocks.at[group, 1 - place.core]
        return remote(block, block, r.core_send.at[group], r.core_recv.at[group], place.partner())

    def send_blocks(group):
        for k in range(1, planes):
            plane_copy(group, k).start()

    own_count = r.counts[place.lat]
    previous = jnp.where(not_first, r.counts[jnp.maximum(place.lat - 1, 0)], 0)
    row_of = r.row_of[...]
    limit = jnp.where(row_of < SHIFT_ROWS, previous - SHIFT_ROWS, own_count + SHIFT_ROWS)
    valid = jnp.where(row_of < jnp.minimum(limit, WIN_ROWS), 1.0, 0.0)
    take_own, take_row, take_side = r.take_own, r.take_row, r.take_side

    def framed_of(own, row, first):
        return (
            jnp.dot(take_own[...], own[...], preferred_element_type=F32)
            + jnp.dot(take_row[...], row[...], preferred_element_type=F32)
            + jnp.dot(take_side[first], side[0], preferred_element_type=F32)
            + jnp.dot(take_side[first + 1], side[1], preferred_element_type=F32)
        )

    hidden, normed, spread, out_grad = r.hidden, r.normed, r.spread, r.out_grad
    def frame():
        rows_out.wait_recv()
        corner_out.wait_recv()
        side_copy.wait_recv()

        framed = framed_of(tok, r.row_tok, 0)
        center = framed - jnp.mean(framed, axis=-1, keepdims=True)
        inverse = lax.rsqrt(jnp.mean(center * center, axis=-1, keepdims=True) + EPSILON)
        normal = center * inverse
        normed[...] = normal
        spread[...] = jnp.broadcast_to(inverse, spread.shape)
        hidden[...] = normal.astype(BF16)
        r.turned_hidden[...] = normal.astype(BF16).T
        framed = framed_of(cot, r.row_cot, 2)
        for j in range(features // 128):
            lanes = slice(j * 128, j * 128 + 128)
            out_grad[:, lanes] = jnp.where(valid > 0.0, framed[:, lanes], 0.0).astype(BF16)

    weight, qkv, qkv_grad = r.weight, r.qkv, r.qkv_grad

    def forward_arrivals(group):
        plane_all(group).wait_recv()
        core_copy(group).start()

    def collect(group):
        core_arrival(group).wait_recv()
        for p in range(planes):
            first = blocks[group, 0, p].astype(F32)
            second = blocks[group, 1, p].astype(F32)
            for z_hi in range(Z_HI):
                take = slice(z_hi * 8, z_hi * 8 + 8)
                rows = pl.ds((z_hi * planes + p) * 16, 16)
                weight[group, rows, :] = jnp.concatenate([first[take], second[take]], axis=0).astype(BF16)

    factor = HEAD_DIM ** (-0.5)
    whole, rest = divmod(GROUP * PAD, 128)
    allowed = jnp.concatenate([valid[0:PAD]] * whole + [valid[0:PAD, 0:rest]], axis=1) > 0.0
    mask = r.head_mask[...]
    windows = hidden.shape[0] // PAD

    def project(group):
        qkv[group] = jnp.dot(hidden[...], weight[group], preferred_element_type=F32).astype(BF16)

    def attend(group):
        for window in range(windows):
            at = slice(window * PAD, window * PAD + PAD)
            lanes = [slice(j * width, (j + 1) * width) for j in range(3)]
            query, keyed, valued = (qkv[group, at, lane] for lane in lanes)
            grad = out_grad[at, group * width : (group + 1) * width]
            query = jnp.concatenate([query] * GROUP, axis=0) * mask
            grad = jnp.concatenate([grad] * GROUP, axis=0) * mask
            scores = jnp.where(allowed, contract(keyed, query, ((1,), (1,))), -1000000000.0 / factor)
            exponent = jnp.exp2((scores - jnp.max(scores, axis=0, keepdims=True)) * (factor * LOG2_E))
            probs = exponent * (1.0 / jnp.sum(exponent, axis=0, keepdims=True))
            weight_grad = contract(valued, grad, ((1,), (1,)))
            mixed = jnp.sum(probs * weight_grad, axis=0, keepdims=True)
            score_grad = (probs * (weight_grad - mixed) * factor).astype(BF16)
            value_grad = jnp.dot(probs.astype(BF16), grad, preferred_element_type=F32)
            key_grad = jnp.dot(score_grad, query, preferred_element_type=F32)
            turned = contract(score_grad, keyed, ((0,), (0,)))
            query_grad = turned[0:PAD] * mask[0:PAD].astype(F32)
            for h in range(1, GROUP):
                rows_h = slice(h * PAD, h * PAD + PAD)
                query_grad = query_grad + turned[rows_h] * mask[rows_h].astype(F32)
            for lane, value in zip(lanes, (query_grad, key_grad, value_grad)):
                qkv_grad[group, at, lane] = value.astype(BF16)

    part = r.part

    def weigh(group):
        for j in range(3):
            lanes = slice(j * width, (j + 1) * width)
            piece = jnp.dot(r.turned_hidden[...], qkv_grad[group, :, lanes], preferred_element_type=F32)
            for core in range(CORES):
                for p in range(planes):
                    first = (p * CORES + core) * 8
                    both = [piece[z * planes * CORES * 8 + first :][0:8] for z in range(Z_HI)]
                    part[group, core, p, :, lanes] = jnp.concatenate(both, axis=0).astype(BF16)

    spans = ((0, 1), (1, 2), (2, 3), (3, 4))
    from_core, sums, from_plane, total = r.from_core, r.sums, r.from_plane, r.total

    def core_part(group):
        return remote(
            part.at[group, 1 - place.core], from_core.at[group],
            r.core_part_send.at[group], r.core_part_recv.at[group], place.partner(),
        )

    def plane_part(first, last, k):
        p, device = place.plane[k]
        span = pl.ds(first, last - first)
        return remote(
            sums.at[p, span], from_plane.at[place.p, span],
            r.plane_part_send.at[first], r.plane_part_recv.at[first], device,
        )

    def plane_part_all(first, last):
        others, span = pl.ds(0, planes - 1), pl.ds(first, last - first)
        return remote(
            sums.at[others, span], from_plane.at[others, span],
            r.plane_part_send.at[first], r.plane_part_recv.at[first], place.partner(),
        )

    def send_core(group):
        core_part(group).start()

    def send_plane(first, last):
        for group in range(first, last):
            core_part(group).wait_recv()
            sums[:, group] = (part[group, place.core].astype(F32) + from_core[group].astype(F32)).astype(BF16)
        for k in range(1, planes):
            plane_part(first, last, k).start()
        for group in range(first, last):
            from_plane[place.p, group] = sums[place.p, group]

    def add_plane(first, last):
        plane_part_all(first, last).wait_recv()
        for group in range(first, last):
            total[group] = jnp.sum(from_plane[:, group].astype(F32), axis=0)

    def accumulate(group):
        term = contract(qkv_grad[group], weight[group], ((1,), (1,)))
        if group == 0:
            r.hidden_grad[...] = term
        else:
            r.hidden_grad[...] += term

    def differentiate():
        hidden_grad = r.hidden_grad[...]
        normal = normed[...]
        mean_grad = jnp.mean(hidden_grad, axis=-1, keepdims=True)
        mean_mixed = jnp.mean(hidden_grad * normal, axis=-1, keepdims=True)
        frame_grad = spread[...] * (hidden_grad - mean_grad - normal * mean_mixed)
        back[...] = jnp.dot(r.give[...], frame_grad.astype(BF16), preferred_element_type=F32).astype(BF16)

    def return_relayed():
        rows_back.start_relayed()
        corner_back.start_relayed()

    def return_halos():
        rows_back.start()
        corner_back.start()
        side_return.start()

    def pass_back():
        rows_back.pass_on()
        corner_back.pass_on()

    part_units, from_ring = r.part_units, r.from_ring

    def ring_part(k):
        z, device = place.ring[k]
        return remote(
            part_units.at[z], from_ring.at[place.z], r.ring_part_send.at[0], r.ring_part_recv.at[0], device
        )

    ring_part_all = remote(
        part_units.at[others], from_ring.at[others], r.ring_part_send.at[0], r.ring_part_recv.at[0],
        place.partner(),
    )

    def send_ring_parts():
        for pair in range(lons // 2):
            for z_hi in range(Z_HI):
                tiles = []
                for j in range(3):
                    group, lanes = tile_at(pair * 3 + j)
                    tiles.append(total[group, pl.ds(z_hi * 8, 8), lanes])
                turned = [pltpu.roll(tile, 64, 1) for tile in tiles]
                part_units[z_hi * lons + 2 * pair] = jnp.concatenate([tiles[0], tiles[1]], axis=0).astype(BF16)
                part_units[z_hi * lons + 2 * pair + 1] = jnp.concatenate(
                    [jnp.where(lane_of < 64, turned[1], turned[2]), turned[2]], axis=0
                ).astype(BF16)

        for k in far_first(rings):
            ring_part(k).start()

        from_ring[place.z] = part_units[place.z]

    token_sum_copy = pltpu.make_async_copy(r.token_sum, token_sum, r.store_sem.at[0])
    weight_copy = pltpu.make_async_copy(r.weight_gradient, weight_gradient, r.store_sem.at[1])

    def finish_tokens():
        rows_back.wait_recv()
        corner_back.wait_recv()
        side_return.wait_recv()

        for part_of in range(2):
            rows = pl.ds(part_of * half_rows, half_rows)
            inner = back[0:half_rows] if part_of == 0 else r.row_back[...]
            outer = jnp.dot(r.place_sel[...], side_back[part_of], preferred_element_type=F32)
            r.token_sum[rows] = (cot[rows].astype(F32) + (inner.astype(F32) + outer)).astype(BF16)
        token_sum_copy.start()

    def finish_weight():
        ring_part_all.wait_recv()

        result = from_ring[0].astype(F32)
        for z in range(1, rings):
            result = result + from_ring[z].astype(F32)
        r.weight_gradient[:, 0:128] = result[0:8]
        r.weight_gradient[:, 128:192] = result[8:16, 0:64]
        weight_copy.start()

    def drain():
        token_sum_copy.wait()
        weight_copy.wait()
        rows_out.wait_send()
        rows_back.wait_send()
        corner_out.wait_send()
        corner_back.wait_send()
        side_copy.wait_send()
        side_return.wait_send()
        ring_all.wait_send()
        ring_part_all.wait_send()
        for group in range(groups):
            plane_all(group).wait_send()
            core_copy(group).wait_send()
            core_part(group).wait_send()
        for first, last in spans:
            plane_part_all(first, last).wait_send()

    send_relayed()
    send_ring()
    send_halos()
    pass_on()
    join_ring()
    for group in range(groups):
        send_blocks(group)
    @pl.when(jnp.logical_not(relays.high_end))
    def _():
        frame()

    forward_arrivals(0)
    forward_arrivals(1)

    @pl.when(relays.high_end)
    def _():
        frame()

    for group in range(groups):
        collect(group)
        project(group)
        attend(group)
        if group > 0:
            send_plane(*spans[group - 1])
        if group < groups - 2:
            forward_arrivals(group + 2)
        weigh(group)
        send_core(group)
    for group in range(groups):
        accumulate(group)
    differentiate()
    return_relayed()
    send_plane(*spans[3])
    return_halos()
    pass_back()
    for span in spans:
        add_plane(*span)
    send_ring_parts()
    finish_tokens()
    finish_weight()
    drain()


def finish_kernel(token_sum, weight, token_grad, weight_gradient, first, held, load_sem, store_sem):
    parts = first.shape[0]
    rows = first.shape[1]
    weight_load = pltpu.make_async_copy(weight, held, store_sem.at[parts])
    weight_store = pltpu.make_async_copy(held, weight_gradient, store_sem.at[parts + 1])
    weight_load.start()
    loads, stores = [], []
    for i in range(parts):
        at = pl.ds(i * rows, rows)
        loads.append(
            (
                pltpu.make_async_copy(token_sum.at[at], first.at[i], load_sem.at[i, 0]),
            )
        )
        stores.append(pltpu.make_async_copy(first.at[i], token_grad.at[at], store_sem.at[i]))
    for pair in loads:
        for load in pair:
            load.start()
    weight_load.wait()
    weight_store.start()
    for i in range(parts):
        for load in loads[i]:
            load.wait()
        stores[i].start()
    for store in stores:
        store.wait()
    weight_store.wait()


def finish(token_sum, weight):
    parts = 3
    block = VMEM((parts, token_sum.shape[0] // parts, token_sum.shape[1]), BF16)
    return pl.pallas_call(
        finish_kernel,
        out_shape=(
            jax.ShapeDtypeStruct(token_sum.shape, BF16),
            jax.ShapeDtypeStruct(weight.shape, F32),
        ),
        in_specs=[pl.BlockSpec(memory_space=pl.ANY)] * 2,
        out_specs=[pl.BlockSpec(memory_space=pl.ANY)] * 2,
        scratch_shapes=[
            block, VMEM(weight.shape, F32),
            pltpu.SemaphoreType.DMA((parts, 1)), pltpu.SemaphoreType.DMA((parts + 2,)),
        ],
        compiler_params=pltpu.CompilerParams(vmem_limit_bytes=56 * 2**20),
        name="finish",
    )(token_sum, weight)


def frame_tables(cols):
    windows = cols // WIN_COLS
    total = windows * PAD
    half = SHIFT_ROWS * cols
    own = np.zeros((total, 2 * half), np.float32)
    row = np.zeros((total, half), np.float32)
    side = np.zeros((4, total, 48), np.float32)
    give = np.zeros((2 * half + 64, total), np.float32)
    row_of = np.full((total, 128), WIN_ROWS, np.int32)
    for window in range(windows):
        for r in range(WIN_ROWS):
            for c in range(WIN_COLS):
                t = window * PAD + r * WIN_COLS + c
                row_of[t] = r
                rr, g = r - SHIFT_ROWS, window * WIN_COLS + c - SHIFT_COLS
                upper = rr < 0
                if g >= 0:
                    if upper:
                        row[t, r * cols + g] = 1
                        give[half + r * cols + g, t] = 1
                    else:
                        own[t, rr * cols + g] = 1
                        give[rr * cols + g, t] = 1
                else:
                    at = (r % SHIFT_ROWS) * SHIFT_COLS + g + SHIFT_COLS
                    side[int(upper), t, at] = 1
                    side[2 + int(upper), t, 18 + at] = 1
                    give[2 * half + 32 * int(upper) + at, t] = 1
    return own, row, side, give, row_of


def on_device(lats, lons, tokens, cotangent, qkv_weight, band_rows):
    features = tokens.shape[-1]
    tok = tokens.reshape(-1, features)
    cot = cotangent.reshape(-1, features)
    count = tok.shape[0]
    half = count // 2
    cols = half // SHIFT_ROWS
    planes, rings = Y * X, Z_HI * lons
    columns = qkv_weight.shape[1] * lons
    width = GROUP * HEAD_DIM
    groups = features // width
    take_own, take_row, take_side, give, row_of = frame_tables(cols)
    total = take_own.shape[0]
    sel = np.zeros((2, 48, half), np.float32)
    place_sel = np.zeros((half, 32), np.float32)
    for row in range(SHIFT_ROWS):
        for col in range(SHIFT_COLS):
            at, edge = row * SHIFT_COLS + col, row * cols + cols - SHIFT_COLS + col
            sel[0, at, edge] = 1
            sel[1, 18 + at, edge] = 1
            place_sel[edge, at] = 1
    head_mask = np.zeros((GROUP, PAD, GROUP, HEAD_DIM), np.float32)
    for h in range(GROUP):
        head_mask[h, :, h] = 1
    low = lambda table: jnp.asarray(table, BF16)
    loaded = dict(
        w_in=qkv_weight, counts=band_rows, tok=tok, cot=cot, sel=low(sel), row_of=jnp.asarray(row_of), take_own=low(take_own), take_row=low(take_row),
        take_side=low(take_side), head_mask=low(head_mask.reshape(GROUP * PAD, width)), give=low(give),
        place_sel=low(place_sel),
    )
    dma = pltpu.SemaphoreType.DMA
    scratch = {name: VMEM(array.shape, array.dtype) for name, array in loaded.items()}
    scratch.update(counts=pltpu.SMEM(band_rows.shape, band_rows.dtype))
    scratch.update(
        wide=VMEM((8, 256), F32),
        unit=VMEM((16, 128), BF16),
        units=VMEM((rings, 16, 128), BF16),
        blocks=VMEM((groups, CORES, planes, 16, columns // groups), BF16),
        packed=VMEM((2, 48, features), BF16),
        side=VMEM((2, 48, features), BF16),
        row_tok=VMEM((half, features), BF16),
        row_cot=VMEM((half, features), BF16),
        relay=VMEM((2 * TILE, features), BF16),
        corner=VMEM((TILE, features), BF16),
        relay_back=VMEM((TILE, features), BF16),
        corner_back=VMEM((TILE, features), BF16),
        weight=VMEM((groups, features, columns // groups), BF16),
        hidden=VMEM((total, features), BF16),
        turned_hidden=VMEM((features, total), BF16),
        normed=VMEM((total, features), F32),
        spread=VMEM((total, features), F32),
        hidden_grad=VMEM((total, features), F32),
        out_grad=VMEM((total, features), BF16),
        qkv=VMEM((groups, total, columns // groups), BF16),
        qkv_grad=VMEM((groups, total, columns // groups), BF16),
        part=VMEM((groups, CORES, planes, 16, columns // groups), BF16),
        from_core=VMEM((groups, planes, 16, columns // groups), BF16),
        sums=VMEM((planes, groups, 16, columns // groups), BF16),
        from_plane=VMEM((planes, groups, 16, columns // groups), BF16),
        total=VMEM((groups, 16, columns // groups), F32),
        back=VMEM(give.shape[:1] + (features,), BF16),
        row_back=VMEM((half, features), BF16),
        side_back=VMEM((2, 32, features), BF16),
        part_units=VMEM((rings, 16, 128), BF16),
        from_ring=VMEM((rings, 16, 128), BF16),
        token_sum=VMEM(tok.shape, BF16),
        weight_gradient=VMEM(qkv_weight.shape, F32),
        load_sem=dma((len(loaded),)),
        store_sem=dma((2,)),
        relay_sem=dma((2,)),
        corner_sem=dma((2,)),
        relay_back_sem=dma((2,)),
        corner_back_sem=dma((2,)),
    )
    both = dict(
        ring=(1,), plane=(groups,), core=(groups,), halo=(2,), out=(2,),
        corner=(1,), back=(1,), corner_back=(1,), core_part=(groups,), plane_part=(groups,), ring_part=(1,),
    )
    for name, shape in both.items():
        scratch[name + "_send"] = dma(shape)
        scratch[name + "_recv"] = dma(shape)
    token_sum, weight_gradient = pl.pallas_call(
        functools.partial(kernel, lats, lons, len(loaded), list(scratch)),
        out_shape=(
            jax.ShapeDtypeStruct(tok.shape, BF16),
            jax.ShapeDtypeStruct(qkv_weight.shape, F32),
        ),
        in_specs=[pl.BlockSpec(memory_space=pl.ANY)] * len(loaded),
        out_specs=[pl.BlockSpec(memory_space=pl.ANY)] * 2,
        scratch_shapes=list(scratch.values()),
        compiler_params=pltpu.CompilerParams(
            collective_id=0, has_side_effects=True, vmem_limit_bytes=56 * 2**20
        ),
        name="sub_block",
    )(*loaded.values())
    token_grad, weight_gradient = finish(token_sum, weight_gradient)
    return token_grad.reshape(tokens.shape), weight_gradient


def solution(mesh):
    return jax.shard_map(
        functools.partial(on_device, mesh.shape["lat"], mesh.shape["lon"]),
        mesh=mesh,
        in_specs=(P("lat", "lon", None), P("lat", "lon", None), P("lat", "lon"), P()),
        out_specs=(P("lat", "lon", None), P("lat", "lon")),
        check_vma=False,
    )
```

```python
import functools
import types

import jax
import jax.numpy as jnp
import numpy as np
from jax import lax
from jax.experimental import pallas as pl
from jax.experimental.pallas import tpu as pltpu
from jax.sharding import PartitionSpec as P

MESH = pl.DeviceIdType.MESH
VMEM = pltpu.VMEM
BF16 = jnp.bfloat16
F32 = jnp.float32

WIN_ROWS = 6
WIN_COLS = 12
SHIFT_ROWS = 3
SHIFT_COLS = 6
HEAD_DIM = 32
EPSILON = 1e-05
LOG2_E = 1.4426950408889634

Z_HI, Y, X, CORES = 2, 4, 4, 2


class Place:
    def __init__(self, lats, lons):
        self.lats, self.lons = lats, lons
        self.planes = Y * X
        self.rings = Z_HI * lons
        self.lat = lax.axis_index("lat")
        self.lon = lax.axis_index("lon")
        self.z_hi = lax.div(self.lat, self.planes * CORES)
        self.p = lax.div(lax.rem(self.lat, self.planes * CORES), CORES)
        self.core = lax.rem(self.lat, CORES)
        self.z = self.z_hi * lons + self.lon
        self.ring = [None] + [self._ring(k) for k in range(1, self.rings)]
        self.plane = [None] + [self._plane(k % Y * X + k // Y) for k in range(1, self.planes)]

    def _ring(self, k):
        z = lax.rem(self.z + k, self.rings)
        lat = lax.div(z, self.lons) * self.planes * CORES + self.p * CORES + self.core
        return z, (lat, lax.rem(z, self.lons))

    def _plane(self, k):
        x = lax.rem(lax.rem(self.p, X) + k % X, X)
        y = lax.rem(lax.div(self.p, X) + k // X, Y)
        p = y * X + x
        return p, (self.z_hi * self.planes * CORES + p * CORES + self.core, self.lon)

    def partner(self):
        return (self.lat + 1 - 2 * self.core, self.lon)

    def east(self):
        return lax.rem(self.lon + 1, self.lons)

    def west(self):
        return lax.rem(self.lon + self.lons - 1, self.lons)


def remote(src, dst, send, recv, device):
    return pltpu.make_async_remote_copy(
        src_ref=src, dst_ref=dst, send_sem=send, recv_sem=recv, device_id=device, device_id_type=MESH
    )


OUT_ROWS = (
    (0, Y - 1), (X - 1, 0), (0, 0), (1, 0), (0, 1), (X - 2, 0), (0, Y - 2), (1, Y - 1), (X - 1, 1),
)
OUT_CORNER = ((X - 2, Y - 1), (X - 1, Y - 2), (1, 1))
BACK_ROWS = (
    (X - 1, 0), (0, Y - 1), (X - 1, Y - 1), (X - 2, Y - 1), (X - 1, Y - 2), (1, Y - 1), (X - 1, 1), (X - 2, 0),
    (0, Y - 2),
)
BACK_CORNER = ((1, 0), (X - 2, Y - 2))
TILE = 16

PAD = 80
GROUP = 4


class Relays:
    def __init__(self, place):
        self.last_low = place.planes * CORES - 1
        self.first_high = place.planes * CORES
        self.low_end = place.lat == self.last_low
        self.high_end = place.lat == self.first_high

        def low(columns):
            return [(y * X + x) * CORES + CORES - 1 for x, y in columns]

        def high(columns):
            return [self.first_high + (y * X + x) * CORES for x, y in columns]

        self.out_rows, self.out_corner = low(OUT_ROWS), low(OUT_CORNER)
        self.back_rows, self.back_corner = high(BACK_ROWS), high(BACK_CORNER)


def far_first(count):
    return sorted(range(1, count), key=lambda k: -min(k, count - k))


def announce(place, relays):
    barrier = pltpu.get_barrier_semaphore()

    def signal(device):
        pl.semaphore_signal(barrier, inc=1, device_id=device, device_id_type=MESH)

    count = place.rings + place.planes - 1

    for ends, groups in (
        (relays.high_end, ((relays.out_rows, place.lon), (relays.out_corner, place.west()))),
        (relays.low_end, ((relays.back_rows, place.lon), (relays.back_corner, place.east()))),
    ):
        for lats, lon in groups:
            @pl.when(ends)
            def _():
                for lat in lats:
                    signal((lat, lon))

            for lat in lats:
                count = count + jnp.where(place.lat == lat, 1, 0)

    above = jnp.logical_and(place.lat > 0, jnp.logical_not(relays.high_end))
    below = jnp.logical_and(place.lat < place.lats - 1, jnp.logical_not(relays.low_end))

    @pl.when(above)
    def _():
        signal((place.lat - 1, place.lon))
        signal((place.lat - 1, place.west()))

    @pl.when(below)
    def _():
        signal((place.lat + 1, place.lon))
        signal((place.lat + 1, place.east()))

    count = count + jnp.where(above, 2, 0) + jnp.where(below, 2, 0)

    for k in far_first(place.rings):
        signal(place.ring[k][1])

    for k in range(1, place.planes):
        signal(place.plane[k][1])

    signal(place.partner())
    return count


def contract(left, right, dims):
    return lax.dot_general(left, right, (dims, ((), ())), preferred_element_type=F32)


def kernel(lats, lons, loaded, names, *refs):
    sources, token_sum, weight_gradient = refs[:loaded], refs[loaded], refs[loaded + 1]
    refs = refs[loaded + 2 :]
    targets = refs[:loaded]
    r = types.SimpleNamespace(**dict(zip(names, refs)))
    place = Place(lats, lons)
    relays = Relays(place)
    tok, cot = r.tok, r.cot
    half_rows = tok.shape[0] // 2
    features = tok.shape[1]
    width = GROUP * HEAD_DIM
    groups = features // width
    planes, rings = place.planes, place.rings
    lane_of = lax.broadcasted_iota(jnp.int32, (8, 128), 1)
    not_first = place.lat > 0
    not_last = place.lat < lats - 1

    loads = [
        pltpu.make_async_copy(source, target, r.load_sem.at[i])
        for i, (source, target) in enumerate(zip(sources, targets))
    ]
    expected = announce(place, relays)
    for load in loads:
        load.start()

    wide, unit, units = r.wide, r.unit, r.units
    wide[...] = jnp.zeros_like(wide)
    loads[0].wait()
    wide[:, 0 : r.w_in.shape[1]] = r.w_in[...].astype(F32)
    unit[...] = jnp.concatenate([wide[:, 0:128], wide[:, 128:256]], axis=0).astype(BF16)
    units[place.z] = unit[...]
    for load in loads[1:]:
        load.wait()

    packed, side, sel = r.packed, r.side, r.sel
    for part_of in range(2):
        rows = pl.ds(part_of * half_rows, half_rows)
        packed[part_of] = (
            jnp.dot(sel[0], tok[rows], preferred_element_type=F32)
            + jnp.dot(sel[1], cot[rows], preferred_element_type=F32)
        ).astype(BF16)

    @pl.when(jnp.logical_not(not_first))
    def _():
        side[1] = jnp.zeros(side.shape[1:], BF16)
        r.row_tok[...] = jnp.zeros_like(r.row_tok)
        r.row_cot[...] = jnp.zeros_like(r.row_cot)

    @pl.when(jnp.logical_not(not_last))
    def _():
        r.row_back[...] = jnp.zeros_like(r.row_back)
        r.side_back[1] = jnp.zeros(r.side_back.shape[1:], BF16)

    pl.semaphore_wait(pltpu.get_barrier_semaphore(), expected)

    def ring_copy(k):
        return remote(
            unit, units.at[place.z], r.ring_send.at[0], r.ring_recv.at[0], place.ring[k][1]
        )

    others = pl.ds(0, rings - 1)
    ring_all = remote(units.at[others], units.at[others], r.ring_send.at[0], r.ring_recv.at[0], place.partner())

    def send_ring():
        for k in far_first(rings):
            ring_copy(k).start()

    halo_send, halo_recv = r.halo_send, r.halo_recv
    side_copy = remote(packed.at[0], side.at[0], halo_send.at[0], halo_recv.at[0], (place.lat, place.east()))

    class Crossing:
        def __init__(self, sources, landings, lats, end, sends, receives, target, far, send, recv, relay, relay_sem):
            self.lats, self.end, self.sends, self.receives = lats, end, sends, receives
            self.direct, self.via, self.onward = [], [[] for _ in lats], [[] for _ in lats]
            for j, (source, landing) in enumerate(zip(sources, landings)):
                self.direct.append(remote(source, landing, send.at[j], recv.at[j], target))
                passing = relay.at[pl.ds(j * TILE, TILE)]
                for i, lat in enumerate(lats):
                    rows = pl.ds(i * TILE, TILE)
                    self.via[i].append(
                        remote(source.at[rows], passing, send.at[j], relay_sem.at[0], (lat, place.lon))
                    )
                    self.onward[i].append(
                        remote(passing, landing.at[rows], relay_sem.at[1], recv.at[j], far)
                    )
            self.passing = remote(relay, relay, relay_sem.at[1], relay_sem.at[0], place.partner())

        def start_relayed(self):
            @pl.when(self.end)
            def _():
                for copies in self.via:
                    for copy in copies:
                        copy.start()

        def start(self):
            @pl.when(jnp.logical_and(self.sends, jnp.logical_not(self.end)))
            def _():
                for copy in self.direct:
                    copy.start()

        def pass_on(self):
            is_relay = functools.reduce(jnp.logical_or, [place.lat == lat for lat in self.lats])

            @pl.when(is_relay)
            def _():
                self.passing.wait_recv()

            for lat, copies in zip(self.lats, self.onward):
                @pl.when(place.lat == lat)
                def _():
                    for copy in copies:
                        copy.start()

        def wait_recv(self):
            @pl.when(self.receives)
            def _():
                for copy in self.direct:
                    copy.wait_recv()

        def wait_send(self):
            @pl.when(self.sends)
            def _():
                for copy in self.direct:
                    copy.wait_send()

            is_relay = functools.reduce(jnp.logical_or, [place.lat == lat for lat in self.lats])

            @pl.when(is_relay)
            def _():
                self.passing.wait_send()

    back, side_back = r.back, r.side_back
    last_rows = pl.ds(half_rows, half_rows)
    rows_out = Crossing(
        [tok.at[last_rows], cot.at[last_rows]], [r.row_tok, r.row_cot], relays.out_rows, relays.low_end,
        not_last, not_first, (place.lat + 1, place.lon), (relays.first_high, place.lon),
        r.out_send, r.out_recv, r.relay, r.relay_sem,
    )
    corner_out = Crossing(
        [packed.at[1]], [side.at[1]], relays.out_corner, relays.low_end,
        not_last, not_first, (place.lat + 1, place.east()), (relays.first_high, place.east()),
        r.corner_send, r.corner_recv, r.corner, r.corner_sem,
    )
    rows_back = Crossing(
        [back.at[last_rows]], [r.row_back], relays.back_rows, relays.high_end,
        not_first, not_last, (place.lat - 1, place.lon), (relays.last_low, place.lon),
        r.back_send, r.back_recv, r.relay_back, r.relay_back_sem,
    )
    corner_back = Crossing(
        [back.at[pl.ds(2 * half_rows + 32, 32)]], [side_back.at[1]], relays.back_corner, relays.high_end,
        not_first, not_last, (place.lat - 1, place.west()), (relays.last_low, place.west()),
        r.corner_back_send, r.corner_back_recv, r.corner_back, r.corner_back_sem,
    )
    side_return = remote(
        back.at[pl.ds(2 * half_rows, 32)], side_back.at[0], halo_send.at[1], halo_recv.at[1],
        (place.lat, place.west()),
    )

    def send_relayed():
        rows_out.start_relayed()
        corner_out.start_relayed()

    def send_halos():
        rows_out.start()

    def send_sides():
        corner_out.start()
        side_copy.start()

    def pass_on():
        rows_out.pass_on()
        corner_out.pass_on()

    blocks = r.blocks

    def tile_at(n):
        which, group = divmod(n, groups)
        return group, pl.ds(which * width, width)

    def join_ring():
        ring_all.wait_recv()

        for pair in range(lons // 2):
            tiles = [[], [], []]
            for z_hi in range(Z_HI):
                even = units[z_hi * lons + 2 * pair].astype(F32)
                odd = units[z_hi * lons + 2 * pair + 1].astype(F32)
                turned_top = pltpu.roll(odd[0:8], 64, 1)
                turned_low = pltpu.roll(odd[8:16], 64, 1)
                tiles[0].append(even[0:8])
                tiles[1].append(jnp.where(lane_of < 64, even[8:16], turned_top))
                tiles[2].append(jnp.where(lane_of < 64, turned_top, turned_low))
            for j in range(3):
                group, lanes = tile_at(pair * 3 + j)
                blocks[group, place.core, place.p, :, lanes] = jnp.concatenate(tiles[j], axis=0).astype(BF16)

    def plane_copy(group, k):
        own = blocks.at[group, place.core, place.p]
        return remote(
            own, own, r.plane_send.at[group], r.plane_recv.at[group], place.plane[k][1]
        )

    def plane_all(group):
        others = blocks.at[group, place.core, pl.ds(0, planes - 1)]
        return remote(others, others, r.plane_send.at[group], r.plane_recv.at[group], place.partner())

    def core_copy(group):
        block = blocks.at[group, place.core]
        return remote(block, block, r.core_send.at[group], r.core_recv.at[group], place.partner())

    def core_arrival(group):
        block = blocks.at[group, 1 - place.core]
        return remote(block, block, r.core_send.at[group], r.core_recv.at[group], place.partner())

    def send_blocks(group):
        for k in range(1, planes):
            plane_copy(group, k).start()

    own_count = r.counts[place.lat]
    previous = jnp.where(not_first, r.counts[jnp.maximum(place.lat - 1, 0)], 0)
    row_of = r.row_of[...]
    limit = jnp.where(row_of < SHIFT_ROWS, previous - SHIFT_ROWS, own_count + SHIFT_ROWS)
    valid = jnp.where(row_of < jnp.minimum(limit, WIN_ROWS), 1.0, 0.0)
    take_own, take_row, take_side = r.take_own, r.take_row, r.take_side

    def framed_of(own, row, first):
        return (
            jnp.dot(take_own[...], own[...], preferred_element_type=F32)
            + jnp.dot(take_row[...], row[...], preferred_element_type=F32)
            + jnp.dot(take_side[first], side[0], preferred_element_type=F32)
            + jnp.dot(take_side[first + 1], side[1], preferred_element_type=F32)
        )

    hidden, normed, spread, out_grad = r.hidden, r.normed, r.spread, r.out_grad
    def frame():
        rows_out.wait_recv()
        corner_out.wait_recv()
        side_copy.wait_recv()

        framed = framed_of(tok, r.row_tok, 0)
        center = framed - jnp.mean(framed, axis=-1, keepdims=True)
        inverse = lax.rsqrt(jnp.mean(center * center, axis=-1, keepdims=True) + EPSILON)
        normal = center * inverse
        normed[...] = normal
        spread[...] = jnp.broadcast_to(inverse, spread.shape)
        hidden[...] = normal.astype(BF16)
        r.turned_hidden[...] = normal.astype(BF16).T
        framed = framed_of(cot, r.row_cot, 2)
        for j in range(features // 128):
            lanes = slice(j * 128, j * 128 + 128)
            out_grad[:, lanes] = jnp.where(valid > 0.0, framed[:, lanes], 0.0).astype(BF16)

    weight, qkv, qkv_grad = r.weight, r.qkv, r.qkv_grad

    def forward_arrivals(group):
        plane_all(group).wait_recv()
        core_copy(group).start()

    def collect(group):
        core_arrival(group).wait_recv()
        for p in range(planes):
            first = blocks[group, 0, p].astype(F32)
            second = blocks[group, 1, p].astype(F32)
            for z_hi in range(Z_HI):
                take = slice(z_hi * 8, z_hi * 8 + 8)
                rows = pl.ds((z_hi * planes + p) * 16, 16)
                weight[group, rows, :] = jnp.concatenate([first[take], second[take]], axis=0).astype(BF16)

    factor = HEAD_DIM ** (-0.5)
    whole, rest = divmod(GROUP * PAD, 128)
    allowed = jnp.concatenate([valid[0:PAD]] * whole + [valid[0:PAD, 0:rest]], axis=1) > 0.0
    mask = r.head_mask[...]
    windows = hidden.shape[0] // PAD

    def project(group):
        qkv[group] = jnp.dot(hidden[...], weight[group], preferred_element_type=F32).astype(BF16)

    def attend(group):
        for window in range(windows):
            at = slice(window * PAD, window * PAD + PAD)
            lanes = [slice(j * width, (j + 1) * width) for j in range(3)]
            query, keyed, valued = (qkv[group, at, lane] for lane in lanes)
            grad = out_grad[at, group * width : (group + 1) * width]
            query = jnp.concatenate([query] * GROUP, axis=0) * mask
            grad = jnp.concatenate([grad] * GROUP, axis=0) * mask
            scores = jnp.where(allowed, contract(keyed, query, ((1,), (1,))), -1000000000.0 / factor)
            exponent = jnp.exp2((scores - jnp.max(scores, axis=0, keepdims=True)) * (factor * LOG2_E))
            probs = exponent * (1.0 / jnp.sum(exponent, axis=0, keepdims=True))
            weight_grad = contract(valued, grad, ((1,), (1,)))
            mixed = jnp.sum(probs * weight_grad, axis=0, keepdims=True)
            score_grad = (probs * (weight_grad - mixed) * factor).astype(BF16)
            value_grad = jnp.dot(probs.astype(BF16), grad, preferred_element_type=F32)
            key_grad = jnp.dot(score_grad, query, preferred_element_type=F32)
            turned = contract(score_grad, keyed, ((0,), (0,)))
            query_grad = turned[0:PAD] * mask[0:PAD].astype(F32)
            for h in range(1, GROUP):
                rows_h = slice(h * PAD, h * PAD + PAD)
                query_grad = query_grad + turned[rows_h] * mask[rows_h].astype(F32)
            for lane, value in zip(lanes, (query_grad, key_grad, value_grad)):
                qkv_grad[group, at, lane] = value.astype(BF16)

    part = r.part

    def weigh(group):
        for j in range(3):
            lanes = slice(j * width, (j + 1) * width)
            piece = jnp.dot(r.turned_hidden[...], qkv_grad[group, :, lanes], preferred_element_type=F32)
            for core in range(CORES):
                for p in range(planes):
                    first = (p * CORES + core) * 8
                    both = [piece[z * planes * CORES * 8 + first :][0:8] for z in range(Z_HI)]
                    part[group, core, p, :, lanes] = jnp.concatenate(both, axis=0).astype(BF16)

    spans = ((0, 1), (1, 2), (2, 3), (3, 4))
    from_core, sums, from_plane, total = r.from_core, r.sums, r.from_plane, r.total

    def core_part(group):
        return remote(
            part.at[group, 1 - place.core], from_core.at[group],
            r.core_part_send.at[group], r.core_part_recv.at[group], place.partner(),
        )

    def plane_part(first, last, k):
        p, device = place.plane[k]
        span = pl.ds(first, last - first)
        return remote(
            sums.at[p, span], from_plane.at[place.p, span],
            r.plane_part_send.at[first], r.plane_part_recv.at[first], device,
        )

    def plane_part_all(first, last):
        others, span = pl.ds(0, planes - 1), pl.ds(first, last - first)
        return remote(
            sums.at[others, span], from_plane.at[others, span],
            r.plane_part_send.at[first], r.plane_part_recv.at[first], place.partner(),
        )

    def send_core(group):
        core_part(group).start()

    def send_plane(first, last):
        for group in range(first, last):
            core_part(group).wait_recv()
            sums[:, group] = (part[group, place.core].astype(F32) + from_core[group].astype(F32)).astype(BF16)
        for k in range(1, planes):
            plane_part(first, last, k).start()
        for group in range(first, last):
            from_plane[place.p, group] = sums[place.p, group]

    def add_plane(first, last):
        plane_part_all(first, last).wait_recv()
        for group in range(first, last):
            total[group] = jnp.sum(from_plane[:, group].astype(F32), axis=0)

    def accumulate(group):
        term = contract(qkv_grad[group], weight[group], ((1,), (1,)))
        if group == 0:
            r.hidden_grad[...] = term
        else:
            r.hidden_grad[...] += term

    def differentiate():
        hidden_grad = r.hidden_grad[...]
        normal = normed[...]
        mean_grad = jnp.mean(hidden_grad, axis=-1, keepdims=True)
        mean_mixed = jnp.mean(hidden_grad * normal, axis=-1, keepdims=True)
        frame_grad = spread[...] * (hidden_grad - mean_grad - normal * mean_mixed)
        back[...] = jnp.dot(r.give[...], frame_grad.astype(BF16), preferred_element_type=F32).astype(BF16)

    def return_relayed():
        rows_back.start_relayed()
        corner_back.start_relayed()

    def return_halos():
        rows_back.start()
        corner_back.start()
        side_return.start()

    def pass_back():
        rows_back.pass_on()
        corner_back.pass_on()

    part_units, from_ring = r.part_units, r.from_ring

    def ring_part(k):
        z, device = place.ring[k]
        return remote(
            part_units.at[z], from_ring.at[place.z], r.ring_part_send.at[0], r.ring_part_recv.at[0], device
        )

    ring_part_all = remote(
        part_units.at[others], from_ring.at[others], r.ring_part_send.at[0], r.ring_part_recv.at[0],
        place.partner(),
    )

    def send_ring_parts():
        for pair in range(lons // 2):
            for z_hi in range(Z_HI):
                tiles = []
                for j in range(3):
                    group, lanes = tile_at(pair * 3 + j)
                    tiles.append(total[group, pl.ds(z_hi * 8, 8), lanes])
                turned = [pltpu.roll(tile, 64, 1) for tile in tiles]
                part_units[z_hi * lons + 2 * pair] = jnp.concatenate([tiles[0], tiles[1]], axis=0).astype(BF16)
                part_units[z_hi * lons + 2 * pair + 1] = jnp.concatenate(
                    [jnp.where(lane_of < 64, turned[1], turned[2]), turned[2]], axis=0
                ).astype(BF16)

        for k in far_first(rings):
            ring_part(k).start()

        from_ring[place.z] = part_units[place.z]

    token_sum_copy = pltpu.make_async_copy(r.token_sum, token_sum, r.store_sem.at[0])
    weight_copy = pltpu.make_async_copy(r.weight_gradient, weight_gradient, r.store_sem.at[1])

    def finish_tokens():
        rows_back.wait_recv()
        corner_back.wait_recv()
        side_return.wait_recv()

        for part_of in range(2):
            rows = pl.ds(part_of * half_rows, half_rows)
            inner = back[0:half_rows] if part_of == 0 else r.row_back[...]
            outer = jnp.dot(r.place_sel[...], side_back[part_of], preferred_element_type=F32)
            r.token_sum[rows] = (cot[rows].astype(F32) + (inner.astype(F32) + outer)).astype(BF16)
        token_sum_copy.start()

    def finish_weight():
        ring_part_all.wait_recv()

        result = from_ring[0].astype(F32)
        for z in range(1, rings):
            result = result + from_ring[z].astype(F32)
        r.weight_gradient[:, 0:128] = result[0:8]
        r.weight_gradient[:, 128:192] = result[8:16, 0:64]
        weight_copy.start()

    def drain():
        token_sum_copy.wait()
        weight_copy.wait()
        rows_out.wait_send()
        rows_back.wait_send()
        corner_out.wait_send()
        corner_back.wait_send()
        side_copy.wait_send()
        side_return.wait_send()
        ring_all.wait_send()
        ring_part_all.wait_send()
        for group in range(groups):
            plane_all(group).wait_send()
            core_copy(group).wait_send()
            core_part(group).wait_send()
        for first, last in spans:
            plane_part_all(first, last).wait_send()

    send_relayed()
    send_ring()
    send_halos()
    pass_on()
    join_ring()
    send_blocks(0)
    send_sides()
    for group in range(1, groups):
        send_blocks(group)
    @pl.when(jnp.logical_not(relays.high_end))
    def _():
        frame()

    forward_arrivals(0)
    forward_arrivals(1)

    @pl.when(relays.high_end)
    def _():
        frame()

    for group in range(groups):
        collect(group)
        project(group)
        attend(group)
        if group > 0:
            send_plane(*spans[group - 1])
        if group < groups - 2:
            forward_arrivals(group + 2)
        weigh(group)
        send_core(group)
    for group in range(groups):
        accumulate(group)
    differentiate()
    return_relayed()
    send_plane(*spans[3])
    return_halos()
    pass_back()
    for span in spans:
        add_plane(*span)
    send_ring_parts()
    finish_tokens()
    finish_weight()
    drain()


def finish_kernel(token_sum, weight, token_grad, weight_gradient, first, held, load_sem, store_sem):
    parts = first.shape[0]
    rows = first.shape[1]
    weight_load = pltpu.make_async_copy(weight, held, store_sem.at[parts])
    weight_store = pltpu.make_async_copy(held, weight_gradient, store_sem.at[parts + 1])
    weight_load.start()
    loads, stores = [], []
    for i in range(parts):
        at = pl.ds(i * rows, rows)
        loads.append(
            (
                pltpu.make_async_copy(token_sum.at[at], first.at[i], load_sem.at[i, 0]),
            )
        )
        stores.append(pltpu.make_async_copy(first.at[i], token_grad.at[at], store_sem.at[i]))
    for pair in loads:
        for load in pair:
            load.start()
    weight_load.wait()
    weight_store.start()
    for i in range(parts):
        for load in loads[i]:
            load.wait()
        stores[i].start()
    for store in stores:
        store.wait()
    weight_store.wait()


def finish(token_sum, weight):
    parts = 3
    block = VMEM((parts, token_sum.shape[0] // parts, token_sum.shape[1]), BF16)
    return pl.pallas_call(
        finish_kernel,
        out_shape=(
            jax.ShapeDtypeStruct(token_sum.shape, BF16),
            jax.ShapeDtypeStruct(weight.shape, F32),
        ),
        in_specs=[pl.BlockSpec(memory_space=pl.ANY)] * 2,
        out_specs=[pl.BlockSpec(memory_space=pl.ANY)] * 2,
        scratch_shapes=[
            block, VMEM(weight.shape, F32),
            pltpu.SemaphoreType.DMA((parts, 1)), pltpu.SemaphoreType.DMA((parts + 2,)),
        ],
        compiler_params=pltpu.CompilerParams(vmem_limit_bytes=56 * 2**20),
        name="finish",
    )(token_sum, weight)


def frame_tables(cols):
    windows = cols // WIN_COLS
    total = windows * PAD
    half = SHIFT_ROWS * cols
    own = np.zeros((total, 2 * half), np.float32)
    row = np.zeros((total, half), np.float32)
    side = np.zeros((4, total, 48), np.float32)
    give = np.zeros((2 * half + 64, total), np.float32)
    row_of = np.full((total, 128), WIN_ROWS, np.int32)
    for window in range(windows):
        for r in range(WIN_ROWS):
            for c in range(WIN_COLS):
                t = window * PAD + r * WIN_COLS + c
                row_of[t] = r
                rr, g = r - SHIFT_ROWS, window * WIN_COLS + c - SHIFT_COLS
                upper = rr < 0
                if g >= 0:
                    if upper:
                        row[t, r * cols + g] = 1
                        give[half + r * cols + g, t] = 1
                    else:
                        own[t, rr * cols + g] = 1
                        give[rr * cols + g, t] = 1
                else:
                    at = (r % SHIFT_ROWS) * SHIFT_COLS + g + SHIFT_COLS
                    side[int(upper), t, at] = 1
                    side[2 + int(upper), t, 18 + at] = 1
                    give[2 * half + 32 * int(upper) + at, t] = 1
    return own, row, side, give, row_of


def on_device(lats, lons, tokens, cotangent, qkv_weight, band_rows):
    features = tokens.shape[-1]
    tok = tokens.reshape(-1, features)
    cot = cotangent.reshape(-1, features)
    count = tok.shape[0]
    half = count // 2
    cols = half // SHIFT_ROWS
    planes, rings = Y * X, Z_HI * lons
    columns = qkv_weight.shape[1] * lons
    width = GROUP * HEAD_DIM
    groups = features // width
    take_own, take_row, take_side, give, row_of = frame_tables(cols)
    total = take_own.shape[0]
    sel = np.zeros((2, 48, half), np.float32)
    place_sel = np.zeros((half, 32), np.float32)
    for row in range(SHIFT_ROWS):
        for col in range(SHIFT_COLS):
            at, edge = row * SHIFT_COLS + col, row * cols + cols - SHIFT_COLS + col
            sel[0, at, edge] = 1
            sel[1, 18 + at, edge] = 1
            place_sel[edge, at] = 1
    head_mask = np.zeros((GROUP, PAD, GROUP, HEAD_DIM), np.float32)
    for h in range(GROUP):
        head_mask[h, :, h] = 1
    low = lambda table: jnp.asarray(table, BF16)
    loaded = dict(
        w_in=qkv_weight, counts=band_rows, tok=tok, cot=cot, sel=low(sel), row_of=jnp.asarray(row_of), take_own=low(take_own), take_row=low(take_row),
        take_side=low(take_side), head_mask=low(head_mask.reshape(GROUP * PAD, width)), give=low(give),
        place_sel=low(place_sel),
    )
    dma = pltpu.SemaphoreType.DMA
    scratch = {name: VMEM(array.shape, array.dtype) for name, array in loaded.items()}
    scratch.update(counts=pltpu.SMEM(band_rows.shape, band_rows.dtype))
    scratch.update(
        wide=VMEM((8, 256), F32),
        unit=VMEM((16, 128), BF16),
        units=VMEM((rings, 16, 128), BF16),
        blocks=VMEM((groups, CORES, planes, 16, columns // groups), BF16),
        packed=VMEM((2, 48, features), BF16),
        side=VMEM((2, 48, features), BF16),
        row_tok=VMEM((half, features), BF16),
        row_cot=VMEM((half, features), BF16),
        relay=VMEM((2 * TILE, features), BF16),
        corner=VMEM((TILE, features), BF16),
        relay_back=VMEM((TILE, features), BF16),
        corner_back=VMEM((TILE, features), BF16),
        weight=VMEM((groups, features, columns // groups), BF16),
        hidden=VMEM((total, features), BF16),
        turned_hidden=VMEM((features, total), BF16),
        normed=VMEM((total, features), F32),
        spread=VMEM((total, features), F32),
        hidden_grad=VMEM((total, features), F32),
        out_grad=VMEM((total, features), BF16),
        qkv=VMEM((groups, total, columns // groups), BF16),
        qkv_grad=VMEM((groups, total, columns // groups), BF16),
        part=VMEM((groups, CORES, planes, 16, columns // groups), BF16),
        from_core=VMEM((groups, planes, 16, columns // groups), BF16),
        sums=VMEM((planes, groups, 16, columns // groups), BF16),
        from_plane=VMEM((planes, groups, 16, columns // groups), BF16),
        total=VMEM((groups, 16, columns // groups), F32),
        back=VMEM(give.shape[:1] + (features,), BF16),
        row_back=VMEM((half, features), BF16),
        side_back=VMEM((2, 32, features), BF16),
        part_units=VMEM((rings, 16, 128), BF16),
        from_ring=VMEM((rings, 16, 128), BF16),
        token_sum=VMEM(tok.shape, BF16),
        weight_gradient=VMEM(qkv_weight.shape, F32),
        load_sem=dma((len(loaded),)),
        store_sem=dma((2,)),
        relay_sem=dma((2,)),
        corner_sem=dma((2,)),
        relay_back_sem=dma((2,)),
        corner_back_sem=dma((2,)),
    )
    both = dict(
        ring=(1,), plane=(groups,), core=(groups,), halo=(2,), out=(2,),
        corner=(1,), back=(1,), corner_back=(1,), core_part=(groups,), plane_part=(groups,), ring_part=(1,),
    )
    for name, shape in both.items():
        scratch[name + "_send"] = dma(shape)
        scratch[name + "_recv"] = dma(shape)
    token_sum, weight_gradient = pl.pallas_call(
        functools.partial(kernel, lats, lons, len(loaded), list(scratch)),
        out_shape=(
            jax.ShapeDtypeStruct(tok.shape, BF16),
            jax.ShapeDtypeStruct(qkv_weight.shape, F32),
        ),
        in_specs=[pl.BlockSpec(memory_space=pl.ANY)] * len(loaded),
        out_specs=[pl.BlockSpec(memory_space=pl.ANY)] * 2,
        scratch_shapes=list(scratch.values()),
        compiler_params=pltpu.CompilerParams(
            collective_id=0, has_side_effects=True, vmem_limit_bytes=56 * 2**20
        ),
        name="sub_block",
    )(*loaded.values())
    token_grad, weight_gradient = finish(token_sum, weight_gradient)
    return token_grad.reshape(tokens.shape), weight_gradient


def solution(mesh):
    return jax.shard_map(
        functools.partial(on_device, mesh.shape["lat"], mesh.shape["lon"]),
        mesh=mesh,
        in_specs=(P("lat", "lon", None), P("lat", "lon", None), P("lat", "lon"), P()),
        out_specs=(P("lat", "lon", None), P("lat", "lon")),
        check_vma=False,
    )
```
